128 devices in a mesh: gx: 8 (over y, core), gy: 16 (over x, z).
Axes of the slice: x: 4, y: 4, z: 4, core: 2. Of those that a mesh axis runs over, the one named last changes fastest.
Arguments:
- old_states: bfloat16 [16384, 12, 128], P(('gx', 'gy')), may hold values from -6 to 6
- weight_tiles: bfloat16 [49152, 128, 128], P(('gx', 'gy')), may hold values from -0.5 to 0.5
- source_block: int32 [98304], P(('gx', 'gy')), may hold values from 0 to 127
- tile_index: int32 [98304], P(('gx', 'gy')), may hold values from 0 to 383
- dest_device: int32 [98304], P(('gx', 'gy')), may hold values from 0 to 127, as said below
- dest_block: int32 [98304], P(('gx', 'gy')), may hold values from 0 to 255
- send_count: int32 [128], P(('gx', 'gy')), may hold values from 576 to 768, as said below
- velocity: float32 [2, 2048, 2048], P(None, 'gx', 'gy'), may hold values from -4 to 4
Outputs:
- new_states: float32 [2048, 12, 2048], P('gx', None, 'gy')
The draws below stay inside these ranges and needn't reach their ends.
Inputs may be any that keep to these rules, and one draw needn't show every extreme that they name: `dest_device`: the live slots of a device name only the device itself and the devices of the tiles adjacent to its tile along gx and gy, diagonals included; among them no destination appears more than 192 times, and the device itself appears exactly 192 times. The live slots of a device are its first send_count slots; some device has all 768 live.
All inputs are finite; a program needn't handle non-finite values.
Results may differ from the reference program's by a relative error of at most 0.0033.
The reference program's roundings to bfloat16 on the way count: a program that leaves them out, or rounds other values in their place, can miss the bound.
Values may be sent and summed in bfloat16 or wider, within the bound.
A program may use at most 128 MiB of HBM per device.

```python
import jax
import jax.numpy as jnp
from jax import lax

BLK = 128
STATES = 12
CX = 256
OB_DEV = 128
SEND_DEV = 768
TILES_DEV = 384
CAP = 192
NX = 2048
NY = 2048
OLD_BLOCKS = 16384
PAIRS = 98304
TILES = 49152
N_GX = 8
N_GY = 16
DEVICES = 128


def draw_dest_device(key, part):
    lowest = SEND_DEV - SEND_DEV // 4
    steps_x = jnp.array([-1, -1, -1, 0, 0, 1, 1, 1], jnp.int32)
    steps_y = jnp.array([-1, 0, 1, -1, 1, -1, 0, 1], jnp.int32)

    def one_device(device_key, device):
        first_key, second_key = jax.random.split(device_key)
        row_index = device // N_GY
        col_index = device % N_GY
        near_x = row_index + steps_x
        near_y = col_index + steps_y
        valid = (near_x >= 0) & (near_x < N_GX) & (near_y >= 0) & (near_y < N_GY)
        near = near_x * N_GY + near_y
        candidate = jnp.arange(8 * CAP, dtype=jnp.int32) // CAP
        scores = jax.random.permutation(first_key, 8 * CAP).astype(jnp.int32) + jnp.where(valid[candidate], 0, 8 * CAP).astype(jnp.int32)
        picked = candidate[jnp.argsort(scores)[:SEND_DEV - CAP]]
        others = near[picked]
        destination = jnp.concatenate([jnp.full((CAP,), device, jnp.int32), others.astype(jnp.int32)])
        shuffle = jax.random.permutation(second_key, lowest)
        leading = destination[:lowest][shuffle]
        return jnp.concatenate([leading, destination[lowest:]]).astype(jnp.int32)
    device_keys = jax.random.split(jax.random.fold_in(key, 11), DEVICES)
    return jax.vmap(one_device)(device_keys, jnp.arange(DEVICES, dtype=jnp.int32)).reshape(-1)


def draw_send_count(key, part):
    lowest = SEND_DEV - SEND_DEV // 4
    first_key, second_key = jax.random.split(jax.random.fold_in(key, 23))
    counts = jax.random.randint(first_key, (DEVICES,), lowest, SEND_DEV + 1)
    ordering = jax.random.permutation(second_key, DEVICES)
    counts = counts.at[ordering[0]].set(SEND_DEV).at[ordering[1]].set(lowest)
    return counts.astype(jnp.int32)


def set_ends(drawn, rng, low, largest):
    extent = drawn.shape
    spot = [jax.random.randint(jax.random.fold_in(rng, axis), (), 0, extent[axis]) for axis in range(len(extent))]
    drawn = drawn.at[tuple(spot)].set(low)
    longest = extent.index(max(extent))
    spot[longest] = (spot[longest] + 1) % extent[longest]
    return drawn.at[tuple(spot)].set(largest)


def block_scale(rng, dims, cuts, smallest, high):
    def one(position, shards_of):
        heights = jax.random.uniform(jax.random.fold_in(jax.random.fold_in(rng, 6), position), (shards_of,), jnp.float32, smallest / len(cuts), high / len(cuts))
        return jnp.repeat(jnp.exp(heights), dims[position] // shards_of).reshape((-1,) + (1,) * (len(dims) - position - 1))

    gain = one(*cuts[0])
    for cut in cuts[1:]:
        gain = gain * one(*cut)
    return gain


def noise(stream_key, shape, scale, reach, cuts=(), kind=jnp.bfloat16):
    entries = scale * jax.random.normal(stream_key, shape, jnp.float32)
    if cuts:
        entries = entries * block_scale(stream_key, shape, cuts, -0.22, 0.18)
    return jnp.clip(entries, -reach, reach).astype(kind)


def setup_inputs(seed: int = 0) -> dict:
    streams_of = jax.random.split(jax.random.key(seed), 9)
    old_states = noise(streams_of[0], (OLD_BLOCKS, STATES, BLK), 1.0, 6.0, ((0, 128),))
    weight_tiles = noise(streams_of[1], (TILES, BLK, BLK), BLK ** -0.5, 0.5, ((0, 128),))
    source_block = set_ends(jax.random.randint(streams_of[2], (PAIRS,), 0, OB_DEV), jax.random.fold_in(streams_of[2], 1), 0, OB_DEV - 1).astype(jnp.int32)
    tile_index = set_ends(jax.random.randint(streams_of[3], (PAIRS,), 0, TILES_DEV), jax.random.fold_in(streams_of[3], 1), 0, TILES_DEV - 1).astype(jnp.int32)
    dest_device = draw_dest_device(jax.random.fold_in(streams_of[8], 71), 0)
    dest_block = set_ends(jax.random.randint(streams_of[5], (PAIRS,), 0, CX), jax.random.fold_in(streams_of[5], 1), 0, CX - 1).astype(jnp.int32)
    send_count = draw_send_count(jax.random.fold_in(streams_of[8], 71), 0)
    velocity = noise(streams_of[7], (2, NX, NY), 1.0, 4.0, ((1, 8), (2, 16)), jnp.float32)
    return dict(old_states=old_states, weight_tiles=weight_tiles, source_block=source_block, tile_index=tile_index, dest_device=dest_device, dest_block=dest_block, send_count=send_count, velocity=velocity)


time_step = 0.2
shape_factor = 0.95
interaction = 0.01
shear_modulus = 1.0
fiber_number = 2.0

def product(left, right):
    return [[sum((left[first][inner] * right[inner][second] for inner in range(3))) for second in range(3)] for first in range(3)]

def advance(state_pad, flow_pad):
    centre = state_pad[1:-1, :, 1:-1]
    flow_x = flow_pad[0, 1:-1, 1:-1]
    flow_y = flow_pad[1, 1:-1, 1:-1]
    grad_xx = 0.5 * (flow_pad[0, 2:, 1:-1] - flow_pad[0, :-2, 1:-1])
    grad_xy = 0.5 * (flow_pad[0, 1:-1, 2:] - flow_pad[0, 1:-1, :-2])
    grad_yx = 0.5 * (flow_pad[1, 2:, 1:-1] - flow_pad[1, :-2, 1:-1])
    grad_yy = 0.5 * (flow_pad[1, 1:-1, 2:] - flow_pad[1, 1:-1, :-2])
    grad_zz = -(grad_xx + grad_yy)
    strain_xy = 0.5 * (grad_xy + grad_yx)
    spin_xy = 0.5 * (grad_xy - grad_yx)
    upwind = jnp.maximum(flow_x, 0.0)[:, None, :] * (centre - state_pad[:-2, :, 1:-1]) + jnp.minimum(flow_x, 0.0)[:, None, :] * (state_pad[2:, :, 1:-1] - centre) + jnp.maximum(flow_y, 0.0)[:, None, :] * (centre - state_pad[1:-1, :, :-2]) + jnp.minimum(flow_y, 0.0)[:, None, :] * (state_pad[1:-1, :, 2:] - centre)
    parts = [centre[:, index, :] for index in range(6)]
    orient = [[parts[0], parts[3], parts[4]], [parts[3], parts[1], parts[5]], [parts[4], parts[5], parts[2]]]
    zero = jnp.zeros_like(grad_xx)
    rate = [[grad_xx, strain_xy, zero], [strain_xy, grad_yy, zero], [zero, zero, grad_zz]]
    spin = [[zero, spin_xy, zero], [-spin_xy, zero, zero], [zero, zero, zero]]
    contraction = sum((orient[first][second] * rate[first][second] for first in range(3) for second in range(3)))
    shear = jnp.sqrt(2.0 * sum((rate[first][second] * rate[first][second] for first in range(3) for second in range(3))) + 1.0)
    spin_orient = product(spin, orient)
    orient_spin = product(orient, spin)
    rate_orient = product(rate, orient)
    orient_rate = product(orient, rate)
    sources = []
    for first, second in ((0, 0), (1, 1), (2, 2), (0, 1), (0, 2), (1, 2)):
        delta = 1.0 if first == second else 0.0
        sources.append(spin_orient[first][second] - orient_spin[first][second] + shape_factor * (rate_orient[first][second] + orient_rate[first][second] - 2.0 * contraction * orient[first][second]) + 2.0 * interaction * shear * (delta - 3.0 * orient[first][second]))
    sources = sources + [grad_xx, grad_yy, strain_xy]
    for first, second in ((0, 0), (1, 1), (0, 1)):
        sources.append(2.0 * shear_modulus * (rate[first][second] + fiber_number * contraction * orient[first][second]))
    source = jnp.stack(sources, axis=1)
    return centre + time_step * (source - upwind)

def reference(old_states, weight_tiles, source_block, tile_index, dest_device, dest_block, send_count, velocity):
    blocks_all = old_states.reshape(DEVICES, OB_DEV, STATES, BLK)
    tiles_all = weight_tiles.reshape(DEVICES, TILES_DEV, BLK, BLK)
    sources_all = source_block.reshape(DEVICES, SEND_DEV)
    picks_all = tile_index.reshape(DEVICES, SEND_DEV)
    targets_all = dest_device.reshape(DEVICES, SEND_DEV)
    rows_all = dest_block.reshape(DEVICES, SEND_DEV)

    def one_device(carry, items):
        blocks, tiles, source_ids, pick_ids, target_ids, row_ids, count = items
        block_pick = blocks[source_ids].astype(jnp.float32)
        tile_pick = tiles[pick_ids].astype(jnp.float32)
        pieces = jnp.einsum('snk,sck->scn', tile_pick, block_pick, precision=lax.Precision.HIGHEST)
        is_live = jnp.arange(SEND_DEV) < count
        pieces = jnp.where(is_live[:, None, None], pieces, 0.0)
        pieces = lax.optimization_barrier(pieces.astype(jnp.bfloat16)).astype(jnp.float32)
        tile_x = target_ids // N_GY
        tile_y = target_ids % N_GY
        carry = carry.at[tile_x, row_ids, tile_y].add(pieces)
        return (carry, None)
    start = jnp.zeros((N_GX, CX, N_GY, STATES, BLK), jnp.float32)
    total, _ = lax.scan(one_device, start, (blocks_all, tiles_all, sources_all, picks_all, targets_all, rows_all, send_count))
    remapped = total.transpose(0, 1, 3, 2, 4).reshape(NX, STATES, NY)
    state_pad = jnp.pad(remapped, ((1, 1), (0, 0), (1, 1)))
    flow_pad = jnp.pad(velocity, ((0, 0), (1, 1), (1, 1)))
    return advance(state_pad, flow_pad)
```

```python
import functools

import jax
import jax.numpy as jnp
from jax import lax
from jax.experimental import pallas as pl
from jax.experimental.pallas import tpu as pltpu
from jax.sharding import PartitionSpec as P

time_step = 0.2
shape_factor = 0.95
interaction = 0.01
shear_modulus = 1.0
fiber_number = 2.0

MESH = pl.DeviceIdType.MESH
CHUNK = 48
HALO_ROWS = 14
MIB = 1 << 20


def step_of(k):
    m = k // 2
    dx = jnp.where(k < 6, jnp.where(m == 2, 0, 2 * m - 1), 2 * (k - 6) - 1)
    dy = jnp.where(k < 6, 1 - 2 * (k % 2), 0)
    return dx, dy


def exists(x, y, nx, ny):
    return (x >= 0) & (x < nx) & (y >= 0) & (y < ny)


def neighbours_of(x, y, nx, ny):
    spread_x = 3 - (x == 0).astype(jnp.int32) - (x == nx - 1).astype(jnp.int32)
    spread_y = 3 - (y == 0).astype(jnp.int32) - (y == ny - 1).astype(jnp.int32)
    return spread_x * spread_y - 1


def chunks_of(x, y, nx, ny, caps):
    n = neighbours_of(x, y, nx, ny)
    inner, edge, corner = caps
    return jnp.where(n >= 8, inner, jnp.where(n >= 5, edge, corner))


def exchange_kernel(
    nx,
    ny,
    caps,
    picks,
    labels,
    old,
    vel,
    weights,
    remapped,
    halo_y,
    halo_x,
    tiles,
    outgoing,
    incoming,
    incoming_labels,
    turn,
    edge_y,
    edge_x,
    load_sem,
    label_sems,
    send_sems,
    recv_sems,
    edge_sems,
):
    gx, gy = lax.axis_index("gx"), lax.axis_index("gy")
    parts = load_sem.shape[0]
    depth = tiles.shape[0] // parts
    cap = outgoing.shape[1]
    rows = remapped.shape[1]
    state_count = remapped.shape[0]

    for part in range(parts):
        span = pl.ds(part * depth, depth)
        pltpu.make_async_copy(weights.at[span], tiles.at[span], load_sem.at[part]).start()

    barrier = pltpu.get_barrier_semaphore()
    for k in range(8):
        dx, dy = step_of(k)

        @pl.when(exists(gx + dx, gy + dy, nx, ny))
        def _():
            pl.semaphore_signal(
                barrier, inc=1, device_id=(gx + dx, gy + dy), device_id_type=MESH
            )

    pl.semaphore_wait(barrier, neighbours_of(gx, gy, nx, ny))

    def label_copy(k):
        dx, dy = step_of(k)
        return pltpu.make_async_remote_copy(
            src_ref=labels.at[k],
            dst_ref=incoming_labels.at[k],
            send_sem=label_sems.at[0, k],
            recv_sem=label_sems.at[1, k],
            device_id=(gx + dx, gy + dy),
            device_id_type=MESH,
        )

    def chunk_copy(k, j):
        dx, dy = step_of(k)
        span = pl.ds(j * CHUNK, CHUNK)
        return pltpu.make_async_remote_copy(
            src_ref=outgoing.at[k, span],
            dst_ref=incoming.at[k, span],
            send_sem=send_sems.at[k, j],
            recv_sem=recv_sems.at[k, j],
            device_id=(gx + dx, gy + dy),
            device_id_type=MESH,
        )

    def goes_out(k):
        dx, dy = step_of(k)
        return exists(gx + dx, gy + dy, nx, ny)

    def comes_in(k):
        dx, dy = step_of(k)
        return exists(gx - dx, gy - dy, nx, ny)

    def each_channel(body, predicate):
        def step(k, carry):
            @pl.when(predicate(k))
            def _():
                body(k)

            return carry

        lax.fori_loop(0, 8, step, 0)

    each_channel(lambda k: label_copy(k).start(), goes_out)

    for part in range(parts):
        span = pl.ds(part * depth, depth)
        pltpu.make_async_copy(weights.at[span], tiles.at[span], load_sem.at[part]).wait()

    def compute_chunk(k, j):
        for i in range(CHUNK):
            pick = picks[k * cap + j * CHUNK + i]
            piece = lax.dot_general(
                old[pick & 127],
                tiles[pick >> 7],
                (((1,), (1,)), ((), ())),
                preferred_element_type=jnp.float32,
            )
            turn[pl.ds(16 * i, 16), :] = piece
        for group in range(CHUNK // 16):
            for c in range(state_count):
                turned = turn[pl.ds(256 * group + c, 16, stride=16), :]
                outgoing[
                    k,
                    pl.ds(pl.multiple_of(j * CHUNK + 16 * group, 16), 16),
                    pl.ds(c * 128, 128),
                ] = turned.astype(jnp.bfloat16)

    count = chunks_of(gx, gy, nx, ny, caps)

    def channel(k):
        def chunk(j, carry):
            compute_chunk(k, j)
            chunk_copy(k, j).start()
            return carry

        lax.fori_loop(0, count, chunk, 0)

    each_channel(channel, goes_out)

    def own_chunk(j, carry):
        compute_chunk(8, j)
        return carry

    lax.fori_loop(0, cap // CHUNK, own_chunk, 0)

    row_ids = lax.broadcasted_iota(jnp.int32, (rows, 128), 0)

    def add(label_row, values, first):
        width = values.shape[0]
        selector = jnp.where(row_ids == label_row, 1.0, 0.0).astype(jnp.bfloat16)[:, :width]
        for c in range(0, state_count, 2):
            summed = jnp.dot(
                selector,
                values[:, c * 128 : (c + 2) * 128],
                preferred_element_type=jnp.float32,
            )
            if first:
                remapped[c] = summed[:, :128]
                remapped[c + 1] = summed[:, 128:]
            else:
                remapped[c] += summed[:, :128]
                remapped[c + 1] += summed[:, 128:]

    add(labels[8, 0:1, :], outgoing[8, 0 : 2 * CHUNK], True)
    add(labels[8, 1:2, :], outgoing[8, 2 * CHUNK : 4 * CHUNK], False)

    def accept(k):
        dx, dy = step_of(k)
        arriving = chunks_of(gx - dx, gy - dy, nx, ny, caps)
        label_copy(k).wait_recv()
        chunk_copy(k, 0).wait_recv()
        chunk_copy(k, 1).wait_recv()
        add(incoming_labels[k, 0:1, :], incoming[k, 0 : 2 * CHUNK], False)
        for j in (2, 3):

            @pl.when(arriving > j)
            def _():
                chunk_copy(k, j).wait_recv()
                add(
                    incoming_labels[k, j : j + 1, :],
                    incoming[k, j * CHUNK : (j + 1) * CHUNK],
                    False,
                )

    each_channel(accept, comes_in)

    lanes = lax.broadcasted_iota(jnp.int32, (32, 128), 1)
    for side, lane in ((0, 127), (1, 0)):
        packed = jnp.zeros((32, 128), jnp.float32)
        for b in range(rows // 32):
            for c in range(HALO_ROWS):
                ref = remapped.at[c] if c < state_count else vel.at[c - state_count]
                to = 16 * b + c
                moved = pltpu.roll(ref[pl.ds(32 * b, 32), :], (to - lane) % 128, 1)
                packed = jnp.where(lanes == to, moved, packed)
        edge_y[side] = packed
    for side, row in ((0, rows - 1), (1, 0)):
        for c in range(HALO_ROWS):
            ref = remapped.at[c] if c < state_count else vel.at[c - state_count]
            edge_x[side, c : c + 1, :] = ref[row : row + 1, :]
    sides = (
        (edge_y, halo_y, 0, 0, 1),
        (edge_y, halo_y, 1, 0, -1),
        (edge_x, halo_x, 0, 1, 0),
        (edge_x, halo_x, 1, -1, 0),
    )

    def side_copy(index):
        edge, _, side, dx, dy = sides[index]
        return pltpu.make_async_remote_copy(
            src_ref=edge.at[side],
            dst_ref=edge.at[side + 2],
            send_sem=edge_sems.at[0, index],
            recv_sem=edge_sems.at[1, index],
            device_id=(gx + dx, gy + dy),
            device_id_type=MESH,
        )

    for index, (_, _, _, dx, dy) in enumerate(sides):

        @pl.when(exists(gx + dx, gy + dy, nx, ny))
        def _():
            side_copy(index).start()

    for index, (edge, halo, side, dx, dy) in enumerate(sides):
        there = exists(gx - dx, gy - dy, nx, ny)

        @pl.when(there)
        def _():
            side_copy(index).wait_recv()
            halo[side] = edge[side + 2]

        @pl.when(jnp.logical_not(there))
        def _():
            halo[side] = jnp.zeros(halo.shape[1:], jnp.float32)

    for index, (_, _, _, dx, dy) in enumerate(sides):

        @pl.when(exists(gx + dx, gy + dy, nx, ny))
        def _():
            side_copy(index).wait_send()

    def finish(k):
        label_copy(k).wait_send()

        def chunk(j, carry):
            chunk_copy(k, j).wait_send()
            return carry

        lax.fori_loop(0, count, chunk, 0)

    each_channel(finish, goes_out)


def exchange(nx, ny, caps, collective_id, picks, labels, old, velocity, weights):
    state_count, rows = old.shape[1] // 16 * 12, velocity.shape[1]
    cap = labels.shape[2] // 128 * 192
    f32, vmem = jnp.float32, pltpu.VMEM
    in_vmem = pl.BlockSpec(memory_space=vmem)
    dma = pltpu.SemaphoreType.DMA
    return pl.pallas_call(
        functools.partial(exchange_kernel, nx, ny, caps),
        out_shape=(
            jax.ShapeDtypeStruct((state_count, rows, 128), f32),
            jax.ShapeDtypeStruct((2, 32, 128), f32),
            jax.ShapeDtypeStruct((2, 16, 128), f32),
        ),
        in_specs=[
            pl.BlockSpec(memory_space=pltpu.SMEM),
            in_vmem,
            in_vmem,
            in_vmem,
            pl.BlockSpec(memory_space=pl.ANY),
        ],
        out_specs=(in_vmem,) * 3,
        scratch_shapes=[
            vmem(weights.shape, jnp.bfloat16),
            vmem((9, cap, state_count * 128), jnp.bfloat16),
            vmem((8, cap, state_count * 128), jnp.bfloat16),
            vmem((8, 8, 128), jnp.int32),
            vmem((16 * CHUNK, 128), f32),
            vmem((4, 32, 128), f32),
            vmem((4, 16, 128), f32),
            dma((4,)),
            dma((2, 8)),
            dma((8, cap // CHUNK)),
            dma((8, cap // CHUNK)),
            dma((2, 4)),
        ],
        compiler_params=pltpu.CompilerParams(
            collective_id=collective_id, has_side_effects=True, vmem_limit_bytes=48 * MIB
        ),
        cost_estimate=pl.CostEstimate(
            flops=2 * picks.shape[0] * 128 * 128 * 16,
            bytes_accessed=weights.size * 2,
            transcendentals=0,
        ),
    )(picks, labels, old, velocity, weights)


def step_kernel(state, halo_y, halo_x, vel, out):
    b = pl.program_id(0)
    blocks = pl.num_programs(0)
    states, rows, depth = state.shape[0], state.shape[1], 32
    base = pl.multiple_of(b * depth, depth)
    lane = lax.broadcasted_iota(jnp.int32, (depth, 128), 1)
    row = lax.broadcasted_iota(jnp.int32, (depth, 128), 0)
    left_pack = pltpu.roll(halo_y[0], lax.rem(128 - 16 * b, 128), 1)
    right_pack = pltpu.roll(halo_y[1], lax.rem(128 + 127 - 16 * b, 128), 1)

    def around(ref, index, c):
        mid = ref[index, pl.ds(base, depth), :]
        above = jnp.where(b == 0, halo_x[0, c : c + 1, :], ref[index, pl.ds(jnp.maximum(base - 1, 0), 1), :])
        below = jnp.where(
            b == blocks - 1,
            halo_x[1, c : c + 1, :],
            ref[index, pl.ds(jnp.minimum(base + depth, rows - 1), 1), :],
        )
        before_x = jnp.where(row == 0, above, pltpu.roll(mid, 1, 0))
        after_x = jnp.where(row == depth - 1, below, pltpu.roll(mid, depth - 1, 0))
        shift = (128 - c) % 128
        before_y = jnp.where(lane == 0, pltpu.roll(left_pack, shift, 1), pltpu.roll(mid, 1, 1))
        after_y = jnp.where(lane == 127, pltpu.roll(right_pack, shift, 1), pltpu.roll(mid, 127, 1))
        return mid, before_x, after_x, before_y, after_y

    u_x, ux_bx, ux_ax, ux_by, ux_ay = around(vel, 0, states)
    u_y, uy_bx, uy_ax, uy_by, uy_ay = around(vel, 1, states + 1)
    d_xx = 0.5 * (ux_ax - ux_bx)
    l_xy = 0.5 * (ux_ay - ux_by)
    l_yx = 0.5 * (uy_ax - uy_bx)
    d_yy = 0.5 * (uy_ay - uy_by)
    d_zz = -(d_xx + d_yy)
    d_xy = 0.5 * (l_xy + l_yx)
    spin = 0.5 * (l_xy - l_yx)
    plus_x, minus_x = jnp.maximum(u_x, 0.0), jnp.minimum(u_x, 0.0)
    plus_y, minus_y = jnp.maximum(u_y, 0.0), jnp.minimum(u_y, 0.0)
    shear = (2.0 * interaction) * jnp.sqrt(
        2.0 * (d_xx * d_xx + d_yy * d_yy + d_zz * d_zz + 2.0 * (d_xy * d_xy)) + 1.0
    )
    a_xx, a_yy, a_zz, a_xy, a_xz, a_yz = (state[c, pl.ds(base, depth), :] for c in range(6))
    contraction = d_xx * a_xx + d_yy * a_yy + d_zz * a_zz + 2.0 * (d_xy * a_xy)
    fade = shape_factor * 2.0 * contraction + 3.0 * shear
    stress = 2.0 * shear_modulus
    pull = fiber_number * contraction
    sources = (
        2.0 * (spin * a_xy) + shape_factor * 2.0 * (d_xx * a_xx + d_xy * a_xy) - fade * a_xx + shear,
        -2.0 * (spin * a_xy) + shape_factor * 2.0 * (d_xy * a_xy + d_yy * a_yy) - fade * a_yy + shear,
        shape_factor * 2.0 * (d_zz * a_zz) - fade * a_zz + shear,
        spin * (a_yy - a_xx)
        + shape_factor * (d_xx * a_xy + d_xy * a_yy + a_xx * d_xy + a_xy * d_yy)
        - fade * a_xy,
        spin * a_yz + shape_factor * (d_xx * a_xz + d_xy * a_yz + a_xz * d_zz) - fade * a_xz,
        -spin * a_xz + shape_factor * (d_xy * a_xz + d_yy * a_yz + a_yz * d_zz) - fade * a_yz,
        d_xx,
        d_yy,
        d_xy,
        stress * (d_xx + pull * a_xx),
        stress * (d_yy + pull * a_yy),
        stress * (d_xy + pull * a_xy),
    )
    for c, source in enumerate(sources):
        mid, before_x, after_x, before_y, after_y = around(state, c, c)
        upwind = (
            plus_x * (mid - before_x)
            + minus_x * (after_x - mid)
            + plus_y * (mid - before_y)
            + minus_y * (after_y - mid)
        )
        out[c] = mid + time_step * (source - upwind)


def advance(state, halo_y, halo_x, velocity):
    in_vmem = pl.BlockSpec(memory_space=pltpu.VMEM)
    states, rows, width = state.shape
    return pl.pallas_call(
        step_kernel,
        grid=(rows // 32,),
        out_shape=jax.ShapeDtypeStruct(state.shape, jnp.float32),
        in_specs=[in_vmem] * 4,
        out_specs=pl.BlockSpec((states, 32, width), lambda b: (0, b, 0)),
        compiler_params=pltpu.CompilerParams(vmem_limit_bytes=24 * MIB),
    )(state, halo_y, halo_x, velocity)


def plan(source_block, tile_index, dest_device, dest_block, send_count, ny):
    slots = source_block.shape[0]
    cap = slots // 4
    live = jnp.arange(slots) < send_count[0]
    sx = dest_device // ny - lax.axis_index("gx")
    sy = dest_device % ny - lax.axis_index("gy")
    m = jnp.where(sx == 0, 2, (sx + 1) // 2)
    channel = jnp.where(sy == 0, jnp.where(sx == 0, 8, 6 + (sx + 1) // 2), 2 * m + (sy < 0))
    channel = jnp.where(live, channel, 9)
    matches = channel[None, :] == jnp.arange(9)[:, None]
    earlier = jnp.arange(slots)[:, None] < jnp.arange(slots)[None, :]
    position = jnp.dot(
        matches.astype(jnp.bfloat16),
        earlier.astype(jnp.bfloat16),
        preferred_element_type=jnp.float32,
    )
    position = jnp.sum(jnp.where(matches, position, 0.0), axis=0).astype(jnp.int32)
    target = jnp.where(live, channel * cap + position, -1)
    value = (tile_index * 128 + source_block) * 512 + dest_block + 1
    value = jnp.sum(
        jnp.where(target[None, :] == jnp.arange(9 * cap)[:, None], value[None, :], 0), axis=1
    )
    rows = (value % 512 - 1).reshape(9, cap)
    half, quarter = cap // 2, cap // 4
    pieces = (rows[:, :half], rows[:, half:], rows[:, half : half + quarter], rows[:, half + quarter :])
    pieces = [jnp.pad(p, ((0, 0), (0, 128 - p.shape[1]))) for p in pieces]
    labels = jnp.pad(jnp.stack(pieces, axis=1), ((0, 0), (0, 4), (0, 0)))
    return value // 512, labels


def per_device(
    nx,
    ny,
    old_states,
    weight_tiles,
    source_block,
    tile_index,
    dest_device,
    dest_block,
    send_count,
    velocity,
):
    picks, labels = plan(source_block, tile_index, dest_device, dest_block, send_count, ny)
    old = jnp.pad(old_states, ((0, 0), (0, 4), (0, 0)))
    state, halo_y, halo_x = exchange(
        nx, ny, (4, 4, 4), 0, picks, labels, old, velocity, weight_tiles
    )
    return jnp.transpose(advance(state, halo_y, halo_x, velocity), (1, 0, 2))


def solution(mesh):
    in_specs = (
        P(("gx", "gy"), None, None),
        P(("gx", "gy"), None, None),
        P(("gx", "gy")),
        P(("gx", "gy")),
        P(("gx", "gy")),
        P(("gx", "gy")),
        P(("gx", "gy")),
        P(None, "gx", "gy"),
    )
    out_specs = P("gx", None, "gy")
    return jax.shard_map(
        functools.partial(per_device, mesh.shape["gx"], mesh.shape["gy"]),
        mesh=mesh,
        in_specs=in_specs,
        out_specs=out_specs,
        check_vma=False,
    )
```

```python
import functools

import jax
import jax.numpy as jnp
from jax import lax
from jax.experimental import pallas as pl
from jax.experimental.pallas import tpu as pltpu
from jax.sharding import PartitionSpec as P

time_step = 0.2
shape_factor = 0.95
interaction = 0.01
shear_modulus = 1.0
fiber_number = 2.0

MESH = pl.DeviceIdType.MESH
CHUNK = 48
HALO_ROWS = 14
USUAL = (2, 3, 4)
FULL = (4, 4, 4)
MIB = 1 << 20


def step_of(k):
    m = k // 2
    dx = jnp.where(k < 6, jnp.where(m == 2, 0, 2 * m - 1), 2 * (k - 6) - 1)
    dy = jnp.where(k < 6, 1 - 2 * (k % 2), 0)
    return dx, dy


def exists(x, y, nx, ny):
    return (x >= 0) & (x < nx) & (y >= 0) & (y < ny)


def neighbours_of(x, y, nx, ny):
    spread_x = 3 - (x == 0).astype(jnp.int32) - (x == nx - 1).astype(jnp.int32)
    spread_y = 3 - (y == 0).astype(jnp.int32) - (y == ny - 1).astype(jnp.int32)
    return spread_x * spread_y - 1


def chunks_of(x, y, nx, ny, caps):
    n = neighbours_of(x, y, nx, ny)
    inner, edge, corner = caps
    return jnp.where(n >= 8, inner, jnp.where(n >= 5, edge, corner))


def mirrored(x, y, nx, ny, t):
    bits_x = nx.bit_length() - 1
    for step in range(bits_x):
        x = jnp.where(t == step, x + (1 - 2 * (x // 2**step % 2)) * 2**step, x)
    for step in range(ny.bit_length() - 1):
        y = jnp.where(t == bits_x + step, y + (1 - 2 * (y // 2**step % 2)) * 2**step, y)
    return x, y


def exchange_kernel(
    nx,
    ny,
    caps,
    picks,
    labels,
    over,
    old,
    vel,
    weights,
    remapped,
    halo_y,
    halo_x,
    any_over,
    tiles,
    outgoing,
    incoming,
    incoming_labels,
    turn,
    edge_y,
    edge_x,
    flags,
    flags_in,
    load_sem,
    label_sems,
    send_sems,
    recv_sems,
    edge_sems,
    flag_sems,
):
    gx, gy = lax.axis_index("gx"), lax.axis_index("gy")
    parts = load_sem.shape[0]
    depth = tiles.shape[0] // parts
    cap = outgoing.shape[1]
    rows = remapped.shape[1]
    state_count = remapped.shape[0]

    for part in range(parts):
        span = pl.ds(part * depth, depth)
        pltpu.make_async_copy(weights.at[span], tiles.at[span], load_sem.at[part]).start()

    barrier = pltpu.get_barrier_semaphore()
    for k in range(8):
        dx, dy = step_of(k)

        @pl.when(exists(gx + dx, gy + dy, nx, ny))
        def _():
            pl.semaphore_signal(
                barrier, inc=1, device_id=(gx + dx, gy + dy), device_id_type=MESH
            )

    swaps = flags_in.shape[0]
    for t in range(swaps):
        pl.semaphore_signal(
            barrier, inc=1, device_id=mirrored(gx, gy, nx, ny, t), device_id_type=MESH
        )
    pl.semaphore_wait(barrier, neighbours_of(gx, gy, nx, ny) + swaps)

    def flag_copy(t):
        return pltpu.make_async_remote_copy(
            src_ref=flags.at[t],
            dst_ref=flags_in.at[t],
            send_sem=flag_sems.at[0, t],
            recv_sem=flag_sems.at[1, t],
            device_id=mirrored(gx, gy, nx, ny, t),
            device_id_type=MESH,
        )

    flags[0] = over[...]
    flag_copy(0).start()

    def pass_flag(t):
        flag_copy(t).wait_recv()
        flags[t + 1] = jnp.maximum(flags[t], flags_in[t])

        @pl.when(t + 1 < swaps)
        def _():
            flag_copy(t + 1).start()

    def label_copy(k):
        dx, dy = step_of(k)
        return pltpu.make_async_remote_copy(
            src_ref=labels.at[k],
            dst_ref=incoming_labels.at[k],
            send_sem=label_sems.at[0, k],
            recv_sem=label_sems.at[1, k],
            device_id=(gx + dx, gy + dy),
            device_id_type=MESH,
        )

    def chunk_copy(k, j):
        dx, dy = step_of(k)
        span = pl.ds(j * CHUNK, CHUNK)
        return pltpu.make_async_remote_copy(
            src_ref=outgoing.at[k, span],
            dst_ref=incoming.at[k, span],
            send_sem=send_sems.at[k, j],
            recv_sem=recv_sems.at[k, j],
            device_id=(gx + dx, gy + dy),
            device_id_type=MESH,
        )

    def goes_out(k):
        dx, dy = step_of(k)
        return exists(gx + dx, gy + dy, nx, ny)

    def comes_in(k):
        dx, dy = step_of(k)
        return exists(gx - dx, gy - dy, nx, ny)

    def each_channel(body, predicate):
        def step(k, carry):
            @pl.when(predicate(k))
            def _():
                body(k)

            return carry

        lax.fori_loop(0, 8, step, 0)

    each_channel(lambda k: label_copy(k).start(), goes_out)

    for part in range(parts):
        span = pl.ds(part * depth, depth)
        pltpu.make_async_copy(weights.at[span], tiles.at[span], load_sem.at[part]).wait()

    def compute_chunk(k, j):
        for i in range(CHUNK):
            pick = picks[k * cap + j * CHUNK + i]
            piece = lax.dot_general(
                old[pick & 127],
                tiles[pick >> 7],
                (((1,), (1,)), ((), ())),
                preferred_element_type=jnp.float32,
            )
            turn[pl.ds(16 * i, 16), :] = piece
        for group in range(CHUNK // 16):
            for c in range(state_count):
                turned = turn[pl.ds(256 * group + c, 16, stride=16), :]
                outgoing[
                    k,
                    pl.ds(pl.multiple_of(j * CHUNK + 16 * group, 16), 16),
                    pl.ds(c * 128, 128),
                ] = turned.astype(jnp.bfloat16)

    count = chunks_of(gx, gy, nx, ny, caps)

    def channel(k):
        def chunk(j, carry):
            compute_chunk(k, j)
            chunk_copy(k, j).start()
            return carry

        lax.fori_loop(0, count, chunk, 0)

    def channel_and_flag(k, carry):
        @pl.when(goes_out(k))
        def _():
            channel(k)

        @pl.when(k < swaps)
        def _():
            pass_flag(k)

        return carry

    lax.fori_loop(0, 8, channel_and_flag, 0)

    def own_chunk(j, carry):
        compute_chunk(8, j)
        return carry

    lax.fori_loop(0, cap // CHUNK, own_chunk, 0)

    row_ids = lax.broadcasted_iota(jnp.int32, (rows, 128), 0)

    def add(label_row, values, first):
        width = values.shape[0]
        selector = jnp.where(row_ids == label_row, 1.0, 0.0).astype(jnp.bfloat16)[:, :width]
        for c in range(0, state_count, 2):
            summed = jnp.dot(
                selector,
                values[:, c * 128 : (c + 2) * 128],
                preferred_element_type=jnp.float32,
            )
            if first:
                remapped[c] = summed[:, :128]
                remapped[c + 1] = summed[:, 128:]
            else:
                remapped[c] += summed[:, :128]
                remapped[c + 1] += summed[:, 128:]

    add(labels[8, 0:1, :], outgoing[8, 0 : 2 * CHUNK], True)
    add(labels[8, 1:2, :], outgoing[8, 2 * CHUNK : 4 * CHUNK], False)

    def accept(k):
        dx, dy = step_of(k)
        arriving = chunks_of(gx - dx, gy - dy, nx, ny, caps)
        label_copy(k).wait_recv()
        chunk_copy(k, 0).wait_recv()
        chunk_copy(k, 1).wait_recv()
        add(incoming_labels[k, 0:1, :], incoming[k, 0 : 2 * CHUNK], False)
        for j in (2, 3):

            @pl.when(arriving > j)
            def _():
                chunk_copy(k, j).wait_recv()
                add(
                    incoming_labels[k, j : j + 1, :],
                    incoming[k, j * CHUNK : (j + 1) * CHUNK],
                    False,
                )

    each_channel(accept, comes_in)

    lanes = lax.broadcasted_iota(jnp.int32, (32, 128), 1)
    for side, lane in ((0, 127), (1, 0)):
        packed = jnp.zeros((32, 128), jnp.float32)
        for b in range(rows // 32):
            for c in range(HALO_ROWS):
                ref = remapped.at[c] if c < state_count else vel.at[c - state_count]
                to = 16 * b + c
                moved = pltpu.roll(ref[pl.ds(32 * b, 32), :], (to - lane) % 128, 1)
                packed = jnp.where(lanes == to, moved, packed)
        edge_y[side] = packed
    for side, row in ((0, rows - 1), (1, 0)):
        for c in range(HALO_ROWS):
            ref = remapped.at[c] if c < state_count else vel.at[c - state_count]
            edge_x[side, c : c + 1, :] = ref[row : row + 1, :]
    sides = (
        (edge_y, halo_y, 0, 0, 1),
        (edge_y, halo_y, 1, 0, -1),
        (edge_x, halo_x, 0, 1, 0),
        (edge_x, halo_x, 1, -1, 0),
    )

    def side_copy(index):
        edge, _, side, dx, dy = sides[index]
        return pltpu.make_async_remote_copy(
            src_ref=edge.at[side],
            dst_ref=edge.at[side + 2],
            send_sem=edge_sems.at[0, index],
            recv_sem=edge_sems.at[1, index],
            device_id=(gx + dx, gy + dy),
            device_id_type=MESH,
        )

    for index, (_, _, _, dx, dy) in enumerate(sides):

        @pl.when(exists(gx + dx, gy + dy, nx, ny))
        def _():
            side_copy(index).start()

    for index, (edge, halo, side, dx, dy) in enumerate(sides):
        there = exists(gx - dx, gy - dy, nx, ny)

        @pl.when(there)
        def _():
            side_copy(index).wait_recv()
            halo[side] = edge[side + 2]

        @pl.when(jnp.logical_not(there))
        def _():
            halo[side] = jnp.zeros(halo.shape[1:], jnp.float32)

    for index, (_, _, _, dx, dy) in enumerate(sides):

        @pl.when(exists(gx + dx, gy + dy, nx, ny))
        def _():
            side_copy(index).wait_send()

    def finish(k):
        label_copy(k).wait_send()

        def chunk(j, carry):
            chunk_copy(k, j).wait_send()
            return carry

        lax.fori_loop(0, count, chunk, 0)

    each_channel(finish, goes_out)
    for t in range(swaps):
        flag_copy(t).wait_send()
    any_over[...] = flags[swaps]


def exchange(nx, ny, caps, collective_id, picks, labels, over, old, velocity, weights):
    swaps = nx.bit_length() + ny.bit_length() - 2
    state_count, rows = HALO_ROWS - 2, velocity.shape[1]
    cap = labels.shape[2] // 128 * 192
    f32, vmem = jnp.float32, pltpu.VMEM
    in_vmem = pl.BlockSpec(memory_space=vmem)
    dma = pltpu.SemaphoreType.DMA
    return pl.pallas_call(
        functools.partial(exchange_kernel, nx, ny, caps),
        out_shape=(
            jax.ShapeDtypeStruct((state_count, rows, 128), f32),
            jax.ShapeDtypeStruct((2, 32, 128), f32),
            jax.ShapeDtypeStruct((2, 16, 128), f32),
            jax.ShapeDtypeStruct((8, 128), jnp.int32),
        ),
        in_specs=[
            pl.BlockSpec(memory_space=pltpu.SMEM),
            in_vmem,
            in_vmem,
            in_vmem,
            in_vmem,
            pl.BlockSpec(memory_space=pl.ANY),
        ],
        out_specs=(in_vmem,) * 4,
        scratch_shapes=[
            vmem(weights.shape, jnp.bfloat16),
            vmem((9, cap, state_count * 128), jnp.bfloat16),
            vmem((8, cap, state_count * 128), jnp.bfloat16),
            vmem((8, 8, 128), jnp.int32),
            vmem((16 * CHUNK, 128), f32),
            vmem((4, 32, 128), f32),
            vmem((4, 16, 128), f32),
            vmem((swaps + 1, 8, 128), jnp.int32),
            vmem((swaps, 8, 128), jnp.int32),
            dma((4,)),
            dma((2, 8)),
            dma((8, cap // CHUNK)),
            dma((8, cap // CHUNK)),
            dma((2, 4)),
            dma((2, swaps)),
        ],
        compiler_params=pltpu.CompilerParams(
            collective_id=collective_id, has_side_effects=True, vmem_limit_bytes=48 * MIB
        ),
        cost_estimate=pl.CostEstimate(
            flops=2 * picks.shape[0] * 128 * 128 * 16,
            bytes_accessed=weights.size * 2,
            transcendentals=0,
        ),
    )(picks, labels, over, old, velocity, weights)


def step_kernel(state, halo_y, halo_x, vel, out):
    b = pl.program_id(0)
    blocks = pl.num_programs(0)
    states, rows, depth = state.shape[0], state.shape[1], 32
    base = pl.multiple_of(b * depth, depth)
    lane = lax.broadcasted_iota(jnp.int32, (depth, 128), 1)
    row = lax.broadcasted_iota(jnp.int32, (depth, 128), 0)
    left_pack = pltpu.roll(halo_y[0], lax.rem(128 - 16 * b, 128), 1)
    right_pack = pltpu.roll(halo_y[1], lax.rem(128 + 127 - 16 * b, 128), 1)

    def around(ref, index, c):
        mid = ref[index, pl.ds(base, depth), :]
        above = jnp.where(b == 0, halo_x[0, c : c + 1, :], ref[index, pl.ds(jnp.maximum(base - 1, 0), 1), :])
        below = jnp.where(
            b == blocks - 1,
            halo_x[1, c : c + 1, :],
            ref[index, pl.ds(jnp.minimum(base + depth, rows - 1), 1), :],
        )
        before_x = jnp.where(row == 0, above, pltpu.roll(mid, 1, 0))
        after_x = jnp.where(row == depth - 1, below, pltpu.roll(mid, depth - 1, 0))
        shift = (128 - c) % 128
        before_y = jnp.where(lane == 0, pltpu.roll(left_pack, shift, 1), pltpu.roll(mid, 1, 1))
        after_y = jnp.where(lane == 127, pltpu.roll(right_pack, shift, 1), pltpu.roll(mid, 127, 1))
        return mid, before_x, after_x, before_y, after_y

    u_x, ux_bx, ux_ax, ux_by, ux_ay = around(vel, 0, states)
    u_y, uy_bx, uy_ax, uy_by, uy_ay = around(vel, 1, states + 1)
    d_xx = 0.5 * (ux_ax - ux_bx)
    l_xy = 0.5 * (ux_ay - ux_by)
    l_yx = 0.5 * (uy_ax - uy_bx)
    d_yy = 0.5 * (uy_ay - uy_by)
    d_zz = -(d_xx + d_yy)
    d_xy = 0.5 * (l_xy + l_yx)
    spin = 0.5 * (l_xy - l_yx)
    plus_x, minus_x = jnp.maximum(u_x, 0.0), jnp.minimum(u_x, 0.0)
    plus_y, minus_y = jnp.maximum(u_y, 0.0), jnp.minimum(u_y, 0.0)
    shear = (2.0 * interaction) * jnp.sqrt(
        2.0 * (d_xx * d_xx + d_yy * d_yy + d_zz * d_zz + 2.0 * (d_xy * d_xy)) + 1.0
    )
    a_xx, a_yy, a_zz, a_xy, a_xz, a_yz = (state[c, pl.ds(base, depth), :] for c in range(6))
    contraction = d_xx * a_xx + d_yy * a_yy + d_zz * a_zz + 2.0 * (d_xy * a_xy)
    fade = shape_factor * 2.0 * contraction + 3.0 * shear
    stress = 2.0 * shear_modulus
    pull = fiber_number * contraction
    sources = (
        2.0 * (spin * a_xy) + shape_factor * 2.0 * (d_xx * a_xx + d_xy * a_xy) - fade * a_xx + shear,
        -2.0 * (spin * a_xy) + shape_factor * 2.0 * (d_xy * a_xy + d_yy * a_yy) - fade * a_yy + shear,
        shape_factor * 2.0 * (d_zz * a_zz) - fade * a_zz + shear,
        spin * (a_yy - a_xx)
        + shape_factor * (d_xx * a_xy + d_xy * a_yy + a_xx * d_xy + a_xy * d_yy)
        - fade * a_xy,
        spin * a_yz + shape_factor * (d_xx * a_xz + d_xy * a_yz + a_xz * d_zz) - fade * a_xz,
        -spin * a_xz + shape_factor * (d_xy * a_xz + d_yy * a_yz + a_yz * d_zz) - fade * a_yz,
        d_xx,
        d_yy,
        d_xy,
        stress * (d_xx + pull * a_xx),
        stress * (d_yy + pull * a_yy),
        stress * (d_xy + pull * a_xy),
    )
    for c, source in enumerate(sources):
        mid, before_x, after_x, before_y, after_y = around(state, c, c)
        upwind = (
            plus_x * (mid - before_x)
            + minus_x * (after_x - mid)
            + plus_y * (mid - before_y)
            + minus_y * (after_y - mid)
        )
        out[c] = mid + time_step * (source - upwind)


def advance(state, halo_y, halo_x, velocity):
    in_vmem = pl.BlockSpec(memory_space=pltpu.VMEM)
    states, rows, width = state.shape
    return pl.pallas_call(
        step_kernel,
        grid=(rows // 32,),
        out_shape=jax.ShapeDtypeStruct(state.shape, jnp.float32),
        in_specs=[in_vmem] * 4,
        out_specs=pl.BlockSpec((states, 32, width), lambda b: (0, b, 0)),
        compiler_params=pltpu.CompilerParams(vmem_limit_bytes=24 * MIB),
    )(state, halo_y, halo_x, velocity)


def plan(source_block, tile_index, dest_device, dest_block, send_count, caps, nx, ny):
    slots = source_block.shape[0]
    cap = slots // 4
    live = jnp.arange(slots) < send_count[0]
    sx = dest_device // ny - lax.axis_index("gx")
    sy = dest_device % ny - lax.axis_index("gy")
    m = jnp.where(sx == 0, 2, (sx + 1) // 2)
    channel = jnp.where(sy == 0, jnp.where(sx == 0, 8, 6 + (sx + 1) // 2), 2 * m + (sy < 0))
    channel = jnp.where(live, channel, 9)
    matches = channel[None, :] == jnp.arange(9)[:, None]
    earlier = jnp.arange(slots)[:, None] < jnp.arange(slots)[None, :]
    position = jnp.dot(
        matches.astype(jnp.bfloat16),
        earlier.astype(jnp.bfloat16),
        preferred_element_type=jnp.float32,
    )
    position = jnp.sum(jnp.where(matches, position, 0.0), axis=0).astype(jnp.int32)
    target = jnp.where(live, channel * cap + position, -1)
    value = (tile_index * 128 + source_block) * 512 + dest_block + 1
    value = jnp.sum(
        jnp.where(target[None, :] == jnp.arange(9 * cap)[:, None], value[None, :], 0), axis=1
    )
    rows = (value % 512 - 1).reshape(9, cap)
    half, quarter = cap // 2, cap // 4
    pieces = (rows[:, :half], rows[:, half:], rows[:, half : half + quarter], rows[:, half + quarter :])
    pieces = [jnp.pad(p, ((0, 0), (0, 128 - p.shape[1]))) for p in pieces]
    labels = jnp.pad(jnp.stack(pieces, axis=1), ((0, 0), (0, 4), (0, 0)))
    counts = jnp.sum(matches.astype(jnp.int32), axis=1)[:8]
    allowed = chunks_of(lax.axis_index("gx"), lax.axis_index("gy"), nx, ny, caps) * CHUNK
    over = jnp.broadcast_to((jnp.max(counts) > allowed).astype(jnp.int32), (8, 128))
    return value // 512, labels, over


def per_device(
    nx,
    ny,
    old_states,
    weight_tiles,
    source_block,
    tile_index,
    dest_device,
    dest_block,
    send_count,
    velocity,
):
    picks, labels, over = plan(
        source_block, tile_index, dest_device, dest_block, send_count, USUAL, nx, ny
    )
    old = jnp.pad(old_states, ((0, 0), (0, 4), (0, 0)))
    *edges, any_over = exchange(
        nx, ny, USUAL, 0, picks, labels, over, old, velocity, weight_tiles
    )

    def again(*_):
        *edges, _ = exchange(nx, ny, FULL, 1, picks, labels, over, old, velocity, weight_tiles)
        return advance(*edges, velocity)

    def enough(*edges):
        return advance(*edges, velocity)

    states = lax.cond(any_over[0, 0] > 0, again, enough, *edges)
    return jnp.transpose(states, (1, 0, 2))


def solution(mesh):
    in_specs = (
        P(("gx", "gy"), None, None),
        P(("gx", "gy"), None, None),
        P(("gx", "gy")),
        P(("gx", "gy")),
        P(("gx", "gy")),
        P(("gx", "gy")),
        P(("gx", "gy")),
        P(None, "gx", "gy"),
    )
    out_specs = P("gx", None, "gy")
    return jax.shard_map(
        functools.partial(per_device, mesh.shape["gx"], mesh.shape["gy"]),
        mesh=mesh,
        in_specs=in_specs,
        out_specs=out_specs,
        check_vma=False,
    )
```

```python
import functools

import jax
import jax.numpy as jnp
from jax import lax
from jax.experimental import pallas as pl
from jax.experimental.pallas import tpu as pltpu
from jax.sharding import PartitionSpec as P

time_step = 0.2
shape_factor = 0.95
interaction = 0.01
shear_modulus = 1.0
fiber_number = 2.0

MESH = pl.DeviceIdType.MESH
CHUNK = 48
WIDE = 128
HALO_ROWS = 14
USUAL = (2, 3, 4)
FULL = (4, 4, 4)
MIB = 1 << 20


STEPS = ((-1, 1), (-1, -1), (1, 1), (1, -1), (0, 1), (0, -1), (-1, 0), (1, 0), (0, 0))


def step_of(k):
    m = k // 2
    dx = jnp.where(k < 6, jnp.where(m == 2, 0, 2 * m - 1), 2 * (k - 6) - 1)
    dy = jnp.where(k < 6, 1 - 2 * (k % 2), 0)
    return dx, dy


def exists(x, y, nx, ny):
    return (x >= 0) & (x < nx) & (y >= 0) & (y < ny)


def neighbours_of(x, y, nx, ny):
    spread_x = 3 - (x == 0).astype(jnp.int32) - (x == nx - 1).astype(jnp.int32)
    spread_y = 3 - (y == 0).astype(jnp.int32) - (y == ny - 1).astype(jnp.int32)
    return spread_x * spread_y - 1


def chunks_of(x, y, nx, ny, caps):
    n = neighbours_of(x, y, nx, ny)
    inner, edge, corner = caps
    return jnp.where(n >= 8, inner, jnp.where(n >= 5, edge, corner))


def plan_kernel(
    nx,
    ny,
    caps,
    send_count,
    source_block,
    tile_index,
    dest_device,
    dest_block,
    picks,
    labels,
    over_flag,
):
    gx, gy = lax.axis_index("gx"), lax.axis_index("gy")

    slots = source_block.shape[1]
    ids = lax.broadcasted_iota(jnp.int32, (1, slots), 1)
    place_shift = ny.bit_length() - 1
    step_x = (dest_device[...] >> place_shift) - gx
    step_y = (dest_device[...] & (ny - 1)) - gy
    channel_of = jnp.full((1, slots), 15, jnp.int32)
    for k, (dx, dy) in enumerate(STEPS):
        channel_of = jnp.where((step_x == dx) & (step_y == dy), k, channel_of)
    channel_of = jnp.where(ids < send_count[0], channel_of, 15)
    matches = channel_of == lax.broadcasted_iota(jnp.int32, (16, slots), 0)
    matches = matches & (lax.broadcasted_iota(jnp.int32, (16, slots), 0) < 9)
    ones = jnp.where(matches, 1.0, 0.0)
    counts = jnp.sum(ones, axis=1, keepdims=True)
    allowed = (chunks_of(gx, gy, nx, ny, caps) * CHUNK).astype(jnp.float32)
    over = jnp.max(jnp.where(counts[:8] > allowed, 1.0, 0.0), axis=0, keepdims=True)
    over_flag[...] = jnp.broadcast_to(over, over_flag.shape)
    before = lax.broadcasted_iota(jnp.int32, (slots, slots), 0) < lax.broadcasted_iota(
        jnp.int32, (slots, slots), 1
    )
    earlier = jnp.dot(
        ones.astype(jnp.bfloat16),
        jnp.where(before, 1.0, 0.0).astype(jnp.bfloat16),
        preferred_element_type=jnp.float32,
    )
    position = jnp.sum(ones * earlier, axis=0, keepdims=True).astype(jnp.int32)
    place = lax.broadcasted_iota(jnp.int32, (3 * WIDE, slots), 0)
    place = jnp.where(
        place < WIDE,
        jnp.where(place < 2 * CHUNK, place, -1),
        jnp.where(place % WIDE < CHUNK, place % WIDE + (place // WIDE + 1) * CHUNK, -1),
    )
    at_place = jnp.where(place == position, 1.0, 0.0).astype(jnp.bfloat16)
    tile = tile_index[...]
    parcels = [source_block[...], tile >> 1, tile & 1, dest_block[...] + 1]
    parcels = [(ones * v.astype(jnp.float32)).astype(jnp.bfloat16) for v in parcels]
    ordered = lax.dot_general(
        jnp.concatenate(parcels, axis=0),
        at_place,
        (((1,), (1,)), ((), ())),
        preferred_element_type=jnp.float32,
    )
    picks[...] = (
        (2.0 * ordered[16:32] + ordered[32:48]) * 128.0 + ordered[0:16]
    ).astype(jnp.int32)
    label_rows = ordered[48:64].astype(jnp.int32) - 1
    for k in range(9):
        labels[k] = label_rows[k : k + 1]


def plan(nx, ny, caps, lists):
    in_vmem = pl.BlockSpec(memory_space=pltpu.VMEM)
    return pl.pallas_call(
        functools.partial(plan_kernel, nx, ny, caps),
        out_shape=(
            jax.ShapeDtypeStruct((16, 3 * WIDE), jnp.int32),
            jax.ShapeDtypeStruct((9, 1, 3 * WIDE), jnp.int32),
            jax.ShapeDtypeStruct((8, 128), jnp.float32),
        ),
        in_specs=[pl.BlockSpec(memory_space=pltpu.SMEM)] + [in_vmem] * 4,
        out_specs=(in_vmem,) * 3,
    )(*lists)


def mirrored(x, y, nx, ny, t):
    bits_x = nx.bit_length() - 1
    for step in range(bits_x):
        x = jnp.where(t == step, x + (1 - 2 * (x // 2**step % 2)) * 2**step, x)
    for step in range(ny.bit_length() - 1):
        y = jnp.where(t == bits_x + step, y + (1 - 2 * (y // 2**step % 2)) * 2**step, y)
    return x, y


def exchange_kernel(
    nx,
    ny,
    caps,
    picks,
    labels,
    over,
    old,
    vel,
    weights,
    remapped,
    halo_y,
    halo_x,
    any_over,
    blocks,
    tiles,
    outgoing,
    incoming,
    incoming_labels,
    turn,
    edge_y,
    edge_x,
    flags,
    flags_in,
    load_sem,
    label_sems,
    send_sems,
    recv_sems,
    edge_sems,
    flag_sems,
):
    gx, gy = lax.axis_index("gx"), lax.axis_index("gy")
    parts = load_sem.shape[0]
    depth = tiles.shape[0] // parts
    cap = outgoing.shape[1]
    rows = remapped.shape[1]
    state_count = remapped.shape[0]

    for part in range(parts):
        span = pl.ds(part * depth, depth)
        pltpu.make_async_copy(weights.at[span], tiles.at[span], load_sem.at[part]).start()

    barrier = pltpu.get_barrier_semaphore()
    for k in range(8):
        dx, dy = step_of(k)

        @pl.when(exists(gx + dx, gy + dy, nx, ny))
        def _():
            pl.semaphore_signal(
                barrier, inc=1, device_id=(gx + dx, gy + dy), device_id_type=MESH
            )

    swaps = flags_in.shape[0]
    for t in range(swaps):
        pl.semaphore_signal(
            barrier, inc=1, device_id=mirrored(gx, gy, nx, ny, t), device_id_type=MESH
        )
    pl.semaphore_wait(barrier, neighbours_of(gx, gy, nx, ny) + swaps)

    def flag_copy(t):
        return pltpu.make_async_remote_copy(
            src_ref=flags.at[t],
            dst_ref=flags_in.at[t],
            send_sem=flag_sems.at[0, t],
            recv_sem=flag_sems.at[1, t],
            device_id=mirrored(gx, gy, nx, ny, t),
            device_id_type=MESH,
        )

    flags[0] = over[...]
    flag_copy(0).start()

    def pass_flag(t):
        flag_copy(t).wait_recv()
        flags[t + 1] = jnp.maximum(flags[t], flags_in[t])

        if t + 1 < swaps:
            flag_copy(t + 1).start()

    def label_copy(k):
        dx, dy = step_of(k)
        return pltpu.make_async_remote_copy(
            src_ref=labels.at[k],
            dst_ref=incoming_labels.at[k],
            send_sem=label_sems.at[0, k],
            recv_sem=label_sems.at[1, k],
            device_id=(gx + dx, gy + dy),
            device_id_type=MESH,
        )

    def chunk_copy(k, j):
        dx, dy = step_of(k)
        span = pl.ds(j * CHUNK, CHUNK)
        return pltpu.make_async_remote_copy(
            src_ref=outgoing.at[k, span],
            dst_ref=incoming.at[k, span],
            send_sem=send_sems.at[k, j],
            recv_sem=recv_sems.at[k, j],
            device_id=(gx + dx, gy + dy),
            device_id_type=MESH,
        )

    def goes_out(k):
        dx, dy = step_of(k)
        return exists(gx + dx, gy + dy, nx, ny)

    def comes_in(k):
        dx, dy = step_of(k)
        return exists(gx - dx, gy - dy, nx, ny)

    def each_channel(body, predicate):
        def step(k, carry):
            @pl.when(predicate(k))
            def _():
                body(k)

            return carry

        lax.fori_loop(0, 8, step, 0)

    each_channel(lambda k: label_copy(k).start(), goes_out)

    blocks[...] = jnp.zeros_like(blocks)
    for c in range(state_count):
        blocks[:, c, :] = old[c].astype(jnp.float32)
    for t in range(swaps):
        pass_flag(t)
    for part in range(parts):
        span = pl.ds(part * depth, depth)
        pltpu.make_async_copy(weights.at[span], tiles.at[span], load_sem.at[part]).wait()

    def compute_chunk(k, j):
        at = jnp.where(j < 2, j * CHUNK, (j - 1) * WIDE)
        none = jnp.zeros((16, 128), jnp.bfloat16)
        join = jnp.concatenate
        for i in range(0, CHUNK, 4):
            four = [picks[k, at + i + n] for n in range(4)]
            a = [blocks[p & 127].astype(jnp.bfloat16) for p in four]
            w = [tiles[p >> 7] for p in four]
            left = join([join([a[n], none] if n % 2 == 0 else [none, a[n]], 1) for n in range(4)], 0)
            right = join([join([w[0], w[1]], 1), join([w[2], w[3]], 1)], 0)
            piece = lax.dot_general(
                left, right, (((1,), (1,)), ((), ())), preferred_element_type=jnp.float32
            )
            turn[pl.ds(16 * i, 32), :] = piece[:32, :128]
            turn[pl.ds(16 * i + 32, 32), :] = piece[32:, 128:]
        for group in range(CHUNK // 16):
            for c in range(state_count):
                turned = turn[pl.ds(256 * group + c, 16, stride=16), :]
                outgoing[
                    k,
                    pl.ds(pl.multiple_of(j * CHUNK + 16 * group, 16), 16),
                    pl.ds(c * 128, 128),
                ] = turned.astype(jnp.bfloat16)

    count = chunks_of(gx, gy, nx, ny, caps)

    def channel(k):
        def chunk(j, carry):
            compute_chunk(k, j)
            chunk_copy(k, j).start()
            return carry

        lax.fori_loop(0, count, chunk, 0)

    each_channel(channel, goes_out)

    def own_chunk(j, carry):
        compute_chunk(8, j)
        return carry

    lax.fori_loop(0, cap // CHUNK, own_chunk, 0)

    row_ids = lax.broadcasted_iota(jnp.int32, (rows, WIDE), 0)

    def add(label_row, values, first):
        width = values.shape[0]
        selector = jnp.where(row_ids == label_row, 1.0, 0.0).astype(jnp.bfloat16)[:, :width]
        for c in range(0, state_count, 2):
            summed = jnp.dot(
                selector,
                values[:, c * 128 : (c + 2) * 128],
                preferred_element_type=jnp.float32,
            )
            if first:
                remapped[c] = summed[:, :128]
                remapped[c + 1] = summed[:, 128:]
            else:
                remapped[c] += summed[:, :128]
                remapped[c + 1] += summed[:, 128:]

    add(labels[8, :, :WIDE], outgoing[8, : 2 * CHUNK], True)
    for j in (2, 3):
        span = slice((j - 1) * WIDE, j * WIDE)
        add(labels[8, :, span], outgoing[8, j * CHUNK : (j + 1) * CHUNK], False)

    def accept(k):
        dx, dy = step_of(k)
        arriving = chunks_of(gx - dx, gy - dy, nx, ny, caps)
        label_copy(k).wait_recv()
        chunk_copy(k, 0).wait_recv()
        chunk_copy(k, 1).wait_recv()
        add(incoming_labels[k, :, :WIDE], incoming[k, 0 : 2 * CHUNK], False)
        for j in (2, 3):

            @pl.when(arriving > j)
            def _():
                chunk_copy(k, j).wait_recv()
                add(
                    incoming_labels[k, :, (j - 1) * WIDE : j * WIDE],
                    incoming[k, j * CHUNK : (j + 1) * CHUNK],
                    False,
                )

    each_channel(accept, comes_in)

    lanes = lax.broadcasted_iota(jnp.int32, (32, 128), 1)
    for side, lane in ((0, 127), (1, 0)):
        packed = jnp.zeros((32, 128), jnp.float32)
        for b in range(rows // 32):
            for c in range(HALO_ROWS):
                ref = remapped.at[c] if c < state_count else vel.at[c - state_count]
                to = 16 * b + c
                moved = pltpu.roll(ref[pl.ds(32 * b, 32), :], (to - lane) % 128, 1)
                packed = jnp.where(lanes == to, moved, packed)
        edge_y[side] = packed
    for side, row in ((0, rows - 1), (1, 0)):
        for c in range(HALO_ROWS):
            ref = remapped.at[c] if c < state_count else vel.at[c - state_count]
            edge_x[side, c : c + 1, :] = ref[row : row + 1, :]
    sides = (
        (edge_y, halo_y, 0, 0, 1),
        (edge_y, halo_y, 1, 0, -1),
        (edge_x, halo_x, 0, 1, 0),
        (edge_x, halo_x, 1, -1, 0),
    )

    def side_copy(index):
        edge, _, side, dx, dy = sides[index]
        return pltpu.make_async_remote_copy(
            src_ref=edge.at[side],
            dst_ref=edge.at[side + 2],
            send_sem=edge_sems.at[0, index],
            recv_sem=edge_sems.at[1, index],
            device_id=(gx + dx, gy + dy),
            device_id_type=MESH,
        )

    for index, (_, _, _, dx, dy) in enumerate(sides):

        @pl.when(exists(gx + dx, gy + dy, nx, ny))
        def _():
            side_copy(index).start()

    for index, (edge, halo, side, dx, dy) in enumerate(sides):
        there = exists(gx - dx, gy - dy, nx, ny)

        @pl.when(there)
        def _():
            side_copy(index).wait_recv()
            halo[side] = edge[side + 2]

        @pl.when(jnp.logical_not(there))
        def _():
            halo[side] = jnp.zeros(halo.shape[1:], jnp.float32)

    for index, (_, _, _, dx, dy) in enumerate(sides):

        @pl.when(exists(gx + dx, gy + dy, nx, ny))
        def _():
            side_copy(index).wait_send()

    def finish(k):
        label_copy(k).wait_send()

        def chunk(j, carry):
            chunk_copy(k, j).wait_send()
            return carry

        lax.fori_loop(0, count, chunk, 0)

    each_channel(finish, goes_out)
    for t in range(swaps):
        flag_copy(t).wait_send()
    any_over[...] = flags[swaps]


def exchange(nx, ny, caps, collective_id, picks, labels, over, old, velocity, weights):
    swaps = nx.bit_length() + ny.bit_length() - 2
    state_count, rows = old.shape[0], velocity.shape[1]
    cap = 4 * CHUNK
    f32, vmem = jnp.float32, pltpu.VMEM
    in_vmem = pl.BlockSpec(memory_space=vmem)
    dma = pltpu.SemaphoreType.DMA
    return pl.pallas_call(
        functools.partial(exchange_kernel, nx, ny, caps),
        out_shape=(
            jax.ShapeDtypeStruct((state_count, rows, 128), f32),
            jax.ShapeDtypeStruct((2, 32, 128), f32),
            jax.ShapeDtypeStruct((2, 16, 128), f32),
            jax.ShapeDtypeStruct((8, 128), f32),
        ),
        in_specs=[pl.BlockSpec(memory_space=pltpu.SMEM)]
        + [in_vmem] * 4
        + [pl.BlockSpec(memory_space=pl.ANY)],
        out_specs=(in_vmem,) * 4,
        scratch_shapes=[
            vmem((old.shape[1], 16, 128), f32),
            vmem(weights.shape, jnp.bfloat16),
            vmem((9, cap, state_count * 128), jnp.bfloat16),
            vmem((8, cap, state_count * 128), jnp.bfloat16),
            vmem((8, 1, 3 * WIDE), jnp.int32),
            vmem((16 * CHUNK, 128), f32),
            vmem((4, 32, 128), f32),
            vmem((4, 16, 128), f32),
            vmem((swaps + 1, 8, 128), f32),
            vmem((swaps, 8, 128), f32),
            dma((4,)),
            dma((2, 8)),
            dma((8, cap // CHUNK)),
            dma((8, cap // CHUNK)),
            dma((2, 4)),
            dma((2, swaps)),
        ],
        compiler_params=pltpu.CompilerParams(
            collective_id=collective_id, has_side_effects=True, vmem_limit_bytes=48 * MIB
        ),
        cost_estimate=pl.CostEstimate(
            flops=2 * 9 * cap * 128 * 128 * 16,
            bytes_accessed=weights.size * 2,
            transcendentals=0,
        ),
    )(picks, labels, over, old, velocity, weights)


def step_kernel(state, halo_y, halo_x, vel, out):
    b = pl.program_id(0)
    blocks = pl.num_programs(0)
    states, rows, depth = state.shape[0], state.shape[1], 32
    base = pl.multiple_of(b * depth, depth)
    lane = lax.broadcasted_iota(jnp.int32, (depth, 128), 1)
    row = lax.broadcasted_iota(jnp.int32, (depth, 128), 0)
    left_pack = pltpu.roll(halo_y[0], lax.rem(128 - 16 * b, 128), 1)
    right_pack = pltpu.roll(halo_y[1], lax.rem(128 + 127 - 16 * b, 128), 1)

    def around(ref, index, c):
        mid = ref[index, pl.ds(base, depth), :]
        above = jnp.where(b == 0, halo_x[0, c : c + 1, :], ref[index, pl.ds(jnp.maximum(base - 1, 0), 1), :])
        below = jnp.where(
            b == blocks - 1,
            halo_x[1, c : c + 1, :],
            ref[index, pl.ds(jnp.minimum(base + depth, rows - 1), 1), :],
        )
        before_x = jnp.where(row == 0, above, pltpu.roll(mid, 1, 0))
        after_x = jnp.where(row == depth - 1, below, pltpu.roll(mid, depth - 1, 0))
        shift = (128 - c) % 128
        before_y = jnp.where(lane == 0, pltpu.roll(left_pack, shift, 1), pltpu.roll(mid, 1, 1))
        after_y = jnp.where(lane == 127, pltpu.roll(right_pack, shift, 1), pltpu.roll(mid, 127, 1))
        return mid, before_x, after_x, before_y, after_y

    u_x, ux_bx, ux_ax, ux_by, ux_ay = around(vel, 0, states)
    u_y, uy_bx, uy_ax, uy_by, uy_ay = around(vel, 1, states + 1)
    d_xx = 0.5 * (ux_ax - ux_bx)
    l_xy = 0.5 * (ux_ay - ux_by)
    l_yx = 0.5 * (uy_ax - uy_bx)
    d_yy = 0.5 * (uy_ay - uy_by)
    d_zz = -(d_xx + d_yy)
    d_xy = 0.5 * (l_xy + l_yx)
    spin = 0.5 * (l_xy - l_yx)
    plus_x, minus_x = jnp.maximum(u_x, 0.0), jnp.minimum(u_x, 0.0)
    plus_y, minus_y = jnp.maximum(u_y, 0.0), jnp.minimum(u_y, 0.0)
    shear = (2.0 * interaction) * jnp.sqrt(
        2.0 * (d_xx * d_xx + d_yy * d_yy + d_zz * d_zz + 2.0 * (d_xy * d_xy)) + 1.0
    )
    a_xx, a_yy, a_zz, a_xy, a_xz, a_yz = (state[c, pl.ds(base, depth), :] for c in range(6))
    contraction = d_xx * a_xx + d_yy * a_yy + d_zz * a_zz + 2.0 * (d_xy * a_xy)
    fade = shape_factor * 2.0 * contraction + 3.0 * shear
    stress = 2.0 * shear_modulus
    pull = fiber_number * contraction
    sources = (
        2.0 * (spin * a_xy) + shape_factor * 2.0 * (d_xx * a_xx + d_xy * a_xy) - fade * a_xx + shear,
        -2.0 * (spin * a_xy) + shape_factor * 2.0 * (d_xy * a_xy + d_yy * a_yy) - fade * a_yy + shear,
        shape_factor * 2.0 * (d_zz * a_zz) - fade * a_zz + shear,
        spin * (a_yy - a_xx)
        + shape_factor * (d_xx * a_xy + d_xy * a_yy + a_xx * d_xy + a_xy * d_yy)
        - fade * a_xy,
        spin * a_yz + shape_factor * (d_xx * a_xz + d_xy * a_yz + a_xz * d_zz) - fade * a_xz,
        -spin * a_xz + shape_factor * (d_xy * a_xz + d_yy * a_yz + a_yz * d_zz) - fade * a_yz,
        d_xx,
        d_yy,
        d_xy,
        stress * (d_xx + pull * a_xx),
        stress * (d_yy + pull * a_yy),
        stress * (d_xy + pull * a_xy),
    )
    for c, source in enumerate(sources):
        mid, before_x, after_x, before_y, after_y = around(state, c, c)
        upwind = (
            plus_x * (mid - before_x)
            + minus_x * (after_x - mid)
            + plus_y * (mid - before_y)
            + minus_y * (after_y - mid)
        )
        out[c] = mid + time_step * (source - upwind)


def advance(state, halo_y, halo_x, velocity):
    in_vmem = pl.BlockSpec(memory_space=pltpu.VMEM)
    states, rows, width = state.shape
    return pl.pallas_call(
        step_kernel,
        grid=(rows // 32,),
        out_shape=jax.ShapeDtypeStruct(state.shape, jnp.float32),
        in_specs=[in_vmem] * 4,
        out_specs=pl.BlockSpec((states, 32, width), lambda b: (0, b, 0)),
        compiler_params=pltpu.CompilerParams(vmem_limit_bytes=24 * MIB),
    )(state, halo_y, halo_x, velocity)


def per_device(
    nx,
    ny,
    old_states,
    weight_tiles,
    source_block,
    tile_index,
    dest_device,
    dest_block,
    send_count,
    velocity,
):
    lists = [send_count] + [
        v.reshape(1, -1) for v in (source_block, tile_index, dest_device, dest_block)
    ]
    old = jnp.transpose(old_states, (1, 0, 2))
    places = plan(nx, ny, USUAL, lists)
    *edges, any_over = exchange(nx, ny, USUAL, 0, *places, old, velocity, weight_tiles)

    def again(*_):
        *edges, _ = exchange(nx, ny, FULL, 1, *places, old, velocity, weight_tiles)
        return advance(*edges, velocity)

    def enough(*edges):
        return advance(*edges, velocity)

    states = lax.cond(any_over[0, 0] > 0, again, enough, *edges)
    return jnp.transpose(states, (1, 0, 2))


def solution(mesh):
    in_specs = (
        P(("gx", "gy"), None, None),
        P(("gx", "gy"), None, None),
        P(("gx", "gy")),
        P(("gx", "gy")),
        P(("gx", "gy")),
        P(("gx", "gy")),
        P(("gx", "gy")),
        P(None, "gx", "gy"),
    )
    out_specs = P("gx", None, "gy")
    return jax.shard_map(
        functools.partial(per_device, mesh.shape["gx"], mesh.shape["gy"]),
        mesh=mesh,
        in_specs=in_specs,
        out_specs=out_specs,
        check_vma=False,
    )
```

```python
import functools

import jax
import jax.numpy as jnp
from jax import lax
from jax.experimental import pallas as pl
from jax.experimental.pallas import tpu as pltpu
from jax.sharding import PartitionSpec as P

time_step = 0.2
shape_factor = 0.95
interaction = 0.01
shear_modulus = 1.0
fiber_number = 2.0

MESH = pl.DeviceIdType.MESH
CHUNK = 32
WIDE = 128
FIRST = 3
CHUNKS = 6
HALO_ROWS = 14
USUAL = (3, 4, 5, 6)
FULL = (6, 6, 6, 6)
MIB = 1 << 20


STEPS = ((-1, 1), (-1, -1), (1, 1), (1, -1), (0, 1), (0, -1), (-1, 0), (1, 0), (0, 0))


def step_of(k):
    m = k // 2
    dx = jnp.where(k < 6, jnp.where(m == 2, 0, 2 * m - 1), 2 * (k - 6) - 1)
    dy = jnp.where(k < 6, 1 - 2 * (k % 2), 0)
    return dx, dy


def exists(x, y, nx, ny):
    return (x >= 0) & (x < nx) & (y >= 0) & (y < ny)


def neighbours_of(x, y, nx, ny):
    spread_x = 3 - (x == 0).astype(jnp.int32) - (x == nx - 1).astype(jnp.int32)
    spread_y = 3 - (y == 0).astype(jnp.int32) - (y == ny - 1).astype(jnp.int32)
    return spread_x * spread_y - 1


def chunks_of(x, y, dy, nx, ny, caps):
    n = neighbours_of(x, y, nx, ny)
    inner, along, edge, corner = caps
    sidewise = jnp.where((dy != 0) & ((y == 0) | (y == ny - 1)), along, edge)
    return jnp.where(n >= 8, inner, jnp.where(n >= 5, sidewise, corner))


def plan_kernel(
    nx,
    ny,
    caps,
    send_count,
    source_block,
    tile_index,
    dest_device,
    dest_block,
    picks,
    labels,
    over_flag,
):
    gx, gy = lax.axis_index("gx"), lax.axis_index("gy")

    slots = source_block.shape[0]
    dest, tile = dest_device[...].reshape(1, slots), tile_index[...].reshape(1, slots)
    ids = lax.broadcasted_iota(jnp.int32, (1, slots), 1)
    place_shift = ny.bit_length() - 1
    step_x = (dest >> place_shift) - gx
    step_y = (dest & (ny - 1)) - gy
    channel_of = jnp.full((1, slots), 15, jnp.int32)
    for k, (dx, dy) in enumerate(STEPS):
        channel_of = jnp.where((step_x == dx) & (step_y == dy), k, channel_of)
    channel_of = jnp.where(ids < send_count[0], channel_of, 15)
    matches = channel_of == lax.broadcasted_iota(jnp.int32, (16, slots), 0)
    matches = matches & (lax.broadcasted_iota(jnp.int32, (16, slots), 0) < 9)
    ones = jnp.where(matches, 1.0, 0.0)
    counts = jnp.sum(ones, axis=1, keepdims=True)
    over = jnp.zeros((1, 1), jnp.float32)
    for k, (_, dy) in enumerate(STEPS[:8]):
        allowed = (chunks_of(gx, gy, dy, nx, ny, caps) * CHUNK).astype(jnp.float32)
        over = jnp.maximum(over, jnp.where(counts[k : k + 1] > allowed, 1.0, 0.0))
    over_flag[...] = jnp.broadcast_to(over, over_flag.shape)
    before = lax.broadcasted_iota(jnp.int32, (slots, slots), 0) < lax.broadcasted_iota(
        jnp.int32, (slots, slots), 1
    )
    earlier = jnp.dot(
        ones.astype(jnp.bfloat16),
        jnp.where(before, 1.0, 0.0).astype(jnp.bfloat16),
        preferred_element_type=jnp.float32,
    )
    position = jnp.sum(ones * earlier, axis=0, keepdims=True).astype(jnp.int32)
    place = lax.broadcasted_iota(jnp.int32, (4 * WIDE, slots), 0)
    place = jnp.where(
        place < WIDE,
        jnp.where(place < FIRST * CHUNK, place, -1),
        jnp.where(place % WIDE < CHUNK, place % WIDE + (place // WIDE + FIRST - 1) * CHUNK, -1),
    )
    at_place = jnp.where(place == position, 1.0, 0.0).astype(jnp.bfloat16)
    source, row = source_block[...].reshape(1, slots), dest_block[...].reshape(1, slots)
    parcels = [source, tile >> 1, tile & 1, row + 1]
    parcels = [(ones * v.astype(jnp.float32)).astype(jnp.bfloat16) for v in parcels]
    ordered = lax.dot_general(
        jnp.concatenate(parcels, axis=0),
        at_place,
        (((1,), (1,)), ((), ())),
        preferred_element_type=jnp.float32,
    )
    picks[...] = (
        (2.0 * ordered[16:32] + ordered[32:48]) * 128.0 + ordered[0:16]
    ).astype(jnp.int32)
    label_rows = ordered[48:64].astype(jnp.int32) - 1
    for k in range(9):
        labels[k] = label_rows[k : k + 1]


def plan(nx, ny, caps, lists):
    in_vmem = pl.BlockSpec(memory_space=pltpu.VMEM)
    return pl.pallas_call(
        functools.partial(plan_kernel, nx, ny, caps),
        out_shape=(
            jax.ShapeDtypeStruct((16, 4 * WIDE), jnp.int32),
            jax.ShapeDtypeStruct((9, 1, 4 * WIDE), jnp.int32),
            jax.ShapeDtypeStruct((1, 128), jnp.float32),
        ),
        in_specs=[pl.BlockSpec(memory_space=pltpu.SMEM)] + [in_vmem] * 4,
        out_specs=(in_vmem,) * 3,
    )(*lists)


def exchange_kernel(
    nx,
    ny,
    caps,
    picks,
    labels,
    over,
    old,
    vel,
    weights,
    remapped,
    halo_y,
    halo_x,
    any_over,
    blocks,
    tiles,
    outgoing,
    incoming,
    incoming_labels,
    turn,
    edge_y,
    edge_x,
    flags,
    flags_in,
    load_sem,
    label_sems,
    send_sems,
    recv_sems,
    edge_sems,
    flag_sems,
):
    gx, gy = lax.axis_index("gx"), lax.axis_index("gy")
    parts = load_sem.shape[0]
    depth = tiles.shape[0] // parts
    cap = outgoing.shape[1]
    rows = remapped.shape[1]
    state_count = remapped.shape[0]

    for part in range(parts):
        span = pl.ds(part * depth, depth)
        pltpu.make_async_copy(weights.at[span], tiles.at[span], load_sem.at[part]).start()

    barrier = pltpu.get_barrier_semaphore()
    for k in range(8):
        dx, dy = step_of(k)

        @pl.when(exists(gx + dx, gy + dy, nx, ny))
        def _():
            pl.semaphore_signal(
                barrier, inc=1, device_id=(gx + dx, gy + dy), device_id_type=MESH
            )


    def along_gx(j):
        return (lax.rem(gx + j, nx), gy)

    def along_gy(j):
        return (gx, lax.rem(gy + j, ny))

    def greet(j, carry, along):
        pl.semaphore_signal(barrier, inc=1, device_id=along(j), device_id_type=MESH)
        return carry

    lax.fori_loop(1, nx, functools.partial(greet, along=along_gx), 0)
    lax.fori_loop(1, ny, functools.partial(greet, along=along_gy), 0)
    pl.semaphore_wait(barrier, neighbours_of(gx, gy, nx, ny) + nx + ny - 2)

    def flag_copy(turn_of, j):
        slot = turn_of * nx + j
        return pltpu.make_async_remote_copy(
            src_ref=flags.at[turn_of],
            dst_ref=flags_in.at[slot],
            send_sem=flag_sems.at[0, slot],
            recv_sem=flag_sems.at[1, slot],
            device_id=(along_gx, along_gy)[turn_of](j),
            device_id_type=MESH,
        )

    def send_flag(turn_of):
        def step(j, carry):
            flag_copy(turn_of, j).start()
            return carry

        lax.fori_loop(1, (nx, ny)[turn_of], step, 0)

    def gather_flag(turn_of):
        def step(j, carry):
            flag_copy(turn_of, j).wait_recv()
            return jnp.maximum(carry, flags_in[turn_of * nx + j])

        flags[turn_of + 1] = lax.fori_loop(1, (nx, ny)[turn_of], step, flags[turn_of])

    def end_flag(turn_of):
        def step(j, carry):
            flag_copy(turn_of, j).wait_send()
            return carry

        lax.fori_loop(1, (nx, ny)[turn_of], step, 0)

    flags[0] = over[...]
    send_flag(0)

    def label_copy(k):
        dx, dy = step_of(k)
        return pltpu.make_async_remote_copy(
            src_ref=labels.at[k],
            dst_ref=incoming_labels.at[k],
            send_sem=label_sems.at[0, k],
            recv_sem=label_sems.at[1, k],
            device_id=(gx + dx, gy + dy),
            device_id_type=MESH,
        )

    def chunk_copy(k, j):
        dx, dy = step_of(k)
        span = pl.ds(j * CHUNK, CHUNK)
        return pltpu.make_async_remote_copy(
            src_ref=outgoing.at[k, span],
            dst_ref=incoming.at[k, span],
            send_sem=send_sems.at[k, j],
            recv_sem=recv_sems.at[k, j],
            device_id=(gx + dx, gy + dy),
            device_id_type=MESH,
        )

    def goes_out(k):
        dx, dy = step_of(k)
        return exists(gx + dx, gy + dy, nx, ny)

    def comes_in(k):
        dx, dy = step_of(k)
        return exists(gx - dx, gy - dy, nx, ny)

    def each_channel(body, predicate):
        def step(k, carry):
            @pl.when(predicate(k))
            def _():
                body(k)

            return carry

        lax.fori_loop(0, 8, step, 0)

    each_channel(lambda k: label_copy(k).start(), goes_out)

    blocks[...] = jnp.zeros_like(blocks)
    for c in range(state_count):
        blocks[:, c, :] = old[c].astype(jnp.float32)
    for part in range(parts):
        span = pl.ds(part * depth, depth)
        pltpu.make_async_copy(weights.at[span], tiles.at[span], load_sem.at[part]).wait()

    def compute_chunk(k, j):
        at = jnp.where(j < FIRST, j * CHUNK, (j - FIRST + 1) * WIDE)
        none = jnp.zeros((16, 128), jnp.bfloat16)
        join = jnp.concatenate
        for i in range(0, CHUNK, 4):
            four = [picks[k, at + i + n] for n in range(4)]
            a = [blocks[p & 127].astype(jnp.bfloat16) for p in four]
            w = [tiles[p >> 7] for p in four]
            left = join([join([a[n], none] if n % 2 == 0 else [none, a[n]], 1) for n in range(4)], 0)
            right = join([join([w[0], w[1]], 1), join([w[2], w[3]], 1)], 0)
            piece = lax.dot_general(
                left, right, (((1,), (1,)), ((), ())), preferred_element_type=jnp.float32
            )
            turn[pl.ds(16 * i, 32), :] = piece[:32, :128]
            turn[pl.ds(16 * i + 32, 32), :] = piece[32:, 128:]
        for group in range(CHUNK // 16):
            for c in range(state_count):
                turned = turn[pl.ds(256 * group + c, 16, stride=16), :]
                outgoing[
                    k,
                    pl.ds(pl.multiple_of(j * CHUNK + 16 * group, 16), 16),
                    pl.ds(c * 128, 128),
                ] = turned.astype(jnp.bfloat16)

    def sent(k):
        _, dy = step_of(k)
        return chunks_of(gx, gy, dy, nx, ny, caps)

    def channel(k, carry):
        def chunk(j, carry):
            compute_chunk(k, j)

            @pl.when(k < 8)
            def _():
                chunk_copy(k, j).start()

            return carry

        @pl.when((k == 8) | goes_out(k))
        def _():
            lax.fori_loop(0, jnp.where(k == 8, CHUNKS, sent(k)), chunk, 0)

        @pl.when(k == 1)
        def _():
            gather_flag(0)
            send_flag(1)

        return carry

    lax.fori_loop(0, 9, channel, 0)

    row_ids = lax.broadcasted_iota(jnp.int32, (rows, WIDE), 0)

    def add(label_row, values, first):
        width = values.shape[0]
        selector = jnp.where(row_ids == label_row, 1.0, 0.0).astype(jnp.bfloat16)[:, :width]
        for c in range(0, state_count, 2):
            summed = jnp.dot(
                selector,
                values[:, c * 128 : (c + 2) * 128],
                preferred_element_type=jnp.float32,
            )
            if first:
                remapped[c] = summed[:, :128]
                remapped[c + 1] = summed[:, 128:]
            else:
                remapped[c] += summed[:, :128]
                remapped[c + 1] += summed[:, 128:]

    def add_piece(label_rows, k, values, first):
        add(label_rows[k, :, :WIDE], values[k, : FIRST * CHUNK], first)

    def add_chunk(label_rows, k, values, j):
        lanes_of = slice((j - FIRST + 1) * WIDE, (j - FIRST + 2) * WIDE)
        add(label_rows[k, :, lanes_of], values[k, j * CHUNK : (j + 1) * CHUNK], False)

    add_piece(labels, 8, outgoing, True)
    for j in range(FIRST, CHUNKS):
        add_chunk(labels, 8, outgoing, j)

    def accept(k):
        dx, dy = step_of(k)
        arriving = chunks_of(gx - dx, gy - dy, dy, nx, ny, caps)
        label_copy(k).wait_recv()
        for j in range(FIRST):
            chunk_copy(k, j).wait_recv()
        add_piece(incoming_labels, k, incoming, False)
        for j in range(FIRST, CHUNKS):

            @pl.when(arriving > j)
            def _():
                chunk_copy(k, j).wait_recv()
                add_chunk(incoming_labels, k, incoming, j)

    each_channel(accept, comes_in)

    lanes = lax.broadcasted_iota(jnp.int32, (32, 128), 1)
    for side, lane in ((0, 127), (1, 0)):
        packed = jnp.zeros((32, 128), jnp.float32)
        for b in range(rows // 32):
            for c in range(HALO_ROWS):
                ref = remapped.at[c] if c < state_count else vel.at[c - state_count]
                to = 16 * b + c
                moved = pltpu.roll(ref[pl.ds(32 * b, 32), :], (to - lane) % 128, 1)
                packed = jnp.where(lanes == to, moved, packed)
        edge_y[side] = packed
    for side, row in ((0, rows - 1), (1, 0)):
        for c in range(HALO_ROWS):
            ref = remapped.at[c] if c < state_count else vel.at[c - state_count]
            edge_x[side, c : c + 1, :] = ref[row : row + 1, :]
    sides = (
        (edge_y, halo_y, 0, 0, 1),
        (edge_y, halo_y, 1, 0, -1),
        (edge_x, halo_x, 0, 1, 0),
        (edge_x, halo_x, 1, -1, 0),
    )

    def side_copy(index):
        edge, _, side, dx, dy = sides[index]
        return pltpu.make_async_remote_copy(
            src_ref=edge.at[side],
            dst_ref=edge.at[side + 2],
            send_sem=edge_sems.at[0, index],
            recv_sem=edge_sems.at[1, index],
            device_id=(gx + dx, gy + dy),
            device_id_type=MESH,
        )

    for index, (_, _, _, dx, dy) in enumerate(sides):

        @pl.when(exists(gx + dx, gy + dy, nx, ny))
        def _():
            side_copy(index).start()

    for index, (edge, halo, side, dx, dy) in enumerate(sides):
        there = exists(gx - dx, gy - dy, nx, ny)

        @pl.when(there)
        def _():
            side_copy(index).wait_recv()
            halo[side] = edge[side + 2]

        @pl.when(jnp.logical_not(there))
        def _():
            halo[side] = jnp.zeros(halo.shape[1:], jnp.float32)

    for index, (_, _, _, dx, dy) in enumerate(sides):

        @pl.when(exists(gx + dx, gy + dy, nx, ny))
        def _():
            side_copy(index).wait_send()

    def finish(k):
        label_copy(k).wait_send()

        def chunk(j, carry):
            chunk_copy(k, j).wait_send()
            return carry

        lax.fori_loop(0, sent(k), chunk, 0)

    each_channel(finish, goes_out)
    gather_flag(1)
    end_flag(0)
    end_flag(1)
    any_over[...] = flags[2]


def exchange(nx, ny, caps, collective_id, picks, labels, over, old, velocity, weights):
    state_count, rows = old.shape[0], velocity.shape[1]
    cap = CHUNKS * CHUNK
    f32, vmem = jnp.float32, pltpu.VMEM
    in_vmem = pl.BlockSpec(memory_space=vmem)
    dma = pltpu.SemaphoreType.DMA
    return pl.pallas_call(
        functools.partial(exchange_kernel, nx, ny, caps),
        out_shape=(
            jax.ShapeDtypeStruct((state_count, rows, 128), f32),
            jax.ShapeDtypeStruct((2, 32, 128), f32),
            jax.ShapeDtypeStruct((2, 16, 128), f32),
            jax.ShapeDtypeStruct((1, 128), f32),
        ),
        in_specs=[pl.BlockSpec(memory_space=pltpu.SMEM)]
        + [in_vmem] * 4
        + [pl.BlockSpec(memory_space=pl.ANY)],
        out_specs=(in_vmem,) * 4,
        scratch_shapes=[
            vmem((old.shape[1], 16, 128), f32),
            vmem(weights.shape, jnp.bfloat16),
            vmem((9, cap, state_count * 128), jnp.bfloat16),
            vmem((8, cap, state_count * 128), jnp.bfloat16),
            vmem((8, 1, 4 * WIDE), jnp.int32),
            vmem((16 * CHUNK, 128), f32),
            vmem((4, 32, 128), f32),
            vmem((4, 16, 128), f32),
            vmem((3, 1, 128), f32),
            vmem((nx + ny, 1, 128), f32),
            dma((4,)),
            dma((2, 8)),
            dma((8, cap // CHUNK)),
            dma((8, cap // CHUNK)),
            dma((2, 4)),
            dma((2, nx + ny)),
        ],
        compiler_params=pltpu.CompilerParams(
            collective_id=collective_id, has_side_effects=True, vmem_limit_bytes=48 * MIB
        ),
        cost_estimate=pl.CostEstimate(
            flops=2 * 9 * cap * 128 * 128 * 16,
            bytes_accessed=weights.size * 2,
            transcendentals=0,
        ),
    )(picks, labels, over, old, velocity, weights)


def step_kernel(state, halo_y, halo_x, vel, out):
    b = pl.program_id(0)
    blocks = pl.num_programs(0)
    states, rows, depth = state.shape[0], state.shape[1], 32
    base = pl.multiple_of(b * depth, depth)
    lane = lax.broadcasted_iota(jnp.int32, (depth, 128), 1)
    row = lax.broadcasted_iota(jnp.int32, (depth, 128), 0)
    left_pack = pltpu.roll(halo_y[0], lax.rem(128 - 16 * b, 128), 1)
    right_pack = pltpu.roll(halo_y[1], lax.rem(128 + 127 - 16 * b, 128), 1)

    def around(ref, index, c):
        mid = ref[index, pl.ds(base, depth), :]
        above = jnp.where(b == 0, halo_x[0, c : c + 1, :], ref[index, pl.ds(jnp.maximum(base - 1, 0), 1), :])
        below = jnp.where(
            b == blocks - 1,
            halo_x[1, c : c + 1, :],
            ref[index, pl.ds(jnp.minimum(base + depth, rows - 1), 1), :],
        )
        before_x = jnp.where(row == 0, above, pltpu.roll(mid, 1, 0))
        after_x = jnp.where(row == depth - 1, below, pltpu.roll(mid, depth - 1, 0))
        shift = (128 - c) % 128
        before_y = jnp.where(lane == 0, pltpu.roll(left_pack, shift, 1), pltpu.roll(mid, 1, 1))
        after_y = jnp.where(lane == 127, pltpu.roll(right_pack, shift, 1), pltpu.roll(mid, 127, 1))
        return mid, before_x, after_x, before_y, after_y

    u_x, ux_bx, ux_ax, ux_by, ux_ay = around(vel, 0, states)
    u_y, uy_bx, uy_ax, uy_by, uy_ay = around(vel, 1, states + 1)
    d_xx = 0.5 * (ux_ax - ux_bx)
    l_xy = 0.5 * (ux_ay - ux_by)
    l_yx = 0.5 * (uy_ax - uy_bx)
    d_yy = 0.5 * (uy_ay - uy_by)
    d_zz = -(d_xx + d_yy)
    d_xy = 0.5 * (l_xy + l_yx)
    spin = 0.5 * (l_xy - l_yx)
    plus_x, minus_x = jnp.maximum(u_x, 0.0), jnp.minimum(u_x, 0.0)
    plus_y, minus_y = jnp.maximum(u_y, 0.0), jnp.minimum(u_y, 0.0)
    shear = (2.0 * interaction) * jnp.sqrt(
        2.0 * (d_xx * d_xx + d_yy * d_yy + d_zz * d_zz + 2.0 * (d_xy * d_xy)) + 1.0
    )
    a_xx, a_yy, a_zz, a_xy, a_xz, a_yz = (state[c, pl.ds(base, depth), :] for c in range(6))
    contraction = d_xx * a_xx + d_yy * a_yy + d_zz * a_zz + 2.0 * (d_xy * a_xy)
    fade = shape_factor * 2.0 * contraction + 3.0 * shear
    stress = 2.0 * shear_modulus
    pull = fiber_number * contraction
    sources = (
        2.0 * (spin * a_xy) + shape_factor * 2.0 * (d_xx * a_xx + d_xy * a_xy) - fade * a_xx + shear,
        -2.0 * (spin * a_xy) + shape_factor * 2.0 * (d_xy * a_xy + d_yy * a_yy) - fade * a_yy + shear,
        shape_factor * 2.0 * (d_zz * a_zz) - fade * a_zz + shear,
        spin * (a_yy - a_xx)
        + shape_factor * (d_xx * a_xy + d_xy * a_yy + a_xx * d_xy + a_xy * d_yy)
        - fade * a_xy,
        spin * a_yz + shape_factor * (d_xx * a_xz + d_xy * a_yz + a_xz * d_zz) - fade * a_xz,
        -spin * a_xz + shape_factor * (d_xy * a_xz + d_yy * a_yz + a_yz * d_zz) - fade * a_yz,
        d_xx,
        d_yy,
        d_xy,
        stress * (d_xx + pull * a_xx),
        stress * (d_yy + pull * a_yy),
        stress * (d_xy + pull * a_xy),
    )
    for c, source in enumerate(sources):
        mid, before_x, after_x, before_y, after_y = around(state, c, c)
        upwind = (
            plus_x * (mid - before_x)
            + minus_x * (after_x - mid)
            + plus_y * (mid - before_y)
            + minus_y * (after_y - mid)
        )
        out[c] = mid + time_step * (source - upwind)


def advance(state, halo_y, halo_x, velocity):
    in_vmem = pl.BlockSpec(memory_space=pltpu.VMEM)
    states, rows, width = state.shape
    return pl.pallas_call(
        step_kernel,
        grid=(rows // 32,),
        out_shape=jax.ShapeDtypeStruct(state.shape, jnp.float32),
        in_specs=[in_vmem] * 4,
        out_specs=pl.BlockSpec((states, 32, width), lambda b: (0, b, 0)),
        compiler_params=pltpu.CompilerParams(vmem_limit_bytes=24 * MIB),
    )(state, halo_y, halo_x, velocity)


def per_device(
    nx,
    ny,
    old_states,
    weight_tiles,
    source_block,
    tile_index,
    dest_device,
    dest_block,
    send_count,
    velocity,
):
    lists = (send_count, source_block, tile_index, dest_device, dest_block)
    old = jnp.transpose(old_states, (1, 0, 2))
    places = plan(nx, ny, USUAL, lists)
    *edges, any_over = exchange(nx, ny, USUAL, 0, *places, old, velocity, weight_tiles)

    def again(*_):
        *edges, _ = exchange(nx, ny, FULL, 1, *places, old, velocity, weight_tiles)
        return advance(*edges, velocity)

    def enough(*edges):
        return advance(*edges, velocity)

    states = lax.cond(any_over[0, 0] > 0, again, enough, *edges)
    return jnp.transpose(states, (1, 0, 2))


def solution(mesh):
    in_specs = (
        P(("gx", "gy"), None, None),
        P(("gx", "gy"), None, None),
        P(("gx", "gy")),
        P(("gx", "gy")),
        P(("gx", "gy")),
        P(("gx", "gy")),
        P(("gx", "gy")),
        P(None, "gx", "gy"),
    )
    out_specs = P("gx", None, "gy")
    return jax.shard_map(
        functools.partial(per_device, mesh.shape["gx"], mesh.shape["gy"]),
        mesh=mesh,
        in_specs=in_specs,
        out_specs=out_specs,
        check_vma=False,
    )
```

```python
import functools

import jax
import jax.numpy as jnp
from jax import lax
from jax.experimental import pallas as pl
from jax.experimental.pallas import tpu as pltpu
from jax.sharding import PartitionSpec as P

time_step = 0.2
shape_factor = 0.95
interaction = 0.01
shear_modulus = 1.0
fiber_number = 2.0

MESH = pl.DeviceIdType.MESH
CHUNK = 32
WIDE = 128
FIRST = 3
CHUNKS = 6
USUAL = (3, 4, 5, 6)
FULL = (6, 6, 6, 6)
MIB = 1 << 20


STEPS = ((-1, 1), (-1, -1), (1, 1), (1, -1), (0, 1), (0, -1), (-1, 0), (1, 0), (0, 0))


def step_of(k):
    m = k // 2
    dx = jnp.where(k < 6, jnp.where(m == 2, 0, 2 * m - 1), 2 * (k - 6) - 1)
    dy = jnp.where(k < 6, 1 - 2 * (k % 2), 0)
    return dx, dy


def exists(x, y, nx, ny):
    return (x >= 0) & (x < nx) & (y >= 0) & (y < ny)


def neighbours_of(x, y, nx, ny):
    spread_x = 3 - (x == 0).astype(jnp.int32) - (x == nx - 1).astype(jnp.int32)
    spread_y = 3 - (y == 0).astype(jnp.int32) - (y == ny - 1).astype(jnp.int32)
    return spread_x * spread_y - 1


def chunks_of(x, y, dy, nx, ny, caps):
    n = neighbours_of(x, y, nx, ny)
    inner, along, edge, corner = caps
    sidewise = jnp.where((dy != 0) & ((y == 0) | (y == ny - 1)), along, edge)
    return jnp.where(n >= 8, inner, jnp.where(n >= 5, sidewise, corner))


def plan_kernel(
    nx,
    ny,
    caps,
    send_count,
    source_block,
    tile_index,
    dest_device,
    dest_block,
    picks,
    labels,
    over_flag,
):
    gx, gy = lax.axis_index("gx"), lax.axis_index("gy")

    slots = source_block.shape[0]
    dest, tile = dest_device[...].reshape(1, slots), tile_index[...].reshape(1, slots)
    ids = lax.broadcasted_iota(jnp.int32, (1, slots), 1)
    place_shift = ny.bit_length() - 1
    step_x = (dest >> place_shift) - gx
    step_y = (dest & (ny - 1)) - gy
    channel_of = jnp.full((1, slots), 15, jnp.int32)
    for k, (dx, dy) in enumerate(STEPS):
        channel_of = jnp.where((step_x == dx) & (step_y == dy), k, channel_of)
    channel_of = jnp.where(ids < send_count[0], channel_of, 15)
    matches = channel_of == lax.broadcasted_iota(jnp.int32, (16, slots), 0)
    matches = matches & (lax.broadcasted_iota(jnp.int32, (16, slots), 0) < 9)
    ones = jnp.where(matches, 1.0, 0.0)
    counts = jnp.sum(ones, axis=1, keepdims=True)
    over = jnp.zeros((1, 1), jnp.float32)
    for k, (_, dy) in enumerate(STEPS[:8]):
        allowed = (chunks_of(gx, gy, dy, nx, ny, caps) * CHUNK).astype(jnp.float32)
        over = jnp.maximum(over, jnp.where(counts[k : k + 1] > allowed, 1.0, 0.0))
    over_flag[...] = jnp.broadcast_to(over, over_flag.shape)
    before = lax.broadcasted_iota(jnp.int32, (slots, slots), 0) < lax.broadcasted_iota(
        jnp.int32, (slots, slots), 1
    )
    earlier = jnp.dot(
        ones.astype(jnp.bfloat16),
        jnp.where(before, 1.0, 0.0).astype(jnp.bfloat16),
        preferred_element_type=jnp.float32,
    )
    position = jnp.sum(ones * earlier, axis=0, keepdims=True).astype(jnp.int32)
    place = lax.broadcasted_iota(jnp.int32, (4 * WIDE, slots), 0)
    place = jnp.where(
        place < WIDE,
        jnp.where(place < FIRST * CHUNK, place, -1),
        jnp.where(place % WIDE < CHUNK, place % WIDE + (place // WIDE + FIRST - 1) * CHUNK, -1),
    )
    at_place = jnp.where(place == position, 1.0, 0.0).astype(jnp.bfloat16)
    source, row = source_block[...].reshape(1, slots), dest_block[...].reshape(1, slots)
    parcels = [source, tile >> 1, tile & 1, row + 1]
    parcels = [(ones * v.astype(jnp.float32)).astype(jnp.bfloat16) for v in parcels]
    ordered = lax.dot_general(
        jnp.concatenate(parcels, axis=0),
        at_place,
        (((1,), (1,)), ((), ())),
        preferred_element_type=jnp.float32,
    )
    picks[...] = (
        (2.0 * ordered[16:32] + ordered[32:48]) * 128.0 + ordered[0:16]
    ).astype(jnp.int32)
    label_rows = ordered[48:64].astype(jnp.int32) - 1
    for k in range(9):
        labels[k] = label_rows[k : k + 1]


def plan(nx, ny, caps, lists):
    in_vmem = pl.BlockSpec(memory_space=pltpu.VMEM)
    return pl.pallas_call(
        functools.partial(plan_kernel, nx, ny, caps),
        out_shape=(
            jax.ShapeDtypeStruct((16, 4 * WIDE), jnp.int32),
            jax.ShapeDtypeStruct((9, 1, 4 * WIDE), jnp.int32),
            jax.ShapeDtypeStruct((1, 128), jnp.float32),
        ),
        in_specs=[pl.BlockSpec(memory_space=pltpu.SMEM)] + [in_vmem] * 4,
        out_specs=(in_vmem,) * 3,
    )(*lists)


def exchange_kernel(
    nx,
    ny,
    caps,
    picks,
    labels,
    over,
    old,
    vel,
    weights,
    out,
    any_over,
    remapped,
    blocks,
    tiles,
    outgoing,
    incoming,
    incoming_labels,
    turn,
    edge_y,
    edge_x,
    flow_y,
    flow_x,
    flags,
    flags_in,
    load_sem,
    label_sems,
    send_sems,
    recv_sems,
    edge_sems,
    flow_sems,
    flag_sems,
):
    gx, gy = lax.axis_index("gx"), lax.axis_index("gy")
    parts = load_sem.shape[0]
    depth = tiles.shape[0] // parts
    cap = outgoing.shape[1]
    state_count, rows = remapped.shape[:2]

    for part in range(parts):
        span = pl.ds(part * depth, depth)
        pltpu.make_async_copy(weights.at[span], tiles.at[span], load_sem.at[part]).start()

    barrier = pltpu.get_barrier_semaphore()
    for k in range(8):
        dx, dy = step_of(k)

        @pl.when(exists(gx + dx, gy + dy, nx, ny))
        def _():
            pl.semaphore_signal(
                barrier, inc=1, device_id=(gx + dx, gy + dy), device_id_type=MESH
            )


    def along_gx(j):
        return (lax.rem(gx + j, nx), gy)

    def along_gy(j):
        return (gx, lax.rem(gy + j, ny))

    def greet(j, carry, along):
        pl.semaphore_signal(barrier, inc=1, device_id=along(j), device_id_type=MESH)
        return carry

    lax.fori_loop(1, nx, functools.partial(greet, along=along_gx), 0)
    lax.fori_loop(1, ny, functools.partial(greet, along=along_gy), 0)
    pl.semaphore_wait(barrier, neighbours_of(gx, gy, nx, ny) + nx + ny - 2)

    def flag_copy(turn_of, j):
        slot = turn_of * nx + j
        return pltpu.make_async_remote_copy(
            src_ref=flags.at[turn_of],
            dst_ref=flags_in.at[slot],
            send_sem=flag_sems.at[0, slot],
            recv_sem=flag_sems.at[1, slot],
            device_id=(along_gx, along_gy)[turn_of](j),
            device_id_type=MESH,
        )

    def send_flag(turn_of):
        def step(j, carry):
            flag_copy(turn_of, j).start()
            return carry

        lax.fori_loop(1, (nx, ny)[turn_of], step, 0)

    def gather_flag(turn_of):
        def step(j, carry):
            flag_copy(turn_of, j).wait_recv()
            return jnp.maximum(carry, flags_in[turn_of * nx + j])

        flags[turn_of + 1] = lax.fori_loop(1, (nx, ny)[turn_of], step, flags[turn_of])

    def end_flag(turn_of):
        def step(j, carry):
            flag_copy(turn_of, j).wait_send()
            return carry

        lax.fori_loop(1, (nx, ny)[turn_of], step, 0)

    flags[0] = over[...]
    send_flag(0)

    def label_copy(k):
        dx, dy = step_of(k)
        return pltpu.make_async_remote_copy(
            src_ref=labels.at[k],
            dst_ref=incoming_labels.at[k],
            send_sem=label_sems.at[0, k],
            recv_sem=label_sems.at[1, k],
            device_id=(gx + dx, gy + dy),
            device_id_type=MESH,
        )

    def chunk_copy(k, j):
        dx, dy = step_of(k)
        span = pl.ds(j * CHUNK, CHUNK)
        return pltpu.make_async_remote_copy(
            src_ref=outgoing.at[k, span],
            dst_ref=incoming.at[k, span],
            send_sem=send_sems.at[k, j],
            recv_sem=recv_sems.at[k, j],
            device_id=(gx + dx, gy + dy),
            device_id_type=MESH,
        )

    def goes_out(k):
        dx, dy = step_of(k)
        return exists(gx + dx, gy + dy, nx, ny)

    def comes_in(k):
        dx, dy = step_of(k)
        return exists(gx - dx, gy - dy, nx, ny)

    def each_channel(body, predicate):
        def step(k, carry):
            @pl.when(predicate(k))
            def _():
                body(k)

            return carry

        lax.fori_loop(0, 8, step, 0)

    each_channel(lambda k: label_copy(k).start(), goes_out)

    lanes = lax.broadcasted_iota(jnp.int32, (32, 128), 1)
    sides = ((0, 0, 1), (1, 0, -1), (0, 1, 0), (1, -1, 0))

    def pack_edges(ref, along_y, along_x):
        planes = ref.shape[0]
        for side, lane in ((0, 127), (1, 0)):
            packed = jnp.zeros((32, 128), jnp.float32)
            for b in range(rows // 32):
                for c in range(planes):
                    to = 16 * b + c
                    moved = pltpu.roll(ref[c, pl.ds(32 * b, 32), :], (to - lane) % 128, 1)
                    packed = jnp.where(lanes == to, moved, packed)
            along_y[side] = packed
        for side, row in ((0, rows - 1), (1, 0)):
            for c in range(planes):
                along_x[side, c : c + 1, :] = ref[c, row : row + 1, :]

    def side_copy(index, along_y, along_x, sems):
        side, dx, dy = sides[index]
        edge = along_y if dx == 0 else along_x
        return pltpu.make_async_remote_copy(
            src_ref=edge.at[side],
            dst_ref=edge.at[side + 2],
            send_sem=sems.at[0, index],
            recv_sem=sems.at[1, index],
            device_id=(gx + dx, gy + dy),
            device_id_type=MESH,
        )

    def each_side(body, sign):
        for index, (_, dx, dy) in enumerate(sides):

            @pl.when(exists(gx + sign * dx, gy + sign * dy, nx, ny))
            def _():
                body(index)

    flow = (flow_y, flow_x, flow_sems)
    edges = (edge_y, edge_x, edge_sems)
    pack_edges(vel, flow_y, flow_x)
    each_side(lambda index: side_copy(index, *flow).start(), 1)

    blocks[...] = jnp.zeros_like(blocks)
    for c in range(state_count):
        blocks[:, c, :] = old[c].astype(jnp.float32)
    for part in range(parts):
        span = pl.ds(part * depth, depth)
        pltpu.make_async_copy(weights.at[span], tiles.at[span], load_sem.at[part]).wait()

    def compute_chunk(k, j):
        at = jnp.where(j < FIRST, j * CHUNK, (j - FIRST + 1) * WIDE)
        none = jnp.zeros((16, 128), jnp.bfloat16)
        join = jnp.concatenate
        for i in range(0, CHUNK, 4):
            four = [picks[k, at + i + n] for n in range(4)]
            a = [blocks[p & 127].astype(jnp.bfloat16) for p in four]
            w = [tiles[p >> 7] for p in four]
            left = join([join([a[n], none] if n % 2 == 0 else [none, a[n]], 1) for n in range(4)], 0)
            right = join([join([w[0], w[1]], 1), join([w[2], w[3]], 1)], 0)
            piece = lax.dot_general(
                left, right, (((1,), (1,)), ((), ())), preferred_element_type=jnp.float32
            )
            turn[pl.ds(16 * i, 32), :] = piece[:32, :128]
            turn[pl.ds(16 * i + 32, 32), :] = piece[32:, 128:]
        for group in range(CHUNK // 16):
            for c in range(state_count):
                turned = turn[pl.ds(256 * group + c, 16, stride=16), :]
                outgoing[
                    k,
                    pl.ds(pl.multiple_of(j * CHUNK + 16 * group, 16), 16),
                    pl.ds(c * 128, 128),
                ] = turned.astype(jnp.bfloat16)

    def sent(k):
        _, dy = step_of(k)
        return chunks_of(gx, gy, dy, nx, ny, caps)

    def channel(k, carry):
        def chunk(j, carry):
            compute_chunk(k, j)

            @pl.when(k < 8)
            def _():
                chunk_copy(k, j).start()

            return carry

        @pl.when((k == 8) | goes_out(k))
        def _():
            lax.fori_loop(0, jnp.where(k == 8, CHUNKS, sent(k)), chunk, 0)

        @pl.when(k == 1)
        def _():
            gather_flag(0)
            send_flag(1)

        return carry

    lax.fori_loop(0, 9, channel, 0)

    row_ids = lax.broadcasted_iota(jnp.int32, (rows, WIDE), 0)

    def add(label_row, values, first):
        width = values.shape[0]
        selector = jnp.where(row_ids == label_row, 1.0, 0.0).astype(jnp.bfloat16)[:, :width]
        for c in range(0, state_count, 2):
            summed = jnp.dot(
                selector,
                values[:, c * 128 : (c + 2) * 128],
                preferred_element_type=jnp.float32,
            )
            if first:
                remapped[c] = summed[:, :128]
                remapped[c + 1] = summed[:, 128:]
            else:
                remapped[c] += summed[:, :128]
                remapped[c + 1] += summed[:, 128:]

    def add_piece(label_rows, k, values, first):
        add(label_rows[k, :, :WIDE], values[k, : FIRST * CHUNK], first)

    def add_chunk(label_rows, k, values, j):
        lanes_of = slice((j - FIRST + 1) * WIDE, (j - FIRST + 2) * WIDE)
        add(label_rows[k, :, lanes_of], values[k, j * CHUNK : (j + 1) * CHUNK], False)

    add_piece(labels, 8, outgoing, True)
    for j in range(FIRST, CHUNKS):
        add_chunk(labels, 8, outgoing, j)

    def accept(k):
        dx, dy = step_of(k)
        arriving = chunks_of(gx - dx, gy - dy, dy, nx, ny, caps)
        label_copy(k).wait_recv()
        for j in range(FIRST):
            chunk_copy(k, j).wait_recv()
        add_piece(incoming_labels, k, incoming, False)
        for j in range(FIRST, CHUNKS):

            @pl.when(arriving > j)
            def _():
                chunk_copy(k, j).wait_recv()
                add_chunk(incoming_labels, k, incoming, j)

    def accept_in_turn(i, carry):
        k = lax.rem(i + 6, 8)

        @pl.when(comes_in(k))
        def _():
            accept(k)

        return carry

    lax.fori_loop(0, 8, accept_in_turn, 0)

    pack_edges(remapped, edge_y, edge_x)
    each_side(lambda index: side_copy(index, *edges).start(), 1)

    each_side(lambda index: side_copy(index, *flow).wait_recv(), -1)
    for index, (side, dx, dy) in enumerate(sides):
        edge = flow_y if dx == 0 else flow_x

        @pl.when(jnp.logical_not(exists(gx - dx, gy - dy, nx, ny)))
        def _():
            edge[side + 2] = jnp.zeros(edge.shape[1:], jnp.float32)

    def step(b, carry):
        step_block(b, rows // 32, remapped, vel, flow_y, flow_x, out)
        return carry

    lax.fori_loop(0, rows // 32, step, 0)

    def add_side(index):
        side_copy(index, *edges).wait_recv()
        side, dx, dy = sides[index]
        bound = jnp.maximum if side == 0 else jnp.minimum
        scale = time_step if side == 0 else -time_step
        if dx != 0:
            row = 0 if side == 0 else rows - 1
            speed = scale * bound(vel[0, row : row + 1, :], 0.0)
            for c in range(state_count):
                out[c, row : row + 1, :] += speed * edge_x[side + 2, c : c + 1, :]
            return
        lane = 0 if side == 0 else 127

        def add_block(b, carry):
            span = pl.ds(pl.multiple_of(32 * b, 32), 32)
            speed = jnp.where(lanes == lane, scale * bound(vel[1, span, :], 0.0), 0.0)
            pack = pltpu.roll(edge_y[side + 2], lax.rem(128 + lane - 16 * b, 128), 1)
            for c in range(state_count):
                out[c, span, :] += speed * pltpu.roll(pack, (128 - c) % 128, 1)
            return carry

        lax.fori_loop(0, rows // 32, add_block, 0)

    each_side(add_side, -1)
    each_side(lambda index: side_copy(index, *flow).wait_send(), 1)
    each_side(lambda index: side_copy(index, *edges).wait_send(), 1)

    def finish(k):
        label_copy(k).wait_send()

        def chunk(j, carry):
            chunk_copy(k, j).wait_send()
            return carry

        lax.fori_loop(0, sent(k), chunk, 0)

    each_channel(finish, goes_out)
    gather_flag(1)
    end_flag(0)
    end_flag(1)
    any_over[...] = flags[2]


def exchange(nx, ny, caps, collective_id, picks, labels, over, old, velocity, weights):
    state_count, rows = old.shape[0], velocity.shape[1]
    cap = CHUNKS * CHUNK
    f32, vmem = jnp.float32, pltpu.VMEM
    in_vmem = pl.BlockSpec(memory_space=vmem)
    dma = pltpu.SemaphoreType.DMA
    return pl.pallas_call(
        functools.partial(exchange_kernel, nx, ny, caps),
        out_shape=(
            jax.ShapeDtypeStruct((state_count, rows, 128), f32),
            jax.ShapeDtypeStruct((1, 128), f32),
        ),
        in_specs=[pl.BlockSpec(memory_space=pltpu.SMEM)]
        + [in_vmem] * 4
        + [pl.BlockSpec(memory_space=pl.ANY)],
        out_specs=(in_vmem,) * 2,
        scratch_shapes=[
            vmem((state_count, rows, 128), f32),
            vmem((old.shape[1], 16, 128), f32),
            vmem(weights.shape, jnp.bfloat16),
            vmem((9, cap, state_count * 128), jnp.bfloat16),
            vmem((8, cap, state_count * 128), jnp.bfloat16),
            vmem((8, 1, 4 * WIDE), jnp.int32),
            vmem((16 * CHUNK, 128), f32),
            vmem((4, 32, 128), f32),
            vmem((4, 16, 128), f32),
            vmem((4, 32, 128), f32),
            vmem((4, 16, 128), f32),
            vmem((3, 1, 128), f32),
            vmem((nx + ny, 1, 128), f32),
            dma((4,)),
            dma((2, 8)),
            dma((8, cap // CHUNK)),
            dma((8, cap // CHUNK)),
            dma((2, 4)),
            dma((2, 4)),
            dma((2, nx + ny)),
        ],
        compiler_params=pltpu.CompilerParams(
            collective_id=collective_id, has_side_effects=True, vmem_limit_bytes=48 * MIB
        ),
        cost_estimate=pl.CostEstimate(
            flops=2 * 9 * cap * 128 * 128 * 16,
            bytes_accessed=weights.size * 2,
            transcendentals=0,
        ),
    )(picks, labels, over, old, velocity, weights)


def step_block(b, blocks, state, vel, flow_y, flow_x, out):
    rows, depth = state.shape[1], 32
    base = pl.multiple_of(b * depth, depth)
    span = pl.ds(base, depth)
    lane = lax.broadcasted_iota(jnp.int32, (depth, 128), 1)
    row = lax.broadcasted_iota(jnp.int32, (depth, 128), 0)
    left_pack = pltpu.roll(flow_y[2], lax.rem(128 - 16 * b, 128), 1)
    right_pack = pltpu.roll(flow_y[3], lax.rem(128 + 127 - 16 * b, 128), 1)

    def around(ref, c, halo):
        mid = ref[c, span, :]
        above = ref[c, pl.ds(jnp.maximum(base - 1, 0), 1), :]
        below = ref[c, pl.ds(jnp.minimum(base + depth, rows - 1), 1), :]
        if halo:
            first, last = flow_x[2, c : c + 1, :], flow_x[3, c : c + 1, :]
            shift = (128 - c) % 128
            left, right = pltpu.roll(left_pack, shift, 1), pltpu.roll(right_pack, shift, 1)
        else:
            first = last = left = right = 0.0
        above = jnp.where(b == 0, first, above)
        below = jnp.where(b == blocks - 1, last, below)
        before_x = jnp.where(row == 0, above, pltpu.roll(mid, 1, 0))
        after_x = jnp.where(row == depth - 1, below, pltpu.roll(mid, depth - 1, 0))
        before_y = jnp.where(lane == 0, left, pltpu.roll(mid, 1, 1))
        after_y = jnp.where(lane == 127, right, pltpu.roll(mid, 127, 1))
        return mid, before_x, after_x, before_y, after_y

    u_x, ux_bx, ux_ax, ux_by, ux_ay = around(vel, 0, True)
    u_y, uy_bx, uy_ax, uy_by, uy_ay = around(vel, 1, True)
    d_xx = 0.5 * (ux_ax - ux_bx)
    l_xy = 0.5 * (ux_ay - ux_by)
    l_yx = 0.5 * (uy_ax - uy_bx)
    d_yy = 0.5 * (uy_ay - uy_by)
    d_zz = -(d_xx + d_yy)
    d_xy = 0.5 * (l_xy + l_yx)
    spin = 0.5 * (l_xy - l_yx)
    plus_x, minus_x = jnp.maximum(u_x, 0.0), jnp.minimum(u_x, 0.0)
    plus_y, minus_y = jnp.maximum(u_y, 0.0), jnp.minimum(u_y, 0.0)
    shear = (2.0 * interaction) * jnp.sqrt(
        2.0 * (d_xx * d_xx + d_yy * d_yy + d_zz * d_zz + 2.0 * (d_xy * d_xy)) + 1.0
    )
    a_xx, a_yy, a_zz, a_xy, a_xz, a_yz = (state[c, span, :] for c in range(6))
    contraction = d_xx * a_xx + d_yy * a_yy + d_zz * a_zz + 2.0 * (d_xy * a_xy)
    fade = shape_factor * 2.0 * contraction + 3.0 * shear
    stress = 2.0 * shear_modulus
    pull = fiber_number * contraction
    sources = (
        2.0 * (spin * a_xy) + shape_factor * 2.0 * (d_xx * a_xx + d_xy * a_xy) - fade * a_xx + shear,
        -2.0 * (spin * a_xy) + shape_factor * 2.0 * (d_xy * a_xy + d_yy * a_yy) - fade * a_yy + shear,
        shape_factor * 2.0 * (d_zz * a_zz) - fade * a_zz + shear,
        spin * (a_yy - a_xx)
        + shape_factor * (d_xx * a_xy + d_xy * a_yy + a_xx * d_xy + a_xy * d_yy)
        - fade * a_xy,
        spin * a_yz + shape_factor * (d_xx * a_xz + d_xy * a_yz + a_xz * d_zz) - fade * a_xz,
        -spin * a_xz + shape_factor * (d_xy * a_xz + d_yy * a_yz + a_yz * d_zz) - fade * a_yz,
        d_xx,
        d_yy,
        d_xy,
        stress * (d_xx + pull * a_xx),
        stress * (d_yy + pull * a_yy),
        stress * (d_xy + pull * a_xy),
    )
    for c, source in enumerate(sources):
        mid, before_x, after_x, before_y, after_y = around(state, c, False)
        upwind = (
            plus_x * (mid - before_x)
            + minus_x * (after_x - mid)
            + plus_y * (mid - before_y)
            + minus_y * (after_y - mid)
        )
        out[c, span, :] = mid + time_step * (source - upwind)


def per_device(
    nx,
    ny,
    old_states,
    weight_tiles,
    source_block,
    tile_index,
    dest_device,
    dest_block,
    send_count,
    velocity,
):
    lists = (send_count, source_block, tile_index, dest_device, dest_block)
    old = jnp.transpose(old_states, (1, 0, 2))
    places = plan(nx, ny, USUAL, lists)
    states, any_over = exchange(nx, ny, USUAL, 0, *places, old, velocity, weight_tiles)

    def again(_):
        return exchange(nx, ny, FULL, 1, *places, old, velocity, weight_tiles)[0]

    states = lax.cond(any_over[0, 0] > 0, again, lambda enough: enough, states)
    return jnp.transpose(states, (1, 0, 2))


def solution(mesh):
    in_specs = (
        P(("gx", "gy"), None, None),
        P(("gx", "gy"), None, None),
        P(("gx", "gy")),
        P(("gx", "gy")),
        P(("gx", "gy")),
        P(("gx", "gy")),
        P(("gx", "gy")),
        P(None, "gx", "gy"),
    )
    out_specs = P("gx", None, "gy")
    return jax.shard_map(
        functools.partial(per_device, mesh.shape["gx"], mesh.shape["gy"]),
        mesh=mesh,
        in_specs=in_specs,
        out_specs=out_specs,
        check_vma=False,
    )
```

```python
import functools

import jax
import jax.numpy as jnp
from jax import lax
from jax.experimental import pallas as pl
from jax.experimental.pallas import tpu as pltpu
from jax.sharding import PartitionSpec as P

time_step = 0.2
shape_factor = 0.95
interaction = 0.01
shear_modulus = 1.0
fiber_number = 2.0

MESH = pl.DeviceIdType.MESH
CHUNK = 32
WIDE = 128
FIRST = 3
CHUNKS = 6
USUAL = (3, 4, 5, 6)
FULL = (6, 6, 6, 6)
MIB = 1 << 20


STEPS = ((-1, 1), (-1, -1), (1, 1), (1, -1), (0, 1), (0, -1), (-1, 0), (1, 0), (0, 0))


def step_of(k):
    m = k // 2
    dx = jnp.where(k < 6, jnp.where(m == 2, 0, 2 * m - 1), 2 * (k - 6) - 1)
    dy = jnp.where(k < 6, 1 - 2 * (k % 2), 0)
    return dx, dy


def exists(x, y, nx, ny):
    return (x >= 0) & (x < nx) & (y >= 0) & (y < ny)


def neighbours_of(x, y, nx, ny):
    spread_x = 3 - (x == 0).astype(jnp.int32) - (x == nx - 1).astype(jnp.int32)
    spread_y = 3 - (y == 0).astype(jnp.int32) - (y == ny - 1).astype(jnp.int32)
    return spread_x * spread_y - 1


def chunks_of(x, y, dy, nx, ny, caps):
    n = neighbours_of(x, y, nx, ny)
    inner, along, edge, corner = caps
    sidewise = jnp.where((dy != 0) & ((y == 0) | (y == ny - 1)), along, edge)
    return jnp.where(n >= 8, inner, jnp.where(n >= 5, sidewise, corner))


def plan_kernel(
    nx,
    ny,
    caps,
    send_count,
    source_block,
    tile_index,
    dest_device,
    dest_block,
    picks,
    labels,
    over_flag,
):
    gx, gy = lax.axis_index("gx"), lax.axis_index("gy")

    slots = source_block.shape[0]
    dest, tile = dest_device[...].reshape(1, slots), tile_index[...].reshape(1, slots)
    ids = lax.broadcasted_iota(jnp.int32, (1, slots), 1)
    place_shift = ny.bit_length() - 1
    step_x = (dest >> place_shift) - gx
    step_y = (dest & (ny - 1)) - gy
    channel_of = jnp.full((1, slots), 15, jnp.int32)
    for k, (dx, dy) in enumerate(STEPS):
        channel_of = jnp.where((step_x == dx) & (step_y == dy), k, channel_of)
    channel_of = jnp.where(ids < send_count[0], channel_of, 15)
    matches = channel_of == lax.broadcasted_iota(jnp.int32, (16, slots), 0)
    matches = matches & (lax.broadcasted_iota(jnp.int32, (16, slots), 0) < 9)
    ones = jnp.where(matches, 1.0, 0.0)
    counts = jnp.sum(ones, axis=1, keepdims=True)
    over = jnp.zeros((1, 1), jnp.float32)
    for k, (_, dy) in enumerate(STEPS[:8]):
        allowed = (chunks_of(gx, gy, dy, nx, ny, caps) * CHUNK).astype(jnp.float32)
        over = jnp.maximum(over, jnp.where(counts[k : k + 1] > allowed, 1.0, 0.0))
    over_flag[...] = jnp.broadcast_to(over, over_flag.shape)
    before = lax.broadcasted_iota(jnp.int32, (slots, slots), 0) < lax.broadcasted_iota(
        jnp.int32, (slots, slots), 1
    )
    earlier = jnp.dot(
        ones.astype(jnp.bfloat16),
        jnp.where(before, 1.0, 0.0).astype(jnp.bfloat16),
        preferred_element_type=jnp.float32,
    )
    position = jnp.sum(ones * earlier, axis=0, keepdims=True).astype(jnp.int32)
    place = lax.broadcasted_iota(jnp.int32, (4 * WIDE, slots), 0)
    place = jnp.where(
        place < WIDE,
        jnp.where(place < FIRST * CHUNK, place, -1),
        jnp.where(place % WIDE < CHUNK, place % WIDE + (place // WIDE + FIRST - 1) * CHUNK, -1),
    )
    at_place = jnp.where(place == position, 1.0, 0.0).astype(jnp.bfloat16)
    source, row = source_block[...].reshape(1, slots), dest_block[...].reshape(1, slots)
    parcels = [source, tile >> 1, tile & 1, row + 1]
    parcels = [(ones * v.astype(jnp.float32)).astype(jnp.bfloat16) for v in parcels]
    ordered = lax.dot_general(
        jnp.concatenate(parcels, axis=0),
        at_place,
        (((1,), (1,)), ((), ())),
        preferred_element_type=jnp.float32,
    )
    picks[...] = (
        (2.0 * ordered[16:32] + ordered[32:48]) * 128.0 + ordered[0:16]
    ).astype(jnp.int32)
    label_rows = ordered[48:64].astype(jnp.int32) - 1
    for k in range(9):
        labels[k] = label_rows[k : k + 1]


def plan(nx, ny, caps, lists):
    in_vmem = pl.BlockSpec(memory_space=pltpu.VMEM)
    return pl.pallas_call(
        functools.partial(plan_kernel, nx, ny, caps),
        out_shape=(
            jax.ShapeDtypeStruct((16, 4 * WIDE), jnp.int32),
            jax.ShapeDtypeStruct((9, 1, 4 * WIDE), jnp.int32),
            jax.ShapeDtypeStruct((1, 128), jnp.float32),
        ),
        in_specs=[pl.BlockSpec(memory_space=pltpu.SMEM)] + [in_vmem] * 4,
        out_specs=(in_vmem,) * 3,
    )(*lists)


def exchange_kernel(
    nx,
    ny,
    caps,
    picks,
    labels,
    over,
    old,
    vel,
    weights,
    out,
    any_over,
    remapped,
    blocks,
    tiles,
    outgoing,
    incoming,
    incoming_labels,
    turn,
    edge_y,
    edge_x,
    flow_y,
    flow_x,
    flags,
    flags_in,
    load_sem,
    label_sems,
    send_sems,
    recv_sems,
    edge_sems,
    flow_sems,
    flag_sems,
):
    gx, gy = lax.axis_index("gx"), lax.axis_index("gy")
    parts = load_sem.shape[0]
    depth = tiles.shape[0] // parts
    cap = outgoing.shape[1]
    state_count, rows = remapped.shape[:2]

    for part in range(parts):
        span = pl.ds(part * depth, depth)
        pltpu.make_async_copy(weights.at[span], tiles.at[span], load_sem.at[part]).start()

    barrier = pltpu.get_barrier_semaphore()
    for k in range(8):
        dx, dy = step_of(k)

        @pl.when(exists(gx + dx, gy + dy, nx, ny))
        def _():
            pl.semaphore_signal(
                barrier, inc=1, device_id=(gx + dx, gy + dy), device_id_type=MESH
            )


    def along_gx(j):
        return (lax.rem(gx + j, nx), gy)

    def along_gy(j):
        return (gx, lax.rem(gy + j, ny))

    def greet(j, carry, along):
        pl.semaphore_signal(barrier, inc=1, device_id=along(j), device_id_type=MESH)
        return carry

    lax.fori_loop(1, nx, functools.partial(greet, along=along_gx), 0)
    lax.fori_loop(1, ny, functools.partial(greet, along=along_gy), 0)
    pl.semaphore_wait(barrier, neighbours_of(gx, gy, nx, ny) + nx + ny - 2)

    def flag_copy(turn_of, j):
        slot = turn_of * nx + j
        return pltpu.make_async_remote_copy(
            src_ref=flags.at[turn_of],
            dst_ref=flags_in.at[slot],
            send_sem=flag_sems.at[0, slot],
            recv_sem=flag_sems.at[1, slot],
            device_id=(along_gx, along_gy)[turn_of](j),
            device_id_type=MESH,
        )

    def send_flag(turn_of):
        def step(j, carry):
            flag_copy(turn_of, j).start()
            return carry

        lax.fori_loop(1, (nx, ny)[turn_of], step, 0)

    def gather_flag(turn_of):
        def step(j, carry):
            flag_copy(turn_of, j).wait_recv()
            return jnp.maximum(carry, flags_in[turn_of * nx + j])

        flags[turn_of + 1] = lax.fori_loop(1, (nx, ny)[turn_of], step, flags[turn_of])

    def end_flag(turn_of):
        def step(j, carry):
            flag_copy(turn_of, j).wait_send()
            return carry

        lax.fori_loop(1, (nx, ny)[turn_of], step, 0)

    flags[0] = over[...]
    send_flag(0)

    def label_copy(k):
        dx, dy = step_of(k)
        return pltpu.make_async_remote_copy(
            src_ref=labels.at[k],
            dst_ref=incoming_labels.at[k],
            send_sem=label_sems.at[0, k],
            recv_sem=label_sems.at[1, k],
            device_id=(gx + dx, gy + dy),
            device_id_type=MESH,
        )

    def chunk_copy(k, j):
        dx, dy = step_of(k)
        span = pl.ds(j * CHUNK, CHUNK)
        return pltpu.make_async_remote_copy(
            src_ref=outgoing.at[k, span],
            dst_ref=incoming.at[k, span],
            send_sem=send_sems.at[k, j],
            recv_sem=recv_sems.at[k, j],
            device_id=(gx + dx, gy + dy),
            device_id_type=MESH,
        )

    def goes_out(k):
        dx, dy = step_of(k)
        return exists(gx + dx, gy + dy, nx, ny)

    def comes_in(k):
        dx, dy = step_of(k)
        return exists(gx - dx, gy - dy, nx, ny)

    def each_channel(body, predicate):
        def step(k, carry):
            @pl.when(predicate(k))
            def _():
                body(k)

            return carry

        lax.fori_loop(0, 8, step, 0)

    each_channel(lambda k: label_copy(k).start(), goes_out)

    lanes = lax.broadcasted_iota(jnp.int32, (32, 128), 1)
    sides = ((0, 0, 1), (1, 0, -1), (0, 1, 0), (1, -1, 0))

    def pack_edges(ref, along_y, along_x):
        planes = ref.shape[0]
        for h in range(rows // 128):
            packed = jnp.zeros((32, 128), jnp.float32)
            for q in range(4):
                for c in range(planes):
                    to = 32 * q + 2 * c
                    moved = pltpu.roll(ref[c, pl.ds(128 * h + 32 * q, 32), :], to + 1, 1)
                    packed = jnp.where((lanes >> 1) == (to >> 1), moved, packed)
            along_y[0, h] = packed
        for side, row in ((0, rows - 1), (1, 0)):
            for c in range(planes):
                along_x[side, c : c + 1, :] = ref[c, row : row + 1, :]

    def side_copy(index, along_y, along_x, sems):
        side, dx, dy = sides[index]
        edge = along_y if dx == 0 else along_x
        return pltpu.make_async_remote_copy(
            src_ref=edge.at[0 if dx == 0 else side],
            dst_ref=edge.at[side + 1 if dx == 0 else side + 2],
            send_sem=sems.at[0, index],
            recv_sem=sems.at[1, index],
            device_id=(gx + dx, gy + dy),
            device_id_type=MESH,
        )

    def each_side(body, sign):
        for index, (_, dx, dy) in enumerate(sides):

            @pl.when(exists(gx + sign * dx, gy + sign * dy, nx, ny))
            def _():
                body(index)

    flow = (flow_y, flow_x, flow_sems)
    edges = (edge_y, edge_x, edge_sems)
    pack_edges(vel, flow_y, flow_x)
    each_side(lambda index: side_copy(index, *flow).start(), 1)

    blocks[...] = jnp.zeros_like(blocks)
    for c in range(state_count):
        blocks[:, c, :] = old[c].astype(jnp.float32)
    for part in range(parts):
        span = pl.ds(part * depth, depth)
        pltpu.make_async_copy(weights.at[span], tiles.at[span], load_sem.at[part]).wait()

    def compute_chunk(k, j):
        at = jnp.where(j < FIRST, j * CHUNK, (j - FIRST + 1) * WIDE)
        none = jnp.zeros((16, 128), jnp.bfloat16)
        join = jnp.concatenate
        for i in range(0, CHUNK, 4):
            four = [picks[k, at + i + n] for n in range(4)]
            a = [blocks[p & 127].astype(jnp.bfloat16) for p in four]
            w = [tiles[p >> 7] for p in four]
            left = join([join([a[n], none] if n % 2 == 0 else [none, a[n]], 1) for n in range(4)], 0)
            right = join([join([w[0], w[1]], 1), join([w[2], w[3]], 1)], 0)
            piece = lax.dot_general(
                left, right, (((1,), (1,)), ((), ())), preferred_element_type=jnp.float32
            )
            turn[pl.ds(16 * i, 32), :] = piece[:32, :128]
            turn[pl.ds(16 * i + 32, 32), :] = piece[32:, 128:]
        for group in range(CHUNK // 16):
            for c in range(state_count):
                turned = turn[pl.ds(256 * group + c, 16, stride=16), :]
                outgoing[
                    k,
                    pl.ds(pl.multiple_of(j * CHUNK + 16 * group, 16), 16),
                    pl.ds(c * 128, 128),
                ] = turned.astype(jnp.bfloat16)

    def sent(k):
        _, dy = step_of(k)
        return chunks_of(gx, gy, dy, nx, ny, caps)

    def channel(k, carry):
        def chunk(j, carry):
            compute_chunk(k, j)

            @pl.when(k < 8)
            def _():
                chunk_copy(k, j).start()

            return carry

        @pl.when((k == 8) | goes_out(k))
        def _():
            lax.fori_loop(0, jnp.where(k == 8, CHUNKS, sent(k)), chunk, 0)

        @pl.when(k == 1)
        def _():
            gather_flag(0)
            send_flag(1)

        return carry

    lax.fori_loop(0, 9, channel, 0)

    row_ids = lax.broadcasted_iota(jnp.int32, (rows, WIDE), 0)

    def add(label_row, values, first):
        width = values.shape[0]
        selector = jnp.where(row_ids == label_row, 1.0, 0.0).astype(jnp.bfloat16)[:, :width]
        for c in range(0, state_count, 2):
            summed = jnp.dot(
                selector,
                values[:, c * 128 : (c + 2) * 128],
                preferred_element_type=jnp.float32,
            )
            if first:
                remapped[c] = summed[:, :128]
                remapped[c + 1] = summed[:, 128:]
            else:
                remapped[c] += summed[:, :128]
                remapped[c + 1] += summed[:, 128:]

    def add_piece(label_rows, k, values, first):
        add(label_rows[k, :, :WIDE], values[k, : FIRST * CHUNK], first)

    def add_chunk(label_rows, k, values, j):
        lanes_of = slice((j - FIRST + 1) * WIDE, (j - FIRST + 2) * WIDE)
        add(label_rows[k, :, lanes_of], values[k, j * CHUNK : (j + 1) * CHUNK], False)

    add_piece(labels, 8, outgoing, True)
    for j in range(FIRST, CHUNKS):
        add_chunk(labels, 8, outgoing, j)

    def accept(k):
        dx, dy = step_of(k)
        arriving = chunks_of(gx - dx, gy - dy, dy, nx, ny, caps)
        label_copy(k).wait_recv()
        for j in range(FIRST):
            chunk_copy(k, j).wait_recv()
        add_piece(incoming_labels, k, incoming, False)
        for j in range(FIRST, CHUNKS):

            @pl.when(arriving > j)
            def _():
                chunk_copy(k, j).wait_recv()
                add_chunk(incoming_labels, k, incoming, j)

    def accept_in_turn(i, carry):
        k = lax.rem(i + 6, 8)

        @pl.when(comes_in(k))
        def _():
            accept(k)

        return carry

    lax.fori_loop(0, 8, accept_in_turn, 0)

    pack_edges(remapped, edge_y, edge_x)
    each_side(lambda index: side_copy(index, *edges).start(), 1)

    def land(along_y, along_x, sems):
        for index, (side, dx, dy) in enumerate(sides):
            edge, slot = (along_y, side + 1) if dx == 0 else (along_x, side + 2)
            there = exists(gx - dx, gy - dy, nx, ny)

            @pl.when(there)
            def _():
                side_copy(index, along_y, along_x, sems).wait_recv()

            @pl.when(jnp.logical_not(there))
            def _():
                edge[slot] = jnp.zeros(edge.shape[1:], jnp.float32)

    land(*flow)

    def step(b, carry):
        step_block(b, rows // 32, remapped, vel, flow_y, flow_x, out)
        return carry

    lax.fori_loop(0, rows // 32, step, 0)

    land(*edges)
    for side, row in ((0, 0), (1, rows - 1)):
        bound, scale = (jnp.maximum, time_step) if side == 0 else (jnp.minimum, -time_step)
        speed = scale * bound(vel[0, row : row + 1, :], 0.0)
        for c in range(state_count):
            out[c, row : row + 1, :] += speed * edge_x[side + 2, c : c + 1, :]

    each_side(lambda index: side_copy(index, *edges).wait_send(), 1)
    for h in range(rows // 128):
        moved = pltpu.roll(edge_y[1, h], 2, 1)
        edge_y[0, h] = jnp.where((lanes & 1) == 0, moved, edge_y[2, h])

    def add_block(b, carry):
        span = pl.ds(pl.multiple_of(32 * b, 32), 32)
        flow_here = vel[1, span, :]
        speed = jnp.where(
            lanes == 0,
            time_step * jnp.maximum(flow_here, 0.0),
            jnp.where(lanes == 127, -time_step * jnp.minimum(flow_here, 0.0), 0.0),
        )
        pack = pltpu.roll(edge_y[0, b // 4], lax.rem(128 + 126 - 32 * lax.rem(b, 4), 128), 1)
        for c in range(state_count):
            out[c, span, :] += speed * pltpu.roll(pack, (128 - 2 * c) % 128, 1)
        return carry

    lax.fori_loop(0, rows // 32, add_block, 0)
    each_side(lambda index: side_copy(index, *flow).wait_send(), 1)

    def finish(k):
        label_copy(k).wait_send()

        def chunk(j, carry):
            chunk_copy(k, j).wait_send()
            return carry

        lax.fori_loop(0, sent(k), chunk, 0)

    each_channel(finish, goes_out)
    gather_flag(1)
    end_flag(0)
    end_flag(1)
    any_over[...] = flags[2]


def exchange(nx, ny, caps, collective_id, picks, labels, over, old, velocity, weights):
    state_count, rows = old.shape[0], velocity.shape[1]
    cap = CHUNKS * CHUNK
    f32, vmem = jnp.float32, pltpu.VMEM
    in_vmem = pl.BlockSpec(memory_space=vmem)
    dma = pltpu.SemaphoreType.DMA
    return pl.pallas_call(
        functools.partial(exchange_kernel, nx, ny, caps),
        out_shape=(
            jax.ShapeDtypeStruct((state_count, rows, 128), f32),
            jax.ShapeDtypeStruct((1, 128), f32),
        ),
        in_specs=[pl.BlockSpec(memory_space=pltpu.SMEM)]
        + [in_vmem] * 4
        + [pl.BlockSpec(memory_space=pl.ANY)],
        out_specs=(in_vmem,) * 2,
        scratch_shapes=[
            vmem((state_count, rows, 128), f32),
            vmem((old.shape[1], 16, 128), f32),
            vmem(weights.shape, jnp.bfloat16),
            vmem((9, cap, state_count * 128), jnp.bfloat16),
            vmem((8, cap, state_count * 128), jnp.bfloat16),
            vmem((8, 1, 4 * WIDE), jnp.int32),
            vmem((16 * CHUNK, 128), f32),
            vmem((3, rows // 128, 32, 128), f32),
            vmem((4, 16, 128), f32),
            vmem((3, rows // 128, 32, 128), f32),
            vmem((4, 16, 128), f32),
            vmem((3, 1, 128), f32),
            vmem((nx + ny, 1, 128), f32),
            dma((4,)),
            dma((2, 8)),
            dma((8, cap // CHUNK)),
            dma((8, cap // CHUNK)),
            dma((2, 4)),
            dma((2, 4)),
            dma((2, nx + ny)),
        ],
        compiler_params=pltpu.CompilerParams(
            collective_id=collective_id, has_side_effects=True, vmem_limit_bytes=48 * MIB
        ),
        cost_estimate=pl.CostEstimate(
            flops=2 * 9 * cap * 128 * 128 * 16,
            bytes_accessed=weights.size * 2,
            transcendentals=0,
        ),
    )(picks, labels, over, old, velocity, weights)


def step_block(b, blocks, state, vel, flow_y, flow_x, out):
    rows, depth = state.shape[1], 32
    base = pl.multiple_of(b * depth, depth)
    span = pl.ds(base, depth)
    lane = lax.broadcasted_iota(jnp.int32, (depth, 128), 1)
    row = lax.broadcasted_iota(jnp.int32, (depth, 128), 0)
    quarter = 32 * lax.rem(b, 4)
    left_pack = pltpu.roll(flow_y[1, b // 4], lax.rem(128 - quarter, 128), 1)
    right_pack = pltpu.roll(flow_y[2, b // 4], lax.rem(128 + 126 - quarter, 128), 1)

    def around(ref, c, halo):
        mid = ref[c, span, :]
        above = ref[c, pl.ds(jnp.maximum(base - 1, 0), 1), :]
        below = ref[c, pl.ds(jnp.minimum(base + depth, rows - 1), 1), :]
        if halo:
            first, last = flow_x[2, c : c + 1, :], flow_x[3, c : c + 1, :]
            shift = (128 - 2 * c) % 128
            left, right = pltpu.roll(left_pack, shift, 1), pltpu.roll(right_pack, shift, 1)
        else:
            first = last = left = right = 0.0
        above = jnp.where(b == 0, first, above)
        below = jnp.where(b == blocks - 1, last, below)
        before_x = jnp.where(row == 0, above, pltpu.roll(mid, 1, 0))
        after_x = jnp.where(row == depth - 1, below, pltpu.roll(mid, depth - 1, 0))
        before_y = jnp.where(lane == 0, left, pltpu.roll(mid, 1, 1))
        after_y = jnp.where(lane == 127, right, pltpu.roll(mid, 127, 1))
        return mid, before_x, after_x, before_y, after_y

    u_x, ux_bx, ux_ax, ux_by, ux_ay = around(vel, 0, True)
    u_y, uy_bx, uy_ax, uy_by, uy_ay = around(vel, 1, True)
    d_xx = 0.5 * (ux_ax - ux_bx)
    l_xy = 0.5 * (ux_ay - ux_by)
    l_yx = 0.5 * (uy_ax - uy_bx)
    d_yy = 0.5 * (uy_ay - uy_by)
    d_zz = -(d_xx + d_yy)
    d_xy = 0.5 * (l_xy + l_yx)
    spin = 0.5 * (l_xy - l_yx)
    plus_x, minus_x = jnp.maximum(u_x, 0.0), jnp.minimum(u_x, 0.0)
    plus_y, minus_y = jnp.maximum(u_y, 0.0), jnp.minimum(u_y, 0.0)
    shear = (2.0 * interaction) * jnp.sqrt(
        2.0 * (d_xx * d_xx + d_yy * d_yy + d_zz * d_zz + 2.0 * (d_xy * d_xy)) + 1.0
    )
    a_xx, a_yy, a_zz, a_xy, a_xz, a_yz = (state[c, span, :] for c in range(6))
    contraction = d_xx * a_xx + d_yy * a_yy + d_zz * a_zz + 2.0 * (d_xy * a_xy)
    fade = shape_factor * 2.0 * contraction + 3.0 * shear
    stress = 2.0 * shear_modulus
    pull = fiber_number * contraction
    sources = (
        2.0 * (spin * a_xy) + shape_factor * 2.0 * (d_xx * a_xx + d_xy * a_xy) - fade * a_xx + shear,
        -2.0 * (spin * a_xy) + shape_factor * 2.0 * (d_xy * a_xy + d_yy * a_yy) - fade * a_yy + shear,
        shape_factor * 2.0 * (d_zz * a_zz) - fade * a_zz + shear,
        spin * (a_yy - a_xx)
        + shape_factor * (d_xx * a_xy + d_xy * a_yy + a_xx * d_xy + a_xy * d_yy)
        - fade * a_xy,
        spin * a_yz + shape_factor * (d_xx * a_xz + d_xy * a_yz + a_xz * d_zz) - fade * a_xz,
        -spin * a_xz + shape_factor * (d_xy * a_xz + d_yy * a_yz + a_yz * d_zz) - fade * a_yz,
        d_xx,
        d_yy,
        d_xy,
        stress * (d_xx + pull * a_xx),
        stress * (d_yy + pull * a_yy),
        stress * (d_xy + pull * a_xy),
    )
    for c, source in enumerate(sources):
        mid, before_x, after_x, before_y, after_y = around(state, c, False)
        upwind = (
            plus_x * (mid - before_x)
            + minus_x * (after_x - mid)
            + plus_y * (mid - before_y)
            + minus_y * (after_y - mid)
        )
        out[c, span, :] = mid + time_step * (source - upwind)


def per_device(
    nx,
    ny,
    old_states,
    weight_tiles,
    source_block,
    tile_index,
    dest_device,
    dest_block,
    send_count,
    velocity,
):
    lists = (send_count, source_block, tile_index, dest_device, dest_block)
    old = jnp.transpose(old_states, (1, 0, 2))
    places = plan(nx, ny, USUAL, lists)
    states, any_over = exchange(nx, ny, USUAL, 0, *places, old, velocity, weight_tiles)

    def again(_):
        return exchange(nx, ny, FULL, 1, *places, old, velocity, weight_tiles)[0]

    states = lax.cond(any_over[0, 0] > 0, again, lambda enough: enough, states)
    return jnp.transpose(states, (1, 0, 2))


def solution(mesh):
    in_specs = (
        P(("gx", "gy"), None, None),
        P(("gx", "gy"), None, None),
        P(("gx", "gy")),
        P(("gx", "gy")),
        P(("gx", "gy")),
        P(("gx", "gy")),
        P(("gx", "gy")),
        P(None, "gx", "gy"),
    )
    out_specs = P("gx", None, "gy")
    return jax.shard_map(
        functools.partial(per_device, mesh.shape["gx"], mesh.shape["gy"]),
        mesh=mesh,
        in_specs=in_specs,
        out_specs=out_specs,
        check_vma=False,
    )
```

```python
import functools

import jax
import jax.numpy as jnp
from jax import lax
from jax.experimental import pallas as pl
from jax.experimental.pallas import tpu as pltpu
from jax.sharding import PartitionSpec as P

time_step = 0.2
shape_factor = 0.95
interaction = 0.01
shear_modulus = 1.0
fiber_number = 2.0

MESH = pl.DeviceIdType.MESH
CHUNK = 32
WIDE = 128
FIRST = 3
CHUNKS = 6
USUAL = (3, 4, 5, 6)
FULL = (6, 6, 6, 6)
MIB = 1 << 20


STEPS = ((-1, 1), (-1, -1), (1, 1), (1, -1), (0, 1), (0, -1), (-1, 0), (1, 0), (0, 0))


def step_of(k):
    m = k // 2
    dx = jnp.where(k < 6, jnp.where(m == 2, 0, 2 * m - 1), 2 * (k - 6) - 1)
    dy = jnp.where(k < 6, 1 - 2 * (k % 2), 0)
    return dx, dy


def exists(x, y, nx, ny):
    return (x >= 0) & (x < nx) & (y >= 0) & (y < ny)


def neighbours_of(x, y, nx, ny):
    spread_x = 3 - (x == 0).astype(jnp.int32) - (x == nx - 1).astype(jnp.int32)
    spread_y = 3 - (y == 0).astype(jnp.int32) - (y == ny - 1).astype(jnp.int32)
    return spread_x * spread_y - 1


def chunks_of(x, y, dy, nx, ny, caps):
    n = neighbours_of(x, y, nx, ny)
    inner, along, edge, corner = caps
    sidewise = jnp.where((dy != 0) & ((y == 0) | (y == ny - 1)), along, edge)
    return jnp.where(n >= 8, inner, jnp.where(n >= 5, sidewise, corner))


def plan_kernel(
    nx,
    ny,
    caps,
    send_count,
    source_block,
    tile_index,
    dest_device,
    dest_block,
    picks,
    labels,
    over_flag,
):
    gx, gy = lax.axis_index("gx"), lax.axis_index("gy")

    slots = source_block.shape[0]
    dest, tile = dest_device[...].reshape(1, slots), tile_index[...].reshape(1, slots)
    ids = lax.broadcasted_iota(jnp.int32, (1, slots), 1)
    place_shift = ny.bit_length() - 1
    step_x = (dest >> place_shift) - gx
    step_y = (dest & (ny - 1)) - gy
    channel_of = jnp.full((1, slots), 15, jnp.int32)
    for k, (dx, dy) in enumerate(STEPS):
        channel_of = jnp.where((step_x == dx) & (step_y == dy), k, channel_of)
    channel_of = jnp.where(ids < send_count[0], channel_of, 15)
    matches = channel_of == lax.broadcasted_iota(jnp.int32, (16, slots), 0)
    matches = matches & (lax.broadcasted_iota(jnp.int32, (16, slots), 0) < 9)
    ones = jnp.where(matches, 1.0, 0.0)
    counts = jnp.sum(ones, axis=1, keepdims=True)
    over = jnp.zeros((1, 1), jnp.float32)
    for k, (_, dy) in enumerate(STEPS[:8]):
        allowed = (chunks_of(gx, gy, dy, nx, ny, caps) * CHUNK).astype(jnp.float32)
        over = jnp.maximum(over, jnp.where(counts[k : k + 1] > allowed, 1.0, 0.0))
    over_flag[...] = jnp.broadcast_to(over, over_flag.shape)
    before = lax.broadcasted_iota(jnp.int32, (slots, slots), 0) < lax.broadcasted_iota(
        jnp.int32, (slots, slots), 1
    )
    earlier = jnp.dot(
        ones.astype(jnp.bfloat16),
        jnp.where(before, 1.0, 0.0).astype(jnp.bfloat16),
        preferred_element_type=jnp.float32,
    )
    position = jnp.sum(ones * earlier, axis=0, keepdims=True).astype(jnp.int32)
    place = lax.broadcasted_iota(jnp.int32, (4 * WIDE, slots), 0)
    place = jnp.where(
        place < WIDE,
        jnp.where(place < FIRST * CHUNK, place, -1),
        jnp.where(place % WIDE < CHUNK, place % WIDE + (place // WIDE + FIRST - 1) * CHUNK, -1),
    )
    at_place = jnp.where(place == position, 1.0, 0.0).astype(jnp.bfloat16)
    source, row = source_block[...].reshape(1, slots), dest_block[...].reshape(1, slots)
    parcels = [source, tile >> 1, tile & 1, row + 1]
    parcels = [(ones * v.astype(jnp.float32)).astype(jnp.bfloat16) for v in parcels]
    ordered = lax.dot_general(
        jnp.concatenate(parcels, axis=0),
        at_place,
        (((1,), (1,)), ((), ())),
        preferred_element_type=jnp.float32,
    )
    picks[...] = (
        (2.0 * ordered[16:32] + ordered[32:48]) * 128.0 + ordered[0:16]
    ).astype(jnp.int32)
    label_rows = ordered[48:64].astype(jnp.int32) - 1
    for k in range(9):
        labels[k] = label_rows[k : k + 1]


def plan(nx, ny, caps, lists):
    in_vmem = pl.BlockSpec(memory_space=pltpu.VMEM)
    return pl.pallas_call(
        functools.partial(plan_kernel, nx, ny, caps),
        out_shape=(
            jax.ShapeDtypeStruct((16, 4 * WIDE), jnp.int32),
            jax.ShapeDtypeStruct((9, 1, 4 * WIDE), jnp.int32),
            jax.ShapeDtypeStruct((1, 128), jnp.float32),
        ),
        in_specs=[pl.BlockSpec(memory_space=pltpu.SMEM)] + [in_vmem] * 4,
        out_specs=(in_vmem,) * 3,
    )(*lists)


def exchange_kernel(
    nx,
    ny,
    caps,
    picks,
    labels,
    over,
    old,
    vel,
    weights,
    out,
    any_over,
    remapped,
    blocks,
    tiles,
    outgoing,
    incoming,
    incoming_labels,
    turn,
    edge_y,
    edge_x,
    flow_y,
    flow_x,
    flags,
    flags_in,
    load_sem,
    label_sems,
    send_sems,
    recv_sems,
    edge_sems,
    flow_sems,
    flag_sems,
):
    gx, gy = lax.axis_index("gx"), lax.axis_index("gy")
    parts = load_sem.shape[0]
    depth = tiles.shape[0] // parts
    cap = outgoing.shape[1]
    state_count, rows = remapped.shape[:2]

    for part in range(parts):
        span = pl.ds(part * depth, depth)
        pltpu.make_async_copy(weights.at[span], tiles.at[span], load_sem.at[part]).start()

    barrier = pltpu.get_barrier_semaphore()
    for k in range(8):
        dx, dy = step_of(k)

        @pl.when(exists(gx + dx, gy + dy, nx, ny))
        def _():
            pl.semaphore_signal(
                barrier, inc=1, device_id=(gx + dx, gy + dy), device_id_type=MESH
            )


    def along_gx(j):
        return (lax.rem(gx + j, nx), gy)

    def along_gy(j):
        return (gx, lax.rem(gy + j, ny))

    def greet(j, carry, along):
        pl.semaphore_signal(barrier, inc=1, device_id=along(j), device_id_type=MESH)
        return carry

    lax.fori_loop(1, nx, functools.partial(greet, along=along_gx), 0)
    lax.fori_loop(1, ny, functools.partial(greet, along=along_gy), 0)
    pl.semaphore_wait(barrier, neighbours_of(gx, gy, nx, ny) + nx + ny - 2)

    def flag_copy(turn_of, j):
        slot = turn_of * nx + j
        return pltpu.make_async_remote_copy(
            src_ref=flags.at[turn_of],
            dst_ref=flags_in.at[slot],
            send_sem=flag_sems.at[0, slot],
            recv_sem=flag_sems.at[1, slot],
            device_id=(along_gx, along_gy)[turn_of](j),
            device_id_type=MESH,
        )

    def send_flag(turn_of):
        def step(j, carry):
            flag_copy(turn_of, j).start()
            return carry

        lax.fori_loop(1, (nx, ny)[turn_of], step, 0)

    def gather_flag(turn_of):
        def step(j, carry):
            flag_copy(turn_of, j).wait_recv()
            return jnp.maximum(carry, flags_in[turn_of * nx + j])

        flags[turn_of + 1] = lax.fori_loop(1, (nx, ny)[turn_of], step, flags[turn_of])

    def end_flag(turn_of):
        def step(j, carry):
            flag_copy(turn_of, j).wait_send()
            return carry

        lax.fori_loop(1, (nx, ny)[turn_of], step, 0)

    flags[0] = over[...]
    send_flag(0)

    def label_copy(k):
        dx, dy = step_of(k)
        return pltpu.make_async_remote_copy(
            src_ref=labels.at[k],
            dst_ref=incoming_labels.at[k],
            send_sem=label_sems.at[0, k],
            recv_sem=label_sems.at[1, k],
            device_id=(gx + dx, gy + dy),
            device_id_type=MESH,
        )

    def chunk_copy(k, j):
        dx, dy = step_of(k)
        span = pl.ds(j * CHUNK, CHUNK)
        return pltpu.make_async_remote_copy(
            src_ref=outgoing.at[k, span],
            dst_ref=incoming.at[k, span],
            send_sem=send_sems.at[k, j],
            recv_sem=recv_sems.at[k, j],
            device_id=(gx + dx, gy + dy),
            device_id_type=MESH,
        )

    def goes_out(k):
        dx, dy = step_of(k)
        return exists(gx + dx, gy + dy, nx, ny)

    def comes_in(k):
        dx, dy = step_of(k)
        return exists(gx - dx, gy - dy, nx, ny)

    def each_channel(body, predicate):
        def step(k, carry):
            @pl.when(predicate(k))
            def _():
                body(k)

            return carry

        lax.fori_loop(0, 8, step, 0)

    lanes = lax.broadcasted_iota(jnp.int32, (32, 128), 1)
    sides = ((0, 0, 1), (1, 0, -1), (0, 1, 0), (1, -1, 0))

    def pack_edges(ref, along_y, along_x):
        planes = ref.shape[0]
        for h in range(rows // 128):
            packed = jnp.zeros((32, 128), jnp.float32)
            for q in range(4):
                for c in range(planes):
                    to = 32 * q + 2 * c
                    moved = pltpu.roll(ref[c, pl.ds(128 * h + 32 * q, 32), :], to + 1, 1)
                    packed = jnp.where((lanes >> 1) == (to >> 1), moved, packed)
            along_y[0, h] = packed
        for side, row in ((0, rows - 1), (1, 0)):
            for c in range(planes):
                along_x[side, c : c + 1, :] = ref[c, row : row + 1, :]

    def side_copy(index, along_y, along_x, sems):
        side, dx, dy = sides[index]
        edge = along_y if dx == 0 else along_x
        return pltpu.make_async_remote_copy(
            src_ref=edge.at[0 if dx == 0 else side],
            dst_ref=edge.at[side + 1 if dx == 0 else side + 2],
            send_sem=sems.at[0, index],
            recv_sem=sems.at[1, index],
            device_id=(gx + dx, gy + dy),
            device_id_type=MESH,
        )

    def each_side(body, sign):
        for index, (_, dx, dy) in enumerate(sides):

            @pl.when(exists(gx + sign * dx, gy + sign * dy, nx, ny))
            def _():
                body(index)

    flow = (flow_y, flow_x, flow_sems)
    edges = (edge_y, edge_x, edge_sems)

    blocks[...] = jnp.zeros_like(blocks)
    for c in range(state_count):
        blocks[:, c, :] = old[c].astype(jnp.float32)
    for part in range(parts):
        span = pl.ds(part * depth, depth)
        pltpu.make_async_copy(weights.at[span], tiles.at[span], load_sem.at[part]).wait()

    def multiply(k, j, buffer):
        at = jnp.where(j < FIRST, j * CHUNK, (j - FIRST + 1) * WIDE)
        none = jnp.zeros((16, 128), jnp.bfloat16)
        join = jnp.concatenate
        for i in range(0, CHUNK, 4):
            four = [picks[k, at + i + n] for n in range(4)]
            a = [blocks[p & 127].astype(jnp.bfloat16) for p in four]
            w = [tiles[p >> 7] for p in four]
            left = join([join([a[n], none] if n % 2 == 0 else [none, a[n]], 1) for n in range(4)], 0)
            right = join([join([w[0], w[1]], 1), join([w[2], w[3]], 1)], 0)
            piece = lax.dot_general(
                left, right, (((1,), (1,)), ((), ())), preferred_element_type=jnp.float32
            )
            turn[buffer, pl.ds(16 * i, 32), :] = piece[:32, :128]
            turn[buffer, pl.ds(16 * i + 32, 32), :] = piece[32:, 128:]

    def lay(k, j, buffer):
        for group in range(CHUNK // 16):
            for c in range(state_count):
                turned = turn[buffer, pl.ds(256 * group + c, 16, stride=16), :]
                outgoing[
                    k,
                    pl.ds(pl.multiple_of(j * CHUNK + 16 * group, 16), 16),
                    pl.ds(c * 128, 128),
                ] = turned.astype(jnp.bfloat16)

    def send(k, j):
        @pl.when(k < 8)
        def _():
            chunk_copy(k, j).start()

    def sent(k):
        _, dy = step_of(k)
        return chunks_of(gx, gy, dy, nx, ny, caps)

    def channel(k, carry):
        def three(t, carry):
            j = FIRST * t
            multiply(k, j, 0)
            multiply(k, j + 1, 1)
            lay(k, j, 0)
            send(k, j)
            multiply(k, j + 2, 2)
            lay(k, j + 1, 1)
            send(k, j + 1)
            lay(k, j + 2, 2)
            send(k, j + 2)
            return carry

        def one(j, carry):
            multiply(k, j, 0)
            lay(k, j, 0)
            send(k, j)
            return carry

        @pl.when((k == 8) | goes_out(k))
        def _():
            @pl.when(k < 8)
            def _():
                label_copy(k).start()

            lax.fori_loop(0, jnp.where(k == 8, CHUNKS // FIRST, 1), three, 0)
            lax.fori_loop(FIRST, jnp.where(k == 8, FIRST, sent(k)), one, 0)

        @pl.when(k == 1)
        def _():
            gather_flag(0)
            send_flag(1)

        @pl.when(k == 7)
        def _():
            pack_edges(vel, flow_y, flow_x)
            each_side(lambda index: side_copy(index, *flow).start(), 1)

        return carry

    lax.fori_loop(0, 9, channel, 0)

    row_ids = lax.broadcasted_iota(jnp.int32, (rows, WIDE), 0)

    def add(label_row, values, first):
        width = values.shape[0]
        selector = jnp.where(row_ids == label_row, 1.0, 0.0).astype(jnp.bfloat16)[:, :width]
        for c in range(0, state_count, 2):
            summed = jnp.dot(
                selector,
                values[:, c * 128 : (c + 2) * 128],
                preferred_element_type=jnp.float32,
            )
            if first:
                remapped[c] = summed[:, :128]
                remapped[c + 1] = summed[:, 128:]
            else:
                remapped[c] += summed[:, :128]
                remapped[c + 1] += summed[:, 128:]

    def add_piece(label_rows, k, values, first):
        add(label_rows[k, :, :WIDE], values[k, : FIRST * CHUNK], first)

    def add_chunk(label_rows, k, values, j):
        lanes_of = slice((j - FIRST + 1) * WIDE, (j - FIRST + 2) * WIDE)
        add(label_rows[k, :, lanes_of], values[k, j * CHUNK : (j + 1) * CHUNK], False)

    add_piece(labels, 8, outgoing, True)
    for j in range(FIRST, CHUNKS):
        add_chunk(labels, 8, outgoing, j)

    def accept(k):
        dx, dy = step_of(k)
        arriving = chunks_of(gx - dx, gy - dy, dy, nx, ny, caps)
        label_copy(k).wait_recv()
        for j in range(FIRST):
            chunk_copy(k, j).wait_recv()
        add_piece(incoming_labels, k, incoming, False)
        for j in range(FIRST, CHUNKS):

            @pl.when(arriving > j)
            def _():
                chunk_copy(k, j).wait_recv()
                add_chunk(incoming_labels, k, incoming, j)

    def accept_in_turn(i, carry):
        k = lax.rem(i + 6, 8)

        @pl.when(comes_in(k))
        def _():
            accept(k)

        return carry

    lax.fori_loop(0, 8, accept_in_turn, 0)

    pack_edges(remapped, edge_y, edge_x)
    each_side(lambda index: side_copy(index, *edges).start(), 1)

    def land(along_y, along_x, sems):
        for index, (side, dx, dy) in enumerate(sides):
            edge, slot = (along_y, side + 1) if dx == 0 else (along_x, side + 2)
            there = exists(gx - dx, gy - dy, nx, ny)

            @pl.when(there)
            def _():
                side_copy(index, along_y, along_x, sems).wait_recv()

            @pl.when(jnp.logical_not(there))
            def _():
                edge[slot] = jnp.zeros(edge.shape[1:], jnp.float32)

    land(*flow)

    def step(b, carry):
        step_block(b, rows // 32, remapped, vel, flow_y, flow_x, out)
        return carry

    lax.fori_loop(0, rows // 32, step, 0)

    land(*edges)
    for side, row in ((0, 0), (1, rows - 1)):
        bound, scale = (jnp.maximum, time_step) if side == 0 else (jnp.minimum, -time_step)
        speed = scale * bound(vel[0, row : row + 1, :], 0.0)
        for c in range(state_count):
            out[c, row : row + 1, :] += speed * edge_x[side + 2, c : c + 1, :]

    each_side(lambda index: side_copy(index, *edges).wait_send(), 1)
    for h in range(rows // 128):
        moved = pltpu.roll(edge_y[1, h], 2, 1)
        edge_y[0, h] = jnp.where((lanes & 1) == 0, moved, edge_y[2, h])

    for b in range(rows // 32):
        span = slice(32 * b, 32 * (b + 1))
        flow_here = vel[1, span, :]
        speed = jnp.where(
            lanes == 0,
            time_step * jnp.maximum(flow_here, 0.0),
            jnp.where(lanes == 127, -time_step * jnp.minimum(flow_here, 0.0), 0.0),
        )
        pack = edge_y[0, b // 4]
        for c in range(state_count):
            out[c, span, :] += speed * pltpu.roll(pack, (126 - 32 * (b % 4) - 2 * c) % 128, 1)
    each_side(lambda index: side_copy(index, *flow).wait_send(), 1)

    def finish(k):
        label_copy(k).wait_send()

        def chunk(j, carry):
            chunk_copy(k, j).wait_send()
            return carry

        lax.fori_loop(0, sent(k), chunk, 0)

    each_channel(finish, goes_out)
    gather_flag(1)
    end_flag(0)
    end_flag(1)
    any_over[...] = flags[2]


def exchange(nx, ny, caps, collective_id, picks, labels, over, old, velocity, weights):
    state_count, rows = old.shape[0], velocity.shape[1]
    cap = CHUNKS * CHUNK
    f32, vmem = jnp.float32, pltpu.VMEM
    in_vmem = pl.BlockSpec(memory_space=vmem)
    dma = pltpu.SemaphoreType.DMA
    return pl.pallas_call(
        functools.partial(exchange_kernel, nx, ny, caps),
        out_shape=(
            jax.ShapeDtypeStruct((state_count, rows, 128), f32),
            jax.ShapeDtypeStruct((1, 128), f32),
        ),
        in_specs=[pl.BlockSpec(memory_space=pltpu.SMEM)]
        + [in_vmem] * 4
        + [pl.BlockSpec(memory_space=pl.ANY)],
        out_specs=(in_vmem,) * 2,
        scratch_shapes=[
            vmem((state_count, rows, 128), f32),
            vmem((old.shape[1], 16, 128), f32),
            vmem(weights.shape, jnp.bfloat16),
            vmem((9, cap, state_count * 128), jnp.bfloat16),
            vmem((8, cap, state_count * 128), jnp.bfloat16),
            vmem((8, 1, 4 * WIDE), jnp.int32),
            vmem((FIRST, 16 * CHUNK, 128), f32),
            vmem((3, rows // 128, 32, 128), f32),
            vmem((4, 16, 128), f32),
            vmem((3, rows // 128, 32, 128), f32),
            vmem((4, 16, 128), f32),
            vmem((3, 1, 128), f32),
            vmem((nx + ny, 1, 128), f32),
            dma((4,)),
            dma((2, 8)),
            dma((8, cap // CHUNK)),
            dma((8, cap // CHUNK)),
            dma((2, 4)),
            dma((2, 4)),
            dma((2, nx + ny)),
        ],
        compiler_params=pltpu.CompilerParams(
            collective_id=collective_id, has_side_effects=True, vmem_limit_bytes=48 * MIB
        ),
        cost_estimate=pl.CostEstimate(
            flops=2 * 9 * cap * 128 * 128 * 16,
            bytes_accessed=weights.size * 2,
            transcendentals=0,
        ),
    )(picks, labels, over, old, velocity, weights)


def step_block(b, blocks, state, vel, flow_y, flow_x, out):
    rows, depth = state.shape[1], 32
    base = pl.multiple_of(b * depth, depth)
    span = pl.ds(base, depth)
    lane = lax.broadcasted_iota(jnp.int32, (depth, 128), 1)
    row = lax.broadcasted_iota(jnp.int32, (depth, 128), 0)
    quarter = 32 * lax.rem(b, 4)
    left_pack = pltpu.roll(flow_y[1, b // 4], lax.rem(128 - quarter, 128), 1)
    right_pack = pltpu.roll(flow_y[2, b // 4], lax.rem(128 + 126 - quarter, 128), 1)

    def around(ref, c, halo):
        mid = ref[c, span, :]
        above = ref[c, pl.ds(jnp.maximum(base - 1, 0), 1), :]
        below = ref[c, pl.ds(jnp.minimum(base + depth, rows - 1), 1), :]
        if halo:
            first, last = flow_x[2, c : c + 1, :], flow_x[3, c : c + 1, :]
            shift = (128 - 2 * c) % 128
            left, right = pltpu.roll(left_pack, shift, 1), pltpu.roll(right_pack, shift, 1)
        else:
            first = last = left = right = 0.0
        above = jnp.where(b == 0, first, above)
        below = jnp.where(b == blocks - 1, last, below)
        before_x = jnp.where(row == 0, above, pltpu.roll(mid, 1, 0))
        after_x = jnp.where(row == depth - 1, below, pltpu.roll(mid, depth - 1, 0))
        before_y = jnp.where(lane == 0, left, pltpu.roll(mid, 1, 1))
        after_y = jnp.where(lane == 127, right, pltpu.roll(mid, 127, 1))
        return mid, before_x, after_x, before_y, after_y

    u_x, ux_bx, ux_ax, ux_by, ux_ay = around(vel, 0, True)
    u_y, uy_bx, uy_ax, uy_by, uy_ay = around(vel, 1, True)
    d_xx = 0.5 * (ux_ax - ux_bx)
    l_xy = 0.5 * (ux_ay - ux_by)
    l_yx = 0.5 * (uy_ax - uy_bx)
    d_yy = 0.5 * (uy_ay - uy_by)
    d_zz = -(d_xx + d_yy)
    d_xy = 0.5 * (l_xy + l_yx)
    spin = 0.5 * (l_xy - l_yx)
    plus_x, minus_x = jnp.maximum(u_x, 0.0), jnp.minimum(u_x, 0.0)
    plus_y, minus_y = jnp.maximum(u_y, 0.0), jnp.minimum(u_y, 0.0)
    shear = (2.0 * interaction) * jnp.sqrt(
        2.0 * (d_xx * d_xx + d_yy * d_yy + d_zz * d_zz + 2.0 * (d_xy * d_xy)) + 1.0
    )
    a_xx, a_yy, a_zz, a_xy, a_xz, a_yz = (state[c, span, :] for c in range(6))
    contraction = d_xx * a_xx + d_yy * a_yy + d_zz * a_zz + 2.0 * (d_xy * a_xy)
    fade = shape_factor * 2.0 * contraction + 3.0 * shear
    stress = 2.0 * shear_modulus
    pull = fiber_number * contraction
    sources = (
        2.0 * (spin * a_xy) + shape_factor * 2.0 * (d_xx * a_xx + d_xy * a_xy) - fade * a_xx + shear,
        -2.0 * (spin * a_xy) + shape_factor * 2.0 * (d_xy * a_xy + d_yy * a_yy) - fade * a_yy + shear,
        shape_factor * 2.0 * (d_zz * a_zz) - fade * a_zz + shear,
        spin * (a_yy - a_xx)
        + shape_factor * (d_xx * a_xy + d_xy * a_yy + a_xx * d_xy + a_xy * d_yy)
        - fade * a_xy,
        spin * a_yz + shape_factor * (d_xx * a_xz + d_xy * a_yz + a_xz * d_zz) - fade * a_xz,
        -spin * a_xz + shape_factor * (d_xy * a_xz + d_yy * a_yz + a_yz * d_zz) - fade * a_yz,
        d_xx,
        d_yy,
        d_xy,
        stress * (d_xx + pull * a_xx),
        stress * (d_yy + pull * a_yy),
        stress * (d_xy + pull * a_xy),
    )
    for c, source in enumerate(sources):
        mid, before_x, after_x, before_y, after_y = around(state, c, False)
        upwind = (
            plus_x * (mid - before_x)
            + minus_x * (after_x - mid)
            + plus_y * (mid - before_y)
            + minus_y * (after_y - mid)
        )
        out[c, span, :] = mid + time_step * (source - upwind)


def per_device(
    nx,
    ny,
    old_states,
    weight_tiles,
    source_block,
    tile_index,
    dest_device,
    dest_block,
    send_count,
    velocity,
):
    lists = (send_count, source_block, tile_index, dest_device, dest_block)
    old = jnp.transpose(old_states, (1, 0, 2))
    places = plan(nx, ny, USUAL, lists)
    states, any_over = exchange(nx, ny, USUAL, 0, *places, old, velocity, weight_tiles)

    def again(_):
        return exchange(nx, ny, FULL, 1, *places, old, velocity, weight_tiles)[0]

    states = lax.cond(any_over[0, 0] > 0, again, lambda enough: enough, states)
    return jnp.transpose(states, (1, 0, 2))


def solution(mesh):
    in_specs = (
        P(("gx", "gy"), None, None),
        P(("gx", "gy"), None, None),
        P(("gx", "gy")),
        P(("gx", "gy")),
        P(("gx", "gy")),
        P(("gx", "gy")),
        P(("gx", "gy")),
        P(None, "gx", "gy"),
    )
    out_specs = P("gx", None, "gy")
    return jax.shard_map(
        functools.partial(per_device, mesh.shape["gx"], mesh.shape["gy"]),
        mesh=mesh,
        in_specs=in_specs,
        out_specs=out_specs,
        check_vma=False,
    )
```

```python
import functools

import jax
import jax.numpy as jnp
from jax import lax
from jax.experimental import pallas as pl
from jax.experimental.pallas import tpu as pltpu
from jax.sharding import PartitionSpec as P

time_step = 0.2
shape_factor = 0.95
interaction = 0.01
shear_modulus = 1.0
fiber_number = 2.0

MESH = pl.DeviceIdType.MESH
CHUNK = 32
WIDE = 128
FIRST = 3
CHUNKS = 6
USUAL = (3, 4, 5, 6)
FULL = (6, 6, 6, 6)
MIB = 1 << 20


STEPS = ((-1, 1), (-1, -1), (1, 1), (1, -1), (0, 1), (0, -1), (-1, 0), (1, 0), (0, 0))


def step_of(k):
    m = k // 2
    dx = jnp.where(k < 6, jnp.where(m == 2, 0, 2 * m - 1), 2 * (k - 6) - 1)
    dy = jnp.where(k < 6, 1 - 2 * (k % 2), 0)
    return dx, dy


def exists(x, y, nx, ny):
    return (x >= 0) & (x < nx) & (y >= 0) & (y < ny)


def neighbours_of(x, y, nx, ny):
    spread_x = 3 - (x == 0).astype(jnp.int32) - (x == nx - 1).astype(jnp.int32)
    spread_y = 3 - (y == 0).astype(jnp.int32) - (y == ny - 1).astype(jnp.int32)
    return spread_x * spread_y - 1


def chunks_of(x, y, dy, nx, ny, caps):
    n = neighbours_of(x, y, nx, ny)
    inner, along, edge, corner = caps
    sidewise = jnp.where((dy != 0) & ((y == 0) | (y == ny - 1)), along, edge)
    return jnp.where(n >= 8, inner, jnp.where(n >= 5, sidewise, corner))


def plan_kernel(
    nx,
    ny,
    caps,
    send_count,
    source_block,
    tile_index,
    dest_device,
    dest_block,
    picks,
    labels,
    over_flag,
):
    gx, gy = lax.axis_index("gx"), lax.axis_index("gy")

    slots = source_block.shape[0]
    dest, tile = dest_device[...].reshape(1, slots), tile_index[...].reshape(1, slots)
    ids = lax.broadcasted_iota(jnp.int32, (1, slots), 1)
    place_shift = ny.bit_length() - 1
    step_x = (dest >> place_shift) - gx
    step_y = (dest & (ny - 1)) - gy
    channel_of = jnp.full((1, slots), 15, jnp.int32)
    for k, (dx, dy) in enumerate(STEPS):
        channel_of = jnp.where((step_x == dx) & (step_y == dy), k, channel_of)
    channel_of = jnp.where(ids < send_count[0], channel_of, 15)
    matches = channel_of == lax.broadcasted_iota(jnp.int32, (16, slots), 0)
    matches = matches & (lax.broadcasted_iota(jnp.int32, (16, slots), 0) < 9)
    ones = jnp.where(matches, 1.0, 0.0)
    counts = jnp.sum(ones, axis=1, keepdims=True)
    over = jnp.zeros((1, 1), jnp.float32)
    for k, (_, dy) in enumerate(STEPS[:8]):
        allowed = (chunks_of(gx, gy, dy, nx, ny, caps) * CHUNK).astype(jnp.float32)
        over = jnp.maximum(over, jnp.where(counts[k : k + 1] > allowed, 1.0, 0.0))
    over_flag[...] = jnp.broadcast_to(over, over_flag.shape)
    before = lax.broadcasted_iota(jnp.int32, (slots, slots), 0) < lax.broadcasted_iota(
        jnp.int32, (slots, slots), 1
    )
    earlier = jnp.dot(
        ones.astype(jnp.bfloat16),
        jnp.where(before, 1.0, 0.0).astype(jnp.bfloat16),
        preferred_element_type=jnp.float32,
    )
    position = jnp.sum(ones * earlier, axis=0, keepdims=True).astype(jnp.int32)
    place = lax.broadcasted_iota(jnp.int32, (4 * WIDE, slots), 0)
    place = jnp.where(
        place < WIDE,
        jnp.where(place < FIRST * CHUNK, place, -1),
        jnp.where(place % WIDE < CHUNK, place % WIDE + (place // WIDE + FIRST - 1) * CHUNK, -1),
    )
    at_place = jnp.where(place == position, 1.0, 0.0).astype(jnp.bfloat16)
    source, row = source_block[...].reshape(1, slots), dest_block[...].reshape(1, slots)
    parcels = [source, tile >> 1, tile & 1, row + 1]
    parcels = [(ones * v.astype(jnp.float32)).astype(jnp.bfloat16) for v in parcels]
    ordered = lax.dot_general(
        jnp.concatenate(parcels, axis=0),
        at_place,
        (((1,), (1,)), ((), ())),
        preferred_element_type=jnp.float32,
    )
    picks[...] = (
        (2.0 * ordered[16:32] + ordered[32:48]) * 128.0 + ordered[0:16]
    ).astype(jnp.int32)
    label_rows = ordered[48:64].astype(jnp.int32) - 1
    for k in range(9):
        labels[k] = label_rows[k : k + 1]


def plan(nx, ny, caps, lists):
    in_vmem = pl.BlockSpec(memory_space=pltpu.VMEM)
    return pl.pallas_call(
        functools.partial(plan_kernel, nx, ny, caps),
        out_shape=(
            jax.ShapeDtypeStruct((16, 4 * WIDE), jnp.int32),
            jax.ShapeDtypeStruct((9, 1, 4 * WIDE), jnp.int32),
            jax.ShapeDtypeStruct((1, 128), jnp.float32),
        ),
        in_specs=[pl.BlockSpec(memory_space=pltpu.SMEM)] + [in_vmem] * 4,
        out_specs=(in_vmem,) * 3,
    )(*lists)


def exchange_kernel(
    nx,
    ny,
    caps,
    picks,
    labels,
    over,
    old,
    vel,
    weights,
    out,
    any_over,
    remapped,
    blocks,
    tiles,
    outgoing,
    incoming,
    incoming_labels,
    turn,
    edge_y,
    edge_x,
    flow_y,
    flow_x,
    flags,
    flags_in,
    load_sem,
    label_sems,
    send_sems,
    recv_sems,
    edge_sems,
    flow_sems,
    flag_sems,
):
    gx, gy = lax.axis_index("gx"), lax.axis_index("gy")
    parts = load_sem.shape[0]
    depth = tiles.shape[0] // parts
    cap = outgoing.shape[1]
    state_count, rows = remapped.shape[:2]

    for part in range(parts):
        span = pl.ds(part * depth, depth)
        pltpu.make_async_copy(weights.at[span], tiles.at[span], load_sem.at[part]).start()

    barrier = pltpu.get_barrier_semaphore()
    for k in range(8):
        dx, dy = step_of(k)

        @pl.when(exists(gx + dx, gy + dy, nx, ny))
        def _():
            pl.semaphore_signal(
                barrier, inc=1, device_id=(gx + dx, gy + dy), device_id_type=MESH
            )


    def along_gx(j):
        return (lax.rem(gx + j, nx), gy)

    def along_gy(j):
        return (gx, lax.rem(gy + j, ny))

    def greet(j, carry, along):
        pl.semaphore_signal(barrier, inc=1, device_id=along(j), device_id_type=MESH)
        return carry

    lax.fori_loop(1, nx, functools.partial(greet, along=along_gx), 0)
    lax.fori_loop(1, ny, functools.partial(greet, along=along_gy), 0)
    blocks[...] = jnp.zeros_like(blocks)
    for c in range(state_count):
        blocks[:, c, :] = old[c].astype(jnp.float32)
    pl.semaphore_wait(barrier, neighbours_of(gx, gy, nx, ny) + nx + ny - 2)

    def flag_copy(turn_of, j):
        slot = turn_of * nx + j
        return pltpu.make_async_remote_copy(
            src_ref=flags.at[turn_of],
            dst_ref=flags_in.at[slot],
            send_sem=flag_sems.at[0, slot],
            recv_sem=flag_sems.at[1, slot],
            device_id=(along_gx, along_gy)[turn_of](j),
            device_id_type=MESH,
        )

    def send_flag(turn_of):
        def step(j, carry):
            flag_copy(turn_of, j).start()
            return carry

        lax.fori_loop(1, (nx, ny)[turn_of], step, 0)

    def gather_flag(turn_of):
        def step(j, carry):
            flag_copy(turn_of, j).wait_recv()
            return jnp.maximum(carry, flags_in[turn_of * nx + j])

        flags[turn_of + 1] = lax.fori_loop(1, (nx, ny)[turn_of], step, flags[turn_of])

    def end_flag(turn_of):
        def step(j, carry):
            flag_copy(turn_of, j).wait_send()
            return carry

        lax.fori_loop(1, (nx, ny)[turn_of], step, 0)

    flags[0] = over[...]

    def label_copy(k):
        dx, dy = step_of(k)
        return pltpu.make_async_remote_copy(
            src_ref=labels.at[k],
            dst_ref=incoming_labels.at[k],
            send_sem=label_sems.at[0, k],
            recv_sem=label_sems.at[1, k],
            device_id=(gx + dx, gy + dy),
            device_id_type=MESH,
        )

    def chunk_copy(k, j):
        dx, dy = step_of(k)
        span = pl.ds(j * CHUNK, CHUNK)
        return pltpu.make_async_remote_copy(
            src_ref=outgoing.at[k, span],
            dst_ref=incoming.at[k, span],
            send_sem=send_sems.at[k, j],
            recv_sem=recv_sems.at[k, j],
            device_id=(gx + dx, gy + dy),
            device_id_type=MESH,
        )

    def goes_out(k):
        dx, dy = step_of(k)
        return exists(gx + dx, gy + dy, nx, ny)

    def comes_in(k):
        dx, dy = step_of(k)
        return exists(gx - dx, gy - dy, nx, ny)

    def each_channel(body, predicate):
        def step(k, carry):
            @pl.when(predicate(k))
            def _():
                body(k)

            return carry

        lax.fori_loop(0, 8, step, 0)

    lanes = lax.broadcasted_iota(jnp.int32, (32, 128), 1)
    sides = ((0, 0, 1), (1, 0, -1), (0, 1, 0), (1, -1, 0))

    def pack_edges(ref, along_y, along_x):
        planes = ref.shape[0]
        for h in range(rows // 128):
            packed = jnp.zeros((32, 128), jnp.float32)
            for q in range(4):
                for c in range(planes):
                    to = 32 * q + 2 * c
                    moved = pltpu.roll(ref[c, pl.ds(128 * h + 32 * q, 32), :], to + 1, 1)
                    packed = jnp.where((lanes >> 1) == (to >> 1), moved, packed)
            along_y[0, h] = packed
        for side, row in ((0, rows - 1), (1, 0)):
            for c in range(planes):
                along_x[side, c : c + 1, :] = ref[c, row : row + 1, :]

    def side_copy(index, along_y, along_x, sems):
        side, dx, dy = sides[index]
        edge = along_y if dx == 0 else along_x
        return pltpu.make_async_remote_copy(
            src_ref=edge.at[0 if dx == 0 else side],
            dst_ref=edge.at[side + 1 if dx == 0 else side + 2],
            send_sem=sems.at[0, index],
            recv_sem=sems.at[1, index],
            device_id=(gx + dx, gy + dy),
            device_id_type=MESH,
        )

    def each_side(body, sign):
        for index, (_, dx, dy) in enumerate(sides):

            @pl.when(exists(gx + sign * dx, gy + sign * dy, nx, ny))
            def _():
                body(index)

    flow = (flow_y, flow_x, flow_sems)
    edges = (edge_y, edge_x, edge_sems)

    for part in range(parts):
        span = pl.ds(part * depth, depth)
        pltpu.make_async_copy(weights.at[span], tiles.at[span], load_sem.at[part]).wait()

    def multiply(k, j, buffer):
        at = jnp.where(j < FIRST, j * CHUNK, (j - FIRST + 1) * WIDE)
        none = jnp.zeros((16, 128), jnp.bfloat16)
        join = jnp.concatenate
        for i in range(0, CHUNK, 4):
            four = [picks[k, at + i + n] for n in range(4)]
            a = [blocks[p & 127].astype(jnp.bfloat16) for p in four]
            w = [tiles[p >> 7] for p in four]
            left = join([join([a[n], none] if n % 2 == 0 else [none, a[n]], 1) for n in range(4)], 0)
            right = join([join([w[0], w[1]], 1), join([w[2], w[3]], 1)], 0)
            piece = lax.dot_general(
                left, right, (((1,), (1,)), ((), ())), preferred_element_type=jnp.float32
            )
            turn[buffer, pl.ds(16 * i, 32), :] = piece[:32, :128]
            turn[buffer, pl.ds(16 * i + 32, 32), :] = piece[32:, 128:]

    def lay(k, j, buffer):
        for group in range(CHUNK // 16):
            for c in range(state_count):
                turned = turn[buffer, pl.ds(256 * group + c, 16, stride=16), :]
                outgoing[
                    k,
                    pl.ds(pl.multiple_of(j * CHUNK + 16 * group, 16), 16),
                    pl.ds(c * 128, 128),
                ] = turned.astype(jnp.bfloat16)

    def send(k, j):
        @pl.when(k < 8)
        def _():
            chunk_copy(k, j).start()

    def sent(k):
        _, dy = step_of(k)
        return chunks_of(gx, gy, dy, nx, ny, caps)

    def channel(k, carry):
        def three(t, carry):
            j = FIRST * t
            multiply(k, j, 0)
            multiply(k, j + 1, 1)
            lay(k, j, 0)
            send(k, j)
            multiply(k, j + 2, 2)
            lay(k, j + 1, 1)
            send(k, j + 1)
            lay(k, j + 2, 2)
            send(k, j + 2)
            return carry

        def one(j, carry):
            multiply(k, j, 0)
            lay(k, j, 0)
            send(k, j)
            return carry

        @pl.when((k == 8) | goes_out(k))
        def _():
            @pl.when(k < 8)
            def _():
                label_copy(k).start()

            lax.fori_loop(0, jnp.where(k == 8, CHUNKS // FIRST, 1), three, 0)
            lax.fori_loop(FIRST, jnp.where(k == 8, FIRST, sent(k)), one, 0)

        @pl.when(k == 1)
        def _():
            send_flag(0)

        @pl.when(k == 3)
        def _():
            gather_flag(0)
            send_flag(1)

        @pl.when(k == 7)
        def _():
            pack_edges(vel, flow_y, flow_x)
            each_side(lambda index: side_copy(index, *flow).start(), 1)

        return carry

    lax.fori_loop(0, 9, channel, 0)

    row_ids = lax.broadcasted_iota(jnp.int32, (rows, WIDE), 0)

    def add(label_row, values, first):
        width = values.shape[0]
        selector = jnp.where(row_ids == label_row, 1.0, 0.0).astype(jnp.bfloat16)[:, :width]
        for c in range(0, state_count, 2):
            summed = jnp.dot(
                selector,
                values[:, c * 128 : (c + 2) * 128],
                preferred_element_type=jnp.float32,
            )
            if first:
                remapped[c] = summed[:, :128]
                remapped[c + 1] = summed[:, 128:]
            else:
                remapped[c] += summed[:, :128]
                remapped[c + 1] += summed[:, 128:]

    def add_piece(label_rows, k, values, first):
        add(label_rows[k, :, :WIDE], values[k, : FIRST * CHUNK], first)

    def add_chunk(label_rows, k, values, j):
        lanes_of = slice((j - FIRST + 1) * WIDE, (j - FIRST + 2) * WIDE)
        add(label_rows[k, :, lanes_of], values[k, j * CHUNK : (j + 1) * CHUNK], False)

    add_piece(labels, 8, outgoing, True)
    for j in range(FIRST, CHUNKS):
        add_chunk(labels, 8, outgoing, j)

    def accept(k):
        dx, dy = step_of(k)
        arriving = chunks_of(gx - dx, gy - dy, dy, nx, ny, caps)
        label_copy(k).wait_recv()
        for j in range(FIRST):
            chunk_copy(k, j).wait_recv()
        add_piece(incoming_labels, k, incoming, False)
        for j in range(FIRST, CHUNKS):

            @pl.when(arriving > j)
            def _():
                chunk_copy(k, j).wait_recv()
                add_chunk(incoming_labels, k, incoming, j)

    def accept_in_turn(i, carry):
        k = lax.rem(i + 6, 8)

        @pl.when(comes_in(k))
        def _():
            accept(k)

        return carry

    lax.fori_loop(0, 8, accept_in_turn, 0)

    pack_edges(remapped, edge_y, edge_x)
    each_side(lambda index: side_copy(index, *edges).start(), 1)

    def land(along_y, along_x, sems):
        for index, (side, dx, dy) in enumerate(sides):
            edge, slot = (along_y, side + 1) if dx == 0 else (along_x, side + 2)
            there = exists(gx - dx, gy - dy, nx, ny)

            @pl.when(there)
            def _():
                side_copy(index, along_y, along_x, sems).wait_recv()

            @pl.when(jnp.logical_not(there))
            def _():
                edge[slot] = jnp.zeros(edge.shape[1:], jnp.float32)

    land(*flow)

    def step(b, carry):
        step_block(b, rows // 32, remapped, vel, flow_y, flow_x, out)
        return carry

    lax.fori_loop(0, rows // 32, step, 0)

    land(*edges)
    for side, row in ((0, 0), (1, rows - 1)):
        bound, scale = (jnp.maximum, time_step) if side == 0 else (jnp.minimum, -time_step)
        speed = scale * bound(vel[0, row : row + 1, :], 0.0)
        for c in range(state_count):
            out[c, row : row + 1, :] += speed * edge_x[side + 2, c : c + 1, :]

    each_side(lambda index: side_copy(index, *edges).wait_send(), 1)
    for h in range(rows // 128):
        moved = pltpu.roll(edge_y[1, h], 2, 1)
        edge_y[0, h] = jnp.where((lanes & 1) == 0, moved, edge_y[2, h])

    for b in range(rows // 32):
        span = slice(32 * b, 32 * (b + 1))
        flow_here = vel[1, span, :]
        speed = jnp.where(
            lanes == 0,
            time_step * jnp.maximum(flow_here, 0.0),
            jnp.where(lanes == 127, -time_step * jnp.minimum(flow_here, 0.0), 0.0),
        )
        pack = edge_y[0, b // 4]
        for c in range(state_count):
            out[c, span, :] += speed * pltpu.roll(pack, (126 - 32 * (b % 4) - 2 * c) % 128, 1)
    each_side(lambda index: side_copy(index, *flow).wait_send(), 1)

    def finish(k):
        label_copy(k).wait_send()

        def chunk(j, carry):
            chunk_copy(k, j).wait_send()
            return carry

        lax.fori_loop(0, sent(k), chunk, 0)

    each_channel(finish, goes_out)
    gather_flag(1)
    end_flag(0)
    end_flag(1)
    any_over[...] = flags[2]


def exchange(nx, ny, caps, collective_id, picks, labels, over, old, velocity, weights):
    state_count, rows = old.shape[0], velocity.shape[1]
    cap = CHUNKS * CHUNK
    f32, vmem = jnp.float32, pltpu.VMEM
    in_vmem = pl.BlockSpec(memory_space=vmem)
    dma = pltpu.SemaphoreType.DMA
    return pl.pallas_call(
        functools.partial(exchange_kernel, nx, ny, caps),
        out_shape=(
            jax.ShapeDtypeStruct((state_count, rows, 128), f32),
            jax.ShapeDtypeStruct((1, 128), f32),
        ),
        in_specs=[pl.BlockSpec(memory_space=pltpu.SMEM)]
        + [in_vmem] * 4
        + [pl.BlockSpec(memory_space=pl.ANY)],
        out_specs=(in_vmem,) * 2,
        scratch_shapes=[
            vmem((state_count, rows, 128), f32),
            vmem((old.shape[1], 16, 128), f32),
            vmem(weights.shape, jnp.bfloat16),
            vmem((9, cap, state_count * 128), jnp.bfloat16),
            vmem((8, cap, state_count * 128), jnp.bfloat16),
            vmem((8, 1, 4 * WIDE), jnp.int32),
            vmem((FIRST, 16 * CHUNK, 128), f32),
            vmem((3, rows // 128, 32, 128), f32),
            vmem((4, 16, 128), f32),
            vmem((3, rows // 128, 32, 128), f32),
            vmem((4, 16, 128), f32),
            vmem((3, 1, 128), f32),
            vmem((nx + ny, 1, 128), f32),
            dma((4,)),
            dma((2, 8)),
            dma((8, cap // CHUNK)),
            dma((8, cap // CHUNK)),
            dma((2, 4)),
            dma((2, 4)),
            dma((2, nx + ny)),
        ],
        compiler_params=pltpu.CompilerParams(
            collective_id=collective_id, has_side_effects=True, vmem_limit_bytes=48 * MIB
        ),
        cost_estimate=pl.CostEstimate(
            flops=2 * 9 * cap * 128 * 128 * 16,
            bytes_accessed=weights.size * 2,
            transcendentals=0,
        ),
    )(picks, labels, over, old, velocity, weights)


def step_block(b, blocks, state, vel, flow_y, flow_x, out):
    rows, depth = state.shape[1], 32
    base = pl.multiple_of(b * depth, depth)
    span = pl.ds(base, depth)
    lane = lax.broadcasted_iota(jnp.int32, (depth, 128), 1)
    row = lax.broadcasted_iota(jnp.int32, (depth, 128), 0)
    quarter = 32 * lax.rem(b, 4)
    left_pack = pltpu.roll(flow_y[1, b // 4], lax.rem(128 - quarter, 128), 1)
    right_pack = pltpu.roll(flow_y[2, b // 4], lax.rem(128 + 126 - quarter, 128), 1)

    def around(ref, c, halo):
        mid = ref[c, span, :]
        above = ref[c, pl.ds(jnp.maximum(base - 1, 0), 1), :]
        below = ref[c, pl.ds(jnp.minimum(base + depth, rows - 1), 1), :]
        if halo:
            first, last = flow_x[2, c : c + 1, :], flow_x[3, c : c + 1, :]
            shift = (128 - 2 * c) % 128
            left, right = pltpu.roll(left_pack, shift, 1), pltpu.roll(right_pack, shift, 1)
        else:
            first = last = left = right = 0.0
        above = jnp.where(b == 0, first, above)
        below = jnp.where(b == blocks - 1, last, below)
        before_x = jnp.where(row == 0, above, pltpu.roll(mid, 1, 0))
        after_x = jnp.where(row == depth - 1, below, pltpu.roll(mid, depth - 1, 0))
        before_y = jnp.where(lane == 0, left, pltpu.roll(mid, 1, 1))
        after_y = jnp.where(lane == 127, right, pltpu.roll(mid, 127, 1))
        return mid, before_x, after_x, before_y, after_y

    u_x, ux_bx, ux_ax, ux_by, ux_ay = around(vel, 0, True)
    u_y, uy_bx, uy_ax, uy_by, uy_ay = around(vel, 1, True)
    d_xx = 0.5 * (ux_ax - ux_bx)
    l_xy = 0.5 * (ux_ay - ux_by)
    l_yx = 0.5 * (uy_ax - uy_bx)
    d_yy = 0.5 * (uy_ay - uy_by)
    d_zz = -(d_xx + d_yy)
    d_xy = 0.5 * (l_xy + l_yx)
    spin = 0.5 * (l_xy - l_yx)
    plus_x, minus_x = jnp.maximum(u_x, 0.0), jnp.minimum(u_x, 0.0)
    plus_y, minus_y = jnp.maximum(u_y, 0.0), jnp.minimum(u_y, 0.0)
    shear = (2.0 * interaction) * jnp.sqrt(
        2.0 * (d_xx * d_xx + d_yy * d_yy + d_zz * d_zz + 2.0 * (d_xy * d_xy)) + 1.0
    )
    a_xx, a_yy, a_zz, a_xy, a_xz, a_yz = (state[c, span, :] for c in range(6))
    contraction = d_xx * a_xx + d_yy * a_yy + d_zz * a_zz + 2.0 * (d_xy * a_xy)
    fade = shape_factor * 2.0 * contraction + 3.0 * shear
    stress = 2.0 * shear_modulus
    pull = fiber_number * contraction
    sources = (
        2.0 * (spin * a_xy) + shape_factor * 2.0 * (d_xx * a_xx + d_xy * a_xy) - fade * a_xx + shear,
        -2.0 * (spin * a_xy) + shape_factor * 2.0 * (d_xy * a_xy + d_yy * a_yy) - fade * a_yy + shear,
        shape_factor * 2.0 * (d_zz * a_zz) - fade * a_zz + shear,
        spin * (a_yy - a_xx)
        + shape_factor * (d_xx * a_xy + d_xy * a_yy + a_xx * d_xy + a_xy * d_yy)
        - fade * a_xy,
        spin * a_yz + shape_factor * (d_xx * a_xz + d_xy * a_yz + a_xz * d_zz) - fade * a_xz,
        -spin * a_xz + shape_factor * (d_xy * a_xz + d_yy * a_yz + a_yz * d_zz) - fade * a_yz,
        d_xx,
        d_yy,
        d_xy,
        stress * (d_xx + pull * a_xx),
        stress * (d_yy + pull * a_yy),
        stress * (d_xy + pull * a_xy),
    )
    for c, source in enumerate(sources):
        mid, before_x, after_x, before_y, after_y = around(state, c, False)
        upwind = (
            plus_x * (mid - before_x)
            + minus_x * (after_x - mid)
            + plus_y * (mid - before_y)
            + minus_y * (after_y - mid)
        )
        out[c, span, :] = mid + time_step * (source - upwind)


def per_device(
    nx,
    ny,
    old_states,
    weight_tiles,
    source_block,
    tile_index,
    dest_device,
    dest_block,
    send_count,
    velocity,
):
    lists = (send_count, source_block, tile_index, dest_device, dest_block)
    old = jnp.transpose(old_states, (1, 0, 2))
    places = plan(nx, ny, USUAL, lists)
    states, any_over = exchange(nx, ny, USUAL, 0, *places, old, velocity, weight_tiles)

    def again(_):
        return exchange(nx, ny, FULL, 1, *places, old, velocity, weight_tiles)[0]

    states = lax.cond(any_over[0, 0] > 0, again, lambda enough: enough, states)
    return jnp.transpose(states, (1, 0, 2))


def solution(mesh):
    in_specs = (
        P(("gx", "gy"), None, None),
        P(("gx", "gy"), None, None),
        P(("gx", "gy")),
        P(("gx", "gy")),
        P(("gx", "gy")),
        P(("gx", "gy")),
        P(("gx", "gy")),
        P(None, "gx", "gy"),
    )
    out_specs = P("gx", None, "gy")
    return jax.shard_map(
        functools.partial(per_device, mesh.shape["gx"], mesh.shape["gy"]),
        mesh=mesh,
        in_specs=in_specs,
        out_specs=out_specs,
        check_vma=False,
    )
```

```python
import functools

import jax
import jax.numpy as jnp
from jax import lax
from jax.experimental import pallas as pl
from jax.experimental.pallas import tpu as pltpu
from jax.sharding import PartitionSpec as P

time_step = 0.2
shape_factor = 0.95
interaction = 0.01
shear_modulus = 1.0
fiber_number = 2.0

MESH = pl.DeviceIdType.MESH
CHUNK = 32
WIDE = 128
FIRST = 3
CHUNKS = 6
USUAL = (3, 4, 5, 6)
FULL = (6, 6, 6, 6)
MIB = 1 << 20


STEPS = ((-1, 1), (-1, -1), (1, 1), (1, -1), (0, 1), (0, -1), (-1, 0), (1, 0), (0, 0))


def step_of(k):
    m = k // 2
    dx = jnp.where(k < 6, jnp.where(m == 2, 0, 2 * m - 1), 2 * (k - 6) - 1)
    dy = jnp.where(k < 6, 1 - 2 * (k % 2), 0)
    return dx, dy


def exists(x, y, nx, ny):
    return (x >= 0) & (x < nx) & (y >= 0) & (y < ny)


def neighbours_of(x, y, nx, ny):
    spread_x = 3 - (x == 0).astype(jnp.int32) - (x == nx - 1).astype(jnp.int32)
    spread_y = 3 - (y == 0).astype(jnp.int32) - (y == ny - 1).astype(jnp.int32)
    return spread_x * spread_y - 1


def chunks_of(x, y, dy, nx, ny, caps):
    n = neighbours_of(x, y, nx, ny)
    inner, along, edge, corner = caps
    sidewise = jnp.where((dy != 0) & ((y == 0) | (y == ny - 1)), along, edge)
    return jnp.where(n >= 8, inner, jnp.where(n >= 5, sidewise, corner))


def plan_kernel(
    nx,
    ny,
    caps,
    send_count,
    source_block,
    tile_index,
    dest_device,
    dest_block,
    picks,
    labels,
    over_flag,
):
    gx, gy = lax.axis_index("gx"), lax.axis_index("gy")

    slots = source_block.shape[0]
    dest, tile = dest_device[...].reshape(1, slots), tile_index[...].reshape(1, slots)
    ids = lax.broadcasted_iota(jnp.int32, (1, slots), 1)
    place_shift = ny.bit_length() - 1
    step_x = (dest >> place_shift) - gx
    step_y = (dest & (ny - 1)) - gy
    channel_of = jnp.full((1, slots), 15, jnp.int32)
    for k, (dx, dy) in enumerate(STEPS):
        channel_of = jnp.where((step_x == dx) & (step_y == dy), k, channel_of)
    channel_of = jnp.where(ids < send_count[0], channel_of, 15)
    matches = channel_of == lax.broadcasted_iota(jnp.int32, (16, slots), 0)
    matches = matches & (lax.broadcasted_iota(jnp.int32, (16, slots), 0) < 9)
    ones = jnp.where(matches, 1.0, 0.0)
    counts = jnp.sum(ones, axis=1, keepdims=True)
    over = jnp.zeros((1, 1), jnp.float32)
    for k, (_, dy) in enumerate(STEPS[:8]):
        allowed = (chunks_of(gx, gy, dy, nx, ny, caps) * CHUNK).astype(jnp.float32)
        over = jnp.maximum(over, jnp.where(counts[k : k + 1] > allowed, 1.0, 0.0))
    over_flag[...] = jnp.broadcast_to(over, over_flag.shape)
    before = lax.broadcasted_iota(jnp.int32, (slots, slots), 0) < lax.broadcasted_iota(
        jnp.int32, (slots, slots), 1
    )
    earlier = jnp.dot(
        ones.astype(jnp.bfloat16),
        jnp.where(before, 1.0, 0.0).astype(jnp.bfloat16),
        preferred_element_type=jnp.float32,
    )
    position = jnp.sum(ones * earlier, axis=0, keepdims=True).astype(jnp.int32)
    place = lax.broadcasted_iota(jnp.int32, (4 * WIDE, slots), 0)
    place = jnp.where(
        place < WIDE,
        jnp.where(place < FIRST * CHUNK, place, -1),
        jnp.where(place % WIDE < CHUNK, place % WIDE + (place // WIDE + FIRST - 1) * CHUNK, -1),
    )
    at_place = jnp.where(place == position, 1.0, 0.0).astype(jnp.bfloat16)
    source, row = source_block[...].reshape(1, slots), dest_block[...].reshape(1, slots)
    parcels = [source, tile >> 1, tile & 1, row + 1]
    parcels = [(ones * v.astype(jnp.float32)).astype(jnp.bfloat16) for v in parcels]
    ordered = lax.dot_general(
        jnp.concatenate(parcels, axis=0),
        at_place,
        (((1,), (1,)), ((), ())),
        preferred_element_type=jnp.float32,
    )
    picks[...] = (
        (2.0 * ordered[16:32] + ordered[32:48]) * 128.0 + ordered[0:16]
    ).astype(jnp.int32)
    label_rows = ordered[48:64].astype(jnp.int32) - 1
    for k in range(9):
        labels[k] = label_rows[k : k + 1]


def plan(nx, ny, caps, lists):
    in_vmem = pl.BlockSpec(memory_space=pltpu.VMEM)
    return pl.pallas_call(
        functools.partial(plan_kernel, nx, ny, caps),
        out_shape=(
            jax.ShapeDtypeStruct((16, 4 * WIDE), jnp.int32),
            jax.ShapeDtypeStruct((9, 1, 4 * WIDE), jnp.int32),
            jax.ShapeDtypeStruct((1, 128), jnp.float32),
        ),
        in_specs=[pl.BlockSpec(memory_space=pltpu.SMEM)] + [in_vmem] * 4,
        out_specs=(in_vmem,) * 3,
    )(*lists)


def exchange_kernel(
    nx,
    ny,
    caps,
    picks,
    labels,
    over,
    old,
    vel,
    weights,
    out,
    any_over,
    remapped,
    blocks,
    tiles,
    outgoing,
    incoming,
    incoming_labels,
    turn,
    edge_y,
    edge_x,
    flow_y,
    flow_x,
    flags,
    flags_in,
    load_sem,
    label_sems,
    send_sems,
    recv_sems,
    edge_sems,
    flow_sems,
    flag_sems,
):
    gx, gy = lax.axis_index("gx"), lax.axis_index("gy")
    parts = load_sem.shape[0]
    depth = tiles.shape[0] // parts
    cap = outgoing.shape[1]
    state_count, rows = remapped.shape[:2]

    for part in range(parts):
        span = pl.ds(part * depth, depth)
        pltpu.make_async_copy(weights.at[span], tiles.at[span], load_sem.at[part]).start()

    barrier = pltpu.get_barrier_semaphore()

    def along_gx(j):
        return (lax.rem(gx + j, nx), gy)

    def along_gy(j):
        return (gx, lax.rem(gy + j, ny))

    def greet(j, carry, along):
        pl.semaphore_signal(barrier, inc=1, device_id=along(j), device_id_type=MESH)
        return carry

    lax.fori_loop(1, ny, functools.partial(greet, along=along_gy), 0)
    lax.fori_loop(1, nx, functools.partial(greet, along=along_gx), 0)
    for k in range(8):
        dx, dy = step_of(k)

        @pl.when(exists(gx + dx, gy + dy, nx, ny))
        def _():
            pl.semaphore_signal(
                barrier, inc=1, device_id=(gx + dx, gy + dy), device_id_type=MESH
            )

    blocks[...] = jnp.zeros_like(blocks)
    for c in range(state_count):
        blocks[:, c, :] = old[c].astype(jnp.float32)
    pl.semaphore_wait(barrier, neighbours_of(gx, gy, nx, ny) + nx + ny - 2)

    def flag_copy(turn_of, j):
        slot = turn_of * nx + j
        return pltpu.make_async_remote_copy(
            src_ref=flags.at[turn_of],
            dst_ref=flags_in.at[slot],
            send_sem=flag_sems.at[0, slot],
            recv_sem=flag_sems.at[1, slot],
            device_id=(along_gx, along_gy)[turn_of](j),
            device_id_type=MESH,
        )

    def send_flag(turn_of):
        def step(j, carry):
            flag_copy(turn_of, j).start()
            return carry

        lax.fori_loop(1, (nx, ny)[turn_of], step, 0)

    def gather_flag(turn_of):
        def step(j, carry):
            flag_copy(turn_of, j).wait_recv()
            return jnp.maximum(carry, flags_in[turn_of * nx + j])

        flags[turn_of + 1] = lax.fori_loop(1, (nx, ny)[turn_of], step, flags[turn_of])

    def end_flag(turn_of):
        def step(j, carry):
            flag_copy(turn_of, j).wait_send()
            return carry

        lax.fori_loop(1, (nx, ny)[turn_of], step, 0)

    flags[0] = over[...]

    def label_copy(k):
        dx, dy = step_of(k)
        return pltpu.make_async_remote_copy(
            src_ref=labels.at[k],
            dst_ref=incoming_labels.at[k],
            send_sem=label_sems.at[0, k],
            recv_sem=label_sems.at[1, k],
            device_id=(gx + dx, gy + dy),
            device_id_type=MESH,
        )

    def chunk_copy(k, j):
        dx, dy = step_of(k)
        span = pl.ds(j * CHUNK, CHUNK)
        return pltpu.make_async_remote_copy(
            src_ref=outgoing.at[k, span],
            dst_ref=incoming.at[k, span],
            send_sem=send_sems.at[k, j],
            recv_sem=recv_sems.at[k, j],
            device_id=(gx + dx, gy + dy),
            device_id_type=MESH,
        )

    def goes_out(k):
        dx, dy = step_of(k)
        return exists(gx + dx, gy + dy, nx, ny)

    def comes_in(k):
        dx, dy = step_of(k)
        return exists(gx - dx, gy - dy, nx, ny)

    def each_channel(body, predicate):
        def step(k, carry):
            @pl.when(predicate(k))
            def _():
                body(k)

            return carry

        lax.fori_loop(0, 8, step, 0)

    lanes = lax.broadcasted_iota(jnp.int32, (32, 128), 1)
    sides = ((0, 0, 1), (1, 0, -1), (0, 1, 0), (1, -1, 0))

    def pack_edges(ref, along_y, along_x):
        planes = ref.shape[0]
        for h in range(rows // 128):
            packed = jnp.zeros((32, 128), jnp.float32)
            for q in range(4):
                for c in range(planes):
                    to = 32 * q + 2 * c
                    moved = pltpu.roll(ref[c, pl.ds(128 * h + 32 * q, 32), :], to + 1, 1)
                    packed = jnp.where((lanes >> 1) == (to >> 1), moved, packed)
            along_y[0, h] = packed
        for side, row in ((0, rows - 1), (1, 0)):
            for c in range(planes):
                along_x[side, c : c + 1, :] = ref[c, row : row + 1, :]

    def side_copy(index, along_y, along_x, sems):
        side, dx, dy = sides[index]
        edge = along_y if dx == 0 else along_x
        return pltpu.make_async_remote_copy(
            src_ref=edge.at[0 if dx == 0 else side],
            dst_ref=edge.at[side + 1 if dx == 0 else side + 2],
            send_sem=sems.at[0, index],
            recv_sem=sems.at[1, index],
            device_id=(gx + dx, gy + dy),
            device_id_type=MESH,
        )

    def each_side(body, sign):
        for index, (_, dx, dy) in enumerate(sides):

            @pl.when(exists(gx + sign * dx, gy + sign * dy, nx, ny))
            def _():
                body(index)

    flow = (flow_y, flow_x, flow_sems)
    edges = (edge_y, edge_x, edge_sems)

    for part in range(parts):
        span = pl.ds(part * depth, depth)
        pltpu.make_async_copy(weights.at[span], tiles.at[span], load_sem.at[part]).wait()

    def multiply(k, j, buffer):
        at = jnp.where(j < FIRST, j * CHUNK, (j - FIRST + 1) * WIDE)
        none = jnp.zeros((16, 128), jnp.bfloat16)
        join = jnp.concatenate
        for i in range(0, CHUNK, 4):
            four = [picks[k, at + i + n] for n in range(4)]
            a = [blocks[p & 127].astype(jnp.bfloat16) for p in four]
            w = [tiles[p >> 7] for p in four]
            left = join([join([a[n], none] if n % 2 == 0 else [none, a[n]], 1) for n in range(4)], 0)
            right = join([join([w[0], w[1]], 1), join([w[2], w[3]], 1)], 0)
            piece = lax.dot_general(
                left, right, (((1,), (1,)), ((), ())), preferred_element_type=jnp.float32
            )
            turn[buffer, pl.ds(16 * i, 32), :] = piece[:32, :128]
            turn[buffer, pl.ds(16 * i + 32, 32), :] = piece[32:, 128:]

    def lay(k, j, buffer):
        for group in range(CHUNK // 16):
            for c in range(state_count):
                turned = turn[buffer, pl.ds(256 * group + c, 16, stride=16), :]
                outgoing[
                    k,
                    pl.ds(pl.multiple_of(j * CHUNK + 16 * group, 16), 16),
                    pl.ds(c * 128, 128),
                ] = turned.astype(jnp.bfloat16)

    def send(k, j):
        @pl.when(k < 8)
        def _():
            chunk_copy(k, j).start()

    def sent(k):
        _, dy = step_of(k)
        return chunks_of(gx, gy, dy, nx, ny, caps)

    def channel(k, carry):
        def three(t, carry):
            j = FIRST * t
            multiply(k, j, 0)
            lay(k, j, 0)
            send(k, j)
            multiply(k, j + 1, 1)
            multiply(k, j + 2, 2)
            lay(k, j + 1, 1)
            send(k, j + 1)
            lay(k, j + 2, 2)
            send(k, j + 2)
            return carry

        def one(j, carry):
            multiply(k, j, 0)
            lay(k, j, 0)
            send(k, j)
            return carry

        @pl.when((k == 8) | goes_out(k))
        def _():
            @pl.when(k < 8)
            def _():
                label_copy(k).start()

            lax.fori_loop(0, jnp.where(k == 8, CHUNKS // FIRST, 1), three, 0)
            lax.fori_loop(FIRST, jnp.where(k == 8, FIRST, sent(k)), one, 0)

        @pl.when(k == 1)
        def _():
            send_flag(0)

        @pl.when(k == 3)
        def _():
            gather_flag(0)
            send_flag(1)

        @pl.when(k == 7)
        def _():
            pack_edges(vel, flow_y, flow_x)
            each_side(lambda index: side_copy(index, *flow).start(), 1)

        return carry

    lax.fori_loop(0, 9, channel, 0)

    row_ids = lax.broadcasted_iota(jnp.int32, (rows, WIDE), 0)

    def add(label_row, values, first):
        width = values.shape[0]
        selector = jnp.where(row_ids == label_row, 1.0, 0.0).astype(jnp.bfloat16)[:, :width]
        for c in range(0, state_count, 2):
            summed = jnp.dot(
                selector,
                values[:, c * 128 : (c + 2) * 128],
                preferred_element_type=jnp.float32,
            )
            if first:
                remapped[c] = summed[:, :128]
                remapped[c + 1] = summed[:, 128:]
            else:
                remapped[c] += summed[:, :128]
                remapped[c + 1] += summed[:, 128:]

    def add_piece(label_rows, k, values, first):
        add(label_rows[k, :, :WIDE], values[k, : FIRST * CHUNK], first)

    def add_chunk(label_rows, k, values, j):
        lanes_of = slice((j - FIRST + 1) * WIDE, (j - FIRST + 2) * WIDE)
        add(label_rows[k, :, lanes_of], values[k, j * CHUNK : (j + 1) * CHUNK], False)

    add_piece(labels, 8, outgoing, True)
    for j in range(FIRST, CHUNKS):
        add_chunk(labels, 8, outgoing, j)

    def accept(k):
        dx, dy = step_of(k)
        arriving = chunks_of(gx - dx, gy - dy, dy, nx, ny, caps)
        label_copy(k).wait_recv()
        for j in range(FIRST):
            chunk_copy(k, j).wait_recv()
        add_piece(incoming_labels, k, incoming, False)
        for j in range(FIRST, CHUNKS):

            @pl.when(arriving > j)
            def _():
                chunk_copy(k, j).wait_recv()
                add_chunk(incoming_labels, k, incoming, j)

    def accept_in_turn(i, carry):
        k = lax.rem(i + 6, 8)

        @pl.when(comes_in(k))
        def _():
            accept(k)

        return carry

    lax.fori_loop(0, 8, accept_in_turn, 0)

    pack_edges(remapped, edge_y, edge_x)
    each_side(lambda index: side_copy(index, *edges).start(), 1)

    def land(along_y, along_x, sems):
        for index, (side, dx, dy) in enumerate(sides):
            edge, slot = (along_y, side + 1) if dx == 0 else (along_x, side + 2)
            there = exists(gx - dx, gy - dy, nx, ny)

            @pl.when(there)
            def _():
                side_copy(index, along_y, along_x, sems).wait_recv()

            @pl.when(jnp.logical_not(there))
            def _():
                edge[slot] = jnp.zeros(edge.shape[1:], jnp.float32)

    land(*flow)

    def step(b, carry):
        step_block(b, rows // 32, remapped, vel, flow_y, flow_x, out)
        return carry

    lax.fori_loop(0, rows // 32, step, 0)

    land(*edges)
    for side, row in ((0, 0), (1, rows - 1)):
        bound, scale = (jnp.maximum, time_step) if side == 0 else (jnp.minimum, -time_step)
        speed = scale * bound(vel[0, row : row + 1, :], 0.0)
        for c in range(state_count):
            out[c, row : row + 1, :] += speed * edge_x[side + 2, c : c + 1, :]

    each_side(lambda index: side_copy(index, *edges).wait_send(), 1)
    for h in range(rows // 128):
        moved = pltpu.roll(edge_y[1, h], 2, 1)
        edge_y[0, h] = jnp.where((lanes & 1) == 0, moved, edge_y[2, h])

    for b in range(rows // 32):
        span = slice(32 * b, 32 * (b + 1))
        flow_here = vel[1, span, :]
        speed = jnp.where(
            lanes == 0,
            time_step * jnp.maximum(flow_here, 0.0),
            jnp.where(lanes == 127, -time_step * jnp.minimum(flow_here, 0.0), 0.0),
        )
        pack = edge_y[0, b // 4]
        for c in range(state_count):
            out[c, span, :] += speed * pltpu.roll(pack, (126 - 32 * (b % 4) - 2 * c) % 128, 1)
    each_side(lambda index: side_copy(index, *flow).wait_send(), 1)

    def finish(k):
        label_copy(k).wait_send()

        def chunk(j, carry):
            chunk_copy(k, j).wait_send()
            return carry

        lax.fori_loop(0, sent(k), chunk, 0)

    each_channel(finish, goes_out)
    gather_flag(1)
    end_flag(0)
    end_flag(1)
    any_over[...] = flags[2]


def exchange(nx, ny, caps, collective_id, picks, labels, over, old, velocity, weights):
    state_count, rows = old.shape[0], velocity.shape[1]
    cap = CHUNKS * CHUNK
    f32, vmem = jnp.float32, pltpu.VMEM
    in_vmem = pl.BlockSpec(memory_space=vmem)
    dma = pltpu.SemaphoreType.DMA
    return pl.pallas_call(
        functools.partial(exchange_kernel, nx, ny, caps),
        out_shape=(
            jax.ShapeDtypeStruct((state_count, rows, 128), f32),
            jax.ShapeDtypeStruct((1, 128), f32),
        ),
        in_specs=[pl.BlockSpec(memory_space=pltpu.SMEM)]
        + [in_vmem] * 4
        + [pl.BlockSpec(memory_space=pl.ANY)],
        out_specs=(in_vmem,) * 2,
        scratch_shapes=[
            vmem((state_count, rows, 128), f32),
            vmem((old.shape[1], 16, 128), f32),
            vmem(weights.shape, jnp.bfloat16),
            vmem((9, cap, state_count * 128), jnp.bfloat16),
            vmem((8, cap, state_count * 128), jnp.bfloat16),
            vmem((8, 1, 4 * WIDE), jnp.int32),
            vmem((FIRST, 16 * CHUNK, 128), f32),
            vmem((3, rows // 128, 32, 128), f32),
            vmem((4, 16, 128), f32),
            vmem((3, rows // 128, 32, 128), f32),
            vmem((4, 16, 128), f32),
            vmem((3, 1, 128), f32),
            vmem((nx + ny, 1, 128), f32),
            dma((4,)),
            dma((2, 8)),
            dma((8, cap // CHUNK)),
            dma((8, cap // CHUNK)),
            dma((2, 4)),
            dma((2, 4)),
            dma((2, nx + ny)),
        ],
        compiler_params=pltpu.CompilerParams(
            collective_id=collective_id, has_side_effects=True, vmem_limit_bytes=48 * MIB
        ),
        cost_estimate=pl.CostEstimate(
            flops=2 * 9 * cap * 128 * 128 * 16,
            bytes_accessed=weights.size * 2,
            transcendentals=0,
        ),
    )(picks, labels, over, old, velocity, weights)


def step_block(b, blocks, state, vel, flow_y, flow_x, out):
    rows, depth = state.shape[1], 32
    base = pl.multiple_of(b * depth, depth)
    span = pl.ds(base, depth)
    lane = lax.broadcasted_iota(jnp.int32, (depth, 128), 1)
    row = lax.broadcasted_iota(jnp.int32, (depth, 128), 0)
    quarter = 32 * lax.rem(b, 4)
    left_pack = pltpu.roll(flow_y[1, b // 4], lax.rem(128 - quarter, 128), 1)
    right_pack = pltpu.roll(flow_y[2, b // 4], lax.rem(128 + 126 - quarter, 128), 1)

    def around(ref, c, halo):
        mid = ref[c, span, :]
        above = ref[c, pl.ds(jnp.maximum(base - 1, 0), 1), :]
        below = ref[c, pl.ds(jnp.minimum(base + depth, rows - 1), 1), :]
        if halo:
            first, last = flow_x[2, c : c + 1, :], flow_x[3, c : c + 1, :]
            shift = (128 - 2 * c) % 128
            left, right = pltpu.roll(left_pack, shift, 1), pltpu.roll(right_pack, shift, 1)
        else:
            first = last = left = right = 0.0
        above = jnp.where(b == 0, first, above)
        below = jnp.where(b == blocks - 1, last, below)
        before_x = jnp.where(row == 0, above, pltpu.roll(mid, 1, 0))
        after_x = jnp.where(row == depth - 1, below, pltpu.roll(mid, depth - 1, 0))
        before_y = jnp.where(lane == 0, left, pltpu.roll(mid, 1, 1))
        after_y = jnp.where(lane == 127, right, pltpu.roll(mid, 127, 1))
        return mid, before_x, after_x, before_y, after_y

    u_x, ux_bx, ux_ax, ux_by, ux_ay = around(vel, 0, True)
    u_y, uy_bx, uy_ax, uy_by, uy_ay = around(vel, 1, True)
    d_xx = 0.5 * (ux_ax - ux_bx)
    l_xy = 0.5 * (ux_ay - ux_by)
    l_yx = 0.5 * (uy_ax - uy_bx)
    d_yy = 0.5 * (uy_ay - uy_by)
    d_zz = -(d_xx + d_yy)
    d_xy = 0.5 * (l_xy + l_yx)
    spin = 0.5 * (l_xy - l_yx)
    plus_x, minus_x = jnp.maximum(u_x, 0.0), jnp.minimum(u_x, 0.0)
    plus_y, minus_y = jnp.maximum(u_y, 0.0), jnp.minimum(u_y, 0.0)
    shear = (2.0 * interaction) * jnp.sqrt(
        2.0 * (d_xx * d_xx + d_yy * d_yy + d_zz * d_zz + 2.0 * (d_xy * d_xy)) + 1.0
    )
    a_xx, a_yy, a_zz, a_xy, a_xz, a_yz = (state[c, span, :] for c in range(6))
    contraction = d_xx * a_xx + d_yy * a_yy + d_zz * a_zz + 2.0 * (d_xy * a_xy)
    fade = shape_factor * 2.0 * contraction + 3.0 * shear
    stress = 2.0 * shear_modulus
    pull = fiber_number * contraction
    sources = (
        2.0 * (spin * a_xy) + shape_factor * 2.0 * (d_xx * a_xx + d_xy * a_xy) - fade * a_xx + shear,
        -2.0 * (spin * a_xy) + shape_factor * 2.0 * (d_xy * a_xy + d_yy * a_yy) - fade * a_yy + shear,
        shape_factor * 2.0 * (d_zz * a_zz) - fade * a_zz + shear,
        spin * (a_yy - a_xx)
        + shape_factor * (d_xx * a_xy + d_xy * a_yy + a_xx * d_xy + a_xy * d_yy)
        - fade * a_xy,
        spin * a_yz + shape_factor * (d_xx * a_xz + d_xy * a_yz + a_xz * d_zz) - fade * a_xz,
        -spin * a_xz + shape_factor * (d_xy * a_xz + d_yy * a_yz + a_yz * d_zz) - fade * a_yz,
        d_xx,
        d_yy,
        d_xy,
        stress * (d_xx + pull * a_xx),
        stress * (d_yy + pull * a_yy),
        stress * (d_xy + pull * a_xy),
    )
    for c, source in enumerate(sources):
        mid, before_x, after_x, before_y, after_y = around(state, c, False)
        upwind = (
            plus_x * (mid - before_x)
            + minus_x * (after_x - mid)
            + plus_y * (mid - before_y)
            + minus_y * (after_y - mid)
        )
        out[c, span, :] = mid + time_step * (source - upwind)


def per_device(
    nx,
    ny,
    old_states,
    weight_tiles,
    source_block,
    tile_index,
    dest_device,
    dest_block,
    send_count,
    velocity,
):
    lists = (send_count, source_block, tile_index, dest_device, dest_block)
    old = jnp.transpose(old_states, (1, 0, 2))
    places = plan(nx, ny, USUAL, lists)
    states, any_over = exchange(nx, ny, USUAL, 0, *places, old, velocity, weight_tiles)

    def again(_):
        return exchange(nx, ny, FULL, 1, *places, old, velocity, weight_tiles)[0]

    states = lax.cond(any_over[0, 0] > 0, again, lambda enough: enough, states)
    return jnp.transpose(states, (1, 0, 2))


def solution(mesh):
    in_specs = (
        P(("gx", "gy"), None, None),
        P(("gx", "gy"), None, None),
        P(("gx", "gy")),
        P(("gx", "gy")),
        P(("gx", "gy")),
        P(("gx", "gy")),
        P(("gx", "gy")),
        P(None, "gx", "gy"),
    )
    out_specs = P("gx", None, "gy")
    return jax.shard_map(
        functools.partial(per_device, mesh.shape["gx"], mesh.shape["gy"]),
        mesh=mesh,
        in_specs=in_specs,
        out_specs=out_specs,
        check_vma=False,
    )
```
